32 devices in a mesh: dp: 8 (over z, core), tensor: 4 (over y, x).
Axes of the slice: x: 2, y: 2, z: 4, core: 2. Of those that a mesh axis runs over, the one named last changes fastest.
Arguments:
- tokens: bfloat16 [8192, 1024], P(('dp', 'tensor'))
- segments: int32 [8192], P('dp'), may hold values from 0 to 2, as said below
- cotangent: bfloat16 [8192, 1024], P(('dp', 'tensor')), may hold values from -6 to 6
- query_weight: bfloat16 [1024, 1024], P('dp', 'tensor'), may hold values from -0.1875 to 0.1875
- key_weight: bfloat16 [1024, 512], P('dp', 'tensor'), may hold values from -0.1875 to 0.1875
- value_weight: bfloat16 [1024, 512], P('dp', 'tensor'), may hold values from -0.1875 to 0.1875
- out_weight: bfloat16 [1024, 1024], P('tensor', 'dp'), may hold values from -1.5 to 1.5
- gate_weight: bfloat16 [1024, 4608], P('dp', 'tensor'), may hold values from -0.1875 to 0.1875
- up_weight: bfloat16 [1024, 4608], P('dp', 'tensor'), may hold values from -0.1875 to 0.1875
- down_weight: bfloat16 [4608, 1024], P('tensor', 'dp'), may hold values from -0.1875 to 0.1875
- attention_gain: float32 [1024], replicated, may hold values from 0.1 to 1.9
- feedfwd_gain: float32 [1024], replicated, may hold values from 0.1 to 1.9
- query_gain: float32 [64], replicated, may hold values from 0.1 to 1.9
- key_gain: float32 [64], replicated, may hold values from 0.1 to 1.9
Outputs:
- block_out: bfloat16 [8192, 1024], P(('dp', 'tensor'))
- grad_tokens: bfloat16 [8192, 1024], P(('dp', 'tensor'))
- grad_query: float32 [1024, 1024], P('dp', 'tensor')
- grad_key: float32 [1024, 512], P('dp', 'tensor')
- grad_value: float32 [1024, 512], P('dp', 'tensor')
- grad_output: float32 [1024, 1024], P('tensor', 'dp')
- grad_gate: float32 [1024, 4608], P('dp', 'tensor')
- grad_up: float32 [1024, 4608], P('dp', 'tensor')
- grad_down: float32 [4608, 1024], P('tensor', 'dp')
- grad_attention: float32 [1024], replicated
- grad_feedfwd: float32 [1024], replicated
- grad_querynorm: float32 [64], replicated
- grad_keynorm: float32 [64], replicated
The draws below stay inside these ranges and needn't reach their ends.
Inputs may be any that keep to these rules, and one draw needn't show every extreme that they name: `segments`: each sequence of 1024 consecutive tokens holds exactly three documents, numbered 0, 1, 2 in order, each of 204 tokens or more.
All inputs are finite; a program needn't handle non-finite values.
Results may differ from the reference program's by a relative error of at most 0.023.
Values may be sent and summed in bfloat16 or wider, within the bound.
No kernel may reach another device: no remote copies, remote signals or barrier semaphores. Data moves between devices by JAX's collectives and lax.ppermute only.
A program may use at most 128 MiB of HBM per device.

```python
import math
import jax
import jax.numpy as jnp
from jax import lax

D = 1024
HEADS = 16
KVH = 8
HD = 64
FF = 4608
LEN = 1024
BLOCK = 512
TOKENS = 8192


def draw_tokens(key, part):
    key = jax.random.fold_in(key, 11)
    base_key, row_key, column_key = jax.random.split(key, 3)
    base = jax.random.normal(base_key, (TOKENS, D), jnp.float32)
    row_scale = jnp.exp(jax.random.uniform(row_key, (TOKENS, 1), jnp.float32, -0.7, 0.7))
    column_scale = jnp.exp(jax.random.uniform(column_key, (1, D), jnp.float32, -1.2, 1.2))
    return (base * row_scale * column_scale).astype(jnp.bfloat16)


def draw_segments(key, part):
    key = jax.random.fold_in(key, 12)
    first_key, second_key = jax.random.split(key, 2)
    sequences = TOKENS // LEN
    shortest = LEN // 5
    first_cut = jax.random.randint(first_key, (sequences, 1), shortest, LEN - 2 * shortest + 1)
    second_cut = jax.random.randint(second_key, (sequences, 1), first_cut + shortest, LEN - shortest + 1)
    position = jnp.arange(LEN, dtype=jnp.int32)[None, :]
    numbers = (position >= first_cut).astype(jnp.int32) + (position >= second_cut).astype(jnp.int32)
    return numbers.reshape(TOKENS)


def spiked(entries, key, source, target, blocks, factor):
    def block_of(axis_at):
        return (jnp.arange(entries.shape[axis_at]) // (entries.shape[axis_at] // blocks)).reshape((-1,) + (1,) * (entries.ndim - 1 - axis_at))

    one_side = jax.random.permutation(key, blocks)[block_of(target)]
    other_side = (block_of(target) + blocks // 2) % blocks
    return jnp.where((block_of(source) == one_side) | (block_of(source) == other_side), factor * entries, entries)


def levels(stream_key, dims, cuts, low, largest):
    factor_of, own = 1.0, jax.random.fold_in(stream_key, 6)
    for dim, shards_of in cuts:
        heights = jnp.exp(jax.random.uniform(jax.random.fold_in(own, dim), (shards_of,), jnp.float32, low / len(cuts), largest / len(cuts)))
        factor_of = factor_of * jnp.repeat(heights, dims[dim] // shards_of).reshape([-1 if axis == dim else 1 for axis in range(len(dims))])
    return factor_of


def scatter_about(key, shape, spread, reach, cuts=(), kind=jnp.bfloat16):
    level = levels(key, shape, cuts, -0.22, 0.18) if cuts else 1.0
    values = jax.random.normal(key, shape, jnp.float32) * spread * level
    return jnp.minimum(jnp.maximum(values, -reach), reach).astype(kind)


def gaussian_with(own_key, extent, deviation, limit, shards, heavy, kind=jnp.bfloat16):
    result = deviation * jax.random.normal(own_key, extent, jnp.float32)
    if shards:
        result = result * levels(own_key, extent, shards, -0.22, 0.18)
    return jnp.clip(spiked(result, jax.random.fold_in(own_key, 3), *heavy), -limit, limit).astype(kind)


def setup_inputs(seed: int = 0) -> dict:
    keys = jax.random.split(jax.random.key(seed), 15)
    tokens = draw_tokens(jax.random.fold_in(keys[14], 71), 0)
    segments = draw_segments(jax.random.fold_in(keys[14], 71), 0)
    cotangent = gaussian_with(keys[2], (TOKENS, D), 1.0, 6.0, ((0, 32),), (0, 1, 32, 2.75))
    query_weight = scatter_about(keys[3], (D, HEADS * HD), D ** -0.5, 0.1875, ((0, 8), (1, 4)))
    key_weight = scatter_about(keys[4], (D, KVH * HD), D ** -0.5, 0.1875, ((0, 8), (1, 4)))
    value_weight = scatter_about(keys[5], (D, KVH * HD), D ** -0.5, 0.1875, ((0, 8), (1, 4)))
    out_weight = scatter_about(keys[6], (HEADS * HD, D), (max(HEADS * HD // 64, 1)) ** -0.5, 1.5, ((0, 4), (1, 8)))
    gate_weight = scatter_about(keys[7], (D, FF), D ** -0.5, 0.1875, ((0, 8), (1, 4)))
    up_weight = scatter_about(keys[8], (D, FF), D ** -0.5, 0.1875, ((0, 8), (1, 4)))
    down_weight = scatter_about(keys[9], (FF, D), (FF // 4) ** -0.5, 0.1875, ((0, 4), (1, 8)))
    attention_gain = jnp.clip(1.0 + 0.18 * jax.random.normal(keys[10], (D,), jnp.float32), 0.1, 1.9)
    feedfwd_gain = jnp.clip(1.0 + 0.18 * jax.random.normal(keys[11], (D,), jnp.float32), 0.1, 1.9)
    query_gain = jnp.clip(1.0 + 0.18 * jax.random.normal(keys[12], (HD,), jnp.float32), 0.1, 1.9)
    key_gain = jnp.clip(1.0 + 0.18 * jax.random.normal(keys[13], (HD,), jnp.float32), 0.1, 1.9)
    return dict(tokens=tokens, segments=segments, cotangent=cotangent, query_weight=query_weight, key_weight=key_weight, value_weight=value_weight, out_weight=out_weight, gate_weight=gate_weight, up_weight=up_weight, down_weight=down_weight, attention_gain=attention_gain, feedfwd_gain=feedfwd_gain, query_gain=query_gain, key_gain=key_gain)


EPSILON = 1e-05
THETA = 1000000.0
MASKED = -1e+30
HIGHEST = lax.Precision.HIGHEST

@jax.custom_vjp
def low(v):
    return lax.optimization_barrier(v.astype(jnp.bfloat16)).astype(jnp.float32)

@jax.custom_vjp
def low_back(v):
    return v

def low_keep(v):
    return (low(v), None)

def low_pass(kept, grad):
    return (grad,)

def back_keep(v):
    return (v, None)

def back_low(kept, grad):
    return (low(grad),)
low.defvjp(low_keep, low_pass)
low_back.defvjp(back_keep, back_low)

def rms_scale(values, gain):
    return values * lax.rsqrt(lax.optimization_barrier(jnp.mean(values * values, axis=-1, keepdims=True)) + EPSILON) * gain

def doc_positions(seg_row):
    row_order = jnp.arange(seg_row.shape[0], dtype=jnp.int32)
    starting = jnp.concatenate([jnp.ones((1,), jnp.bool_), seg_row[1:] != seg_row[:-1]])
    starts = lax.cummax(jnp.where(starting, row_order, 0), axis=0)
    return row_order - starts

def rope_tables(positions, half_dim):
    step_index = jnp.arange(half_dim, dtype=jnp.float32)
    inverse = jnp.exp(step_index * (-math.log(THETA) / half_dim))
    angles = positions.astype(jnp.float32)[:, None] * inverse[None, :]
    return (jnp.cos(angles), jnp.sin(angles))

def rotate(values, cosine, sine_table):
    half_dim = values.shape[-1] // 2
    first_half = values[..., :half_dim]
    second = values[..., half_dim:]
    cosine = cosine[:, None, :]
    sine_table = sine_table[:, None, :]
    return jnp.concatenate([first_half * cosine - second * sine_table, second * cosine + first_half * sine_table], axis=-1)

def attend_block(queries, key_rows, values, seg_query, seg_all, query_order, key_order):
    group_size = queries.shape[1] // key_rows.shape[1]
    keys_wide = jnp.repeat(key_rows, group_size, axis=1)
    values_wide = jnp.repeat(values, group_size, axis=1)
    scores = jnp.einsum('qhd,khd->hqk', queries, keys_wide, precision=HIGHEST) * queries.shape[2] ** (-0.5)
    scores = low_back(scores)
    allowed = (seg_query[:, None] == seg_all[None, :]) & (key_order[None, :] <= query_order[:, None])
    scores = jnp.where(allowed[None, :, :], scores, MASKED)
    weights = low(jax.nn.softmax(scores, axis=-1))
    return jnp.einsum('hqk,khd->qhd', weights, values_wide, precision=HIGHEST)

def sequence_forward(tokens, seg_row, params):
    query_weight, key_weight, value_weight, out_weight, gate_weight, up_weight, down_weight, attention_gain, feedfwd_gain, query_gain, key_gain = params
    length = tokens.shape[0]
    head_dim = query_gain.shape[0]
    normed = low(rms_scale(tokens, attention_gain))
    query_raw = low_back(jnp.dot(normed, query_weight, precision=HIGHEST)).reshape(length, -1, head_dim)
    key_raw = low_back(jnp.dot(normed, key_weight, precision=HIGHEST)).reshape(length, -1, head_dim)
    values = low(low_back(jnp.dot(normed, value_weight, precision=HIGHEST))).reshape(length, -1, head_dim)
    cosine, sine_table = rope_tables(doc_positions(seg_row), head_dim // 2)
    queries = low(rotate(rms_scale(query_raw, query_gain), cosine, sine_table))
    key_rows = low(rotate(rms_scale(key_raw, key_gain), cosine, sine_table))
    row_order = jnp.arange(length, dtype=jnp.int32)
    blocks = length // BLOCK

    def one_block(block_items):
        return attend_block(block_items[0], key_rows, values, block_items[1], seg_row, block_items[2], row_order)
    attended = lax.map(jax.checkpoint(one_block), (queries.reshape(blocks, BLOCK, queries.shape[1], head_dim), seg_row.reshape(blocks, BLOCK), row_order.reshape(blocks, BLOCK)))
    context = low(low_back(attended.reshape(length, -1)))
    residual = tokens + low_back(jnp.dot(context, out_weight, precision=HIGHEST))
    normed_two = low(rms_scale(residual, feedfwd_gain))
    gate_proj = low_back(jnp.dot(normed_two, gate_weight, precision=HIGHEST))
    upward = low_back(jnp.dot(normed_two, up_weight, precision=HIGHEST))
    hidden = low(jax.nn.silu(gate_proj) * upward)
    return residual + low_back(jnp.dot(hidden, down_weight, precision=HIGHEST))

def reference(tokens, segments, cotangent, query_weight, key_weight, value_weight, out_weight, gate_weight, up_weight, down_weight, attention_gain, feedfwd_gain, query_gain, key_gain):
    params = tuple((weight.astype(jnp.float32) for weight in (query_weight, key_weight, value_weight, out_weight, gate_weight, up_weight, down_weight, attention_gain, feedfwd_gain, query_gain, key_gain)))
    width = tokens.shape[1]
    seg_rows = segments.reshape(-1, LEN)

    def forward(inputs, *weights):

        def one_sequence(carry, pair):
            return (carry, jax.checkpoint(sequence_forward)(pair[0], pair[1], weights))
        carry_out, outputs = lax.scan(one_sequence, jnp.zeros((), jnp.float32), (inputs.reshape(-1, LEN, width), seg_rows))
        return outputs.reshape(-1, width)
    block_out, pullback = jax.vjp(forward, tokens.astype(jnp.float32), *params)
    grads = pullback(cotangent.astype(jnp.float32))
    return (block_out.astype(jnp.bfloat16), grads[0].astype(jnp.bfloat16), grads[1], grads[2], grads[3], grads[4], grads[5], grads[6], grads[7], grads[8], grads[9], grads[10], grads[11])
```

```python
from functools import partial
import math

import jax
import jax.numpy as jnp
from jax import lax
from jax.sharding import PartitionSpec as P

LEN = 1024
BLOCK = 512


EPSILON = 1e-05
THETA = 1000000.0
MASKED = -1e30


def rms_scale(values, gain):
    return values * lax.rsqrt(jnp.mean(values * values, axis=-1, keepdims=True) + EPSILON) * gain


def doc_positions(seg_row):
    row_order = jnp.arange(seg_row.shape[0], dtype=jnp.int32)
    starting = jnp.concatenate([jnp.ones((1,), jnp.bool_), seg_row[1:] != seg_row[:-1]])
    starts = lax.cummax(jnp.where(starting, row_order, 0), axis=0)
    return row_order - starts


def rope_tables(positions, half_dim):
    step_index = jnp.arange(half_dim, dtype=jnp.float32)
    inverse = jnp.exp(step_index * (-math.log(THETA) / half_dim))
    angles = positions.astype(jnp.float32)[:, None] * inverse[None, :]
    return (jnp.cos(angles), jnp.sin(angles))


def rotate(values, cosine, sine_table):
    half_dim = values.shape[-1] // 2
    first_half = values[..., :half_dim]
    second = values[..., half_dim:]
    cosine = cosine[:, None, :]
    sine_table = sine_table[:, None, :]
    return jnp.concatenate(
        [first_half * cosine - second * sine_table, second * cosine + first_half * sine_table],
        axis=-1,
    )


def prepare_heads(cosine, sine_table, raw_rows, gain):
    row_total = raw_rows.shape[0]
    return rotate(
        rms_scale(raw_rows.reshape(row_total, -1, gain.shape[0]), gain), cosine, sine_table
    )


def swiglu(gate_proj, upward):
    return jax.nn.silu(gate_proj) * upward


def masked_scores(query_block, key_block, seg_query, seg_key, row_start, scale):
    scores = (
        jnp.einsum("qcgd,kcd->cgqk", query_block, key_block, preferred_element_type=jnp.float32)
        * scale
    )
    query_pos = row_start + jnp.arange(query_block.shape[0], dtype=jnp.int32)
    key_pos = jnp.arange(key_block.shape[0], dtype=jnp.int32)
    allowed = (seg_query[:, None] == seg_key[None, :]) & (key_pos[None, :] <= query_pos[:, None])
    return jnp.where(allowed, scores, MASKED)


def attention_forward(query_low, key_low, value_low, seg_row, scale):
    outputs = []
    totals = []
    for block_index in range(query_low.shape[0] // BLOCK):
        row_start = block_index * BLOCK
        row_stop = row_start + BLOCK
        scores = masked_scores(
            query_low[row_start:row_stop],
            key_low[:row_stop],
            seg_row[row_start:row_stop],
            seg_row[:row_stop],
            row_start,
            scale,
        )
        row_peak = jnp.max(scores, axis=-1, keepdims=True)
        log_total = row_peak + jnp.log(jnp.sum(jnp.exp(scores - row_peak), axis=-1, keepdims=True))
        probs_low = jnp.exp(scores - log_total).astype(jnp.bfloat16)
        outputs.append(
            jnp.einsum(
                "cgqk,kcd->qcgd",
                probs_low,
                value_low[:row_stop],
                preferred_element_type=jnp.float32,
            )
        )
        totals.append(log_total)
    return (jnp.concatenate(outputs, axis=0), jnp.concatenate(totals, axis=2))


def attention_backward(query_low, key_low, value_low, seg_row, log_totals, grad_low, scale):
    query_parts = []
    grad_keys = jnp.zeros(key_low.shape, jnp.float32)
    grad_values = jnp.zeros(value_low.shape, jnp.float32)
    for block_index in range(query_low.shape[0] // BLOCK):
        row_start = block_index * BLOCK
        row_stop = row_start + BLOCK
        query_block = query_low[row_start:row_stop]
        scores = masked_scores(
            query_block,
            key_low[:row_stop],
            seg_row[row_start:row_stop],
            seg_row[:row_stop],
            row_start,
            scale,
        )
        probs = jnp.exp(scores - log_totals[:, :, row_start:row_stop])
        probs_low = probs.astype(jnp.bfloat16)
        grad_rows = grad_low[row_start:row_stop]
        grad_probs = jnp.einsum(
            "qcgd,kcd->cgqk", grad_rows, value_low[:row_stop], preferred_element_type=jnp.float32
        )
        grad_values = grad_values.at[:row_stop].add(
            jnp.einsum("cgqk,qcgd->kcd", probs_low, grad_rows, preferred_element_type=jnp.float32)
        )
        grad_scores = (
            probs * (grad_probs - jnp.sum(probs * grad_probs, axis=-1, keepdims=True))
        ).astype(jnp.bfloat16)
        query_parts.append(
            jnp.einsum(
                "cgqk,kcd->qcgd",
                grad_scores,
                key_low[:row_stop],
                preferred_element_type=jnp.float32,
            )
            * scale
        )
        grad_keys = grad_keys.at[:row_stop].add(
            jnp.einsum(
                "cgqk,qcgd->kcd", grad_scores, query_block, preferred_element_type=jnp.float32
            )
            * scale
        )
    return (jnp.concatenate(query_parts, axis=0), grad_keys, grad_values)


def swap(value, axis, bit):
    size = lax.axis_size(axis)
    return lax.ppermute(value, axis, [(i, i ^ bit) for i in range(size)])


def axis_bits(axis):
    return [1 << k for k in range(lax.axis_size(axis).bit_length() - 1)]


def gather_blocks(value, axis, bits, dim):
    held, order = value, [0]
    for bit in bits:
        held = jnp.concatenate([held, swap(held, axis, bit)], axis=dim)
        order = order + [r ^ bit for r in order]
    if order != sorted(order):
        parts = jnp.split(held, len(order), axis=dim)
        held = jnp.concatenate([parts[order.index(r)] for r in range(len(order))], axis=dim)
    return held


def scatter_blocks(value, axis, bits, dim):
    count = 1 << len(bits)
    blocks = dict(enumerate(jnp.split(value, count, axis=dim)))
    total = None
    for bit in bits:
        keep = [r for r in sorted(blocks) if not r & bit]
        away = jnp.concatenate([blocks[r ^ bit] for r in keep], axis=dim)
        stay = jnp.concatenate([blocks[r] for r in keep], axis=dim)
        total = stay.astype(jnp.float32) + swap(away, axis, bit).astype(jnp.float32)
        if len(keep) > 1:
            blocks = dict(zip(keep, jnp.split(total.astype(jnp.bfloat16), len(keep), axis=dim)))
    return total


def butterfly_sum(value):
    for axis in ("dp", "tensor"):
        for bit in axis_bits(axis):
            value = value + swap(value, axis, bit)
    return value


def rms_back(values, gain, grad):
    ratio = lax.rsqrt(jnp.mean(values * values, axis=-1, keepdims=True) + EPSILON)
    scaled = grad * gain
    inner = jnp.mean(scaled * values, axis=-1, keepdims=True)
    return ratio * scaled - values * (ratio * ratio * ratio * inner), grad * values * ratio


def on_device(
    tokens,
    segments,
    cotangent,
    query_weight,
    key_weight,
    value_weight,
    out_weight,
    gate_weight,
    up_weight,
    down_weight,
    attention_gain,
    feedfwd_gain,
    query_gain,
    key_gain,
):
    bfloat = jnp.bfloat16
    single = jnp.float32
    head_dim = query_gain.shape[0]
    local_rows, width = tokens.shape
    half_rows = local_rows // 2
    tensor_size, dp_size = lax.axis_size("tensor"), lax.axis_size("dp")
    here, group = lax.axis_index("tensor"), lax.axis_index("dp")
    tensor_bits, dp_bits = axis_bits("tensor"), axis_bits("dp")
    scale = head_dim ** (-0.5)
    half_bits = (tensor_bits, tensor_bits[::-1])
    gather_bits, scatter_bits = dp_bits[::-1], dp_bits

    def weight_gather(value, dim):
        return gather_blocks(value, "dp", gather_bits, dim)

    def rows_gather(halves):
        return [
            gather_blocks(part, "tensor", bits, 0) for part, bits in zip(halves, half_bits)
        ]

    def rows_scatter(halves):
        return [
            scatter_blocks(part, "tensor", bits, 0) for part, bits in zip(halves, half_bits)
        ]

    def halves_of(value):
        return [value[:half_rows], value[half_rows:]]

    def to_natural(halves):
        blocks = [part.reshape(tensor_size, half_rows, -1) for part in halves]
        return jnp.concatenate(
            [
                lax.dynamic_index_in_dim(part, here ^ j, 0, keepdims=False)
                for j in range(tensor_size)
                for part in blocks
            ],
            axis=0,
        )

    def to_relative(value):
        blocks = value.reshape(tensor_size, 2, half_rows, -1)
        return [
            jnp.concatenate(
                [
                    lax.dynamic_index_in_dim(blocks, here ^ r, 0, keepdims=False)[c]
                    for r in range(tensor_size)
                ],
                axis=0,
            )
            for c in range(2)
        ]

    block = width // dp_size
    place = jnp.arange(width, dtype=jnp.int32)
    source = ((place // block) ^ group) * block + place % block
    mixer = (place[:, None] == source[None, :]).astype(bfloat)

    def mix(value):
        return jnp.dot(value, mixer, preferred_element_type=single).astype(bfloat)

    def mix_vector(value):
        blocks = value.reshape(dp_size, block)
        return jnp.concatenate(
            [lax.dynamic_index_in_dim(blocks, group ^ r, 0, keepdims=False) for r in range(dp_size)]
        )

    gain_one, gain_two = mix_vector(attention_gain), mix_vector(feedfwd_gain)
    token_low = mix(tokens)
    token_values = token_low.astype(single)
    normed = rms_scale(token_values, gain_one).astype(bfloat)
    gathered_halves = rows_gather(halves_of(normed))
    qkv_full = weight_gather(
        jnp.concatenate([query_weight, key_weight, value_weight], axis=1), 0
    )
    out_full = weight_gather(out_weight, 1)
    gate_up_full = weight_gather(jnp.concatenate([gate_weight, up_weight], axis=1), 0)
    down_full = weight_gather(down_weight, 1)
    cot_low = mix(cotangent)
    cot_halves = rows_gather(halves_of(cot_low))
    grad_hidden = [
        lax.optimization_barrier(
            jnp.einsum("nd,fd->nf", part, down_full, preferred_element_type=single)
        )
        for part in cot_halves
    ]

    seg_rows = segments.reshape(-1, LEN)
    sequences = seg_rows.shape[0]
    query_cols, key_cols = query_weight.shape[1], key_weight.shape[1]
    key_heads = key_cols // head_dim
    group_size = query_cols // key_cols
    gathered = to_natural(gathered_halves)
    total_rows = gathered.shape[0]
    qkv_raw = jnp.dot(gathered, qkv_full, preferred_element_type=single)
    query_raw = qkv_raw[:, :query_cols]
    key_raw = qkv_raw[:, query_cols : query_cols + key_cols]
    value_low = qkv_raw[:, query_cols + key_cols :].astype(bfloat)
    positions = jax.vmap(doc_positions)(seg_rows).reshape(-1)
    cosine, sine_table = rope_tables(positions, head_dim // 2)
    queries, query_back = jax.vjp(partial(prepare_heads, cosine, sine_table), query_raw, query_gain)
    key_rows, key_back = jax.vjp(partial(prepare_heads, cosine, sine_table), key_raw, key_gain)
    query_low = queries.astype(bfloat).reshape(sequences, LEN, key_heads, group_size, head_dim)
    key_low = key_rows.astype(bfloat).reshape(sequences, LEN, key_heads, head_dim)
    value_seq = value_low.reshape(sequences, LEN, key_heads, head_dim)

    def forward_sequence(inputs_one):
        return attention_forward(inputs_one[0], inputs_one[1], inputs_one[2], inputs_one[3], scale)

    attended, log_totals = lax.map(forward_sequence, (query_low, key_low, value_seq, seg_rows))
    context_low = attended.reshape(total_rows, -1).astype(bfloat)
    out_part = jnp.dot(context_low, out_full, preferred_element_type=single).astype(bfloat)
    attended_sums = rows_scatter(to_relative(out_part))

    residuals, normed_two = [], []
    for token_part, sum_part in zip(halves_of(token_values), attended_sums):
        residuals.append(token_part + sum_part)
        normed_two.append(rms_scale(residuals[-1], gain_two).astype(bfloat))
    two_halves = rows_gather(normed_two)

    hidden_cols = gate_weight.shape[1]
    hidden_low, gate_up_grad = [], []
    for part, grad_part in zip(two_halves, grad_hidden):
        gate_up = jnp.dot(part, gate_up_full, preferred_element_type=single)
        gate_proj, upward = gate_up[:, :hidden_cols], gate_up[:, hidden_cols:]
        sigmoid = 1.0 / (1.0 + jnp.exp(-gate_proj))
        active = gate_proj * sigmoid
        hidden_low.append((active * upward).astype(bfloat))
        gate_grad = grad_part * upward * (sigmoid * (1.0 + gate_proj * (1.0 - sigmoid)))
        gate_up_grad.append(
            jnp.concatenate(
                [gate_grad.astype(bfloat), (grad_part * active).astype(bfloat)], axis=1
            )
        )
    two_sums = rows_scatter(
        [
            jnp.einsum("nf,df->nd", part, gate_up_full, preferred_element_type=single).astype(bfloat)
            for part in gate_up_grad
        ]
    )
    down_sums = rows_scatter(
        [
            jnp.dot(part, down_full, preferred_element_type=single).astype(bfloat)
            for part in hidden_low
        ]
    )
    grad_residual, gain_two_parts = [], []
    for residual_part, sum_part, cot_part in zip(residuals, two_sums, halves_of(cot_low)):
        back, gain_part = rms_back(residual_part, gain_two, sum_part)
        grad_residual.append(cot_part.astype(single) + back)
        gain_two_parts.append(jnp.sum(gain_part, axis=0))
    residual_halves = rows_gather([part.astype(bfloat) for part in grad_residual])
    block_out = mix(
        jnp.concatenate(
            [(res + part).astype(bfloat) for res, part in zip(residuals, down_sums)], axis=0
        )
    )

    def sum_dots(left_parts, right_parts):
        total = 0.0
        for left, right in zip(left_parts, right_parts):
            total = total + jnp.einsum("nd,ne->de", left, right, preferred_element_type=single)
        return total.astype(bfloat)

    def weight_scatter(value, dim):
        return scatter_blocks(value, "dp", scatter_bits, dim)

    grad_gate_up = weight_scatter(sum_dots(two_halves, gate_up_grad), 0)
    grad_down = weight_scatter(sum_dots(hidden_low, cot_halves), 1)

    gathered_grad = to_natural(residual_halves)
    grad_context = jnp.einsum(
        "nd,ed->ne", gathered_grad, out_full, preferred_element_type=single
    ).astype(bfloat)
    grad_context_seq = grad_context.reshape(sequences, LEN, key_heads, group_size, head_dim)

    def backward_sequence(inputs_one):
        query_one, key_one, value_one, seg_one, totals_one, grad_one = inputs_one
        return attention_backward(
            query_one, key_one, value_one, seg_one, totals_one, grad_one, scale
        )

    grad_queries, grad_keys, grad_values = lax.map(
        backward_sequence, (query_low, key_low, value_seq, seg_rows, log_totals, grad_context_seq)
    )
    grad_query_raw, grad_query_norm = query_back(grad_queries.reshape(total_rows, -1, head_dim))
    grad_key_raw, grad_key_norm = key_back(grad_keys.reshape(total_rows, -1, head_dim))
    qkv_grad = jnp.concatenate(
        [
            grad_query_raw.astype(bfloat),
            grad_key_raw.astype(bfloat),
            grad_values.reshape(total_rows, -1).astype(bfloat),
        ],
        axis=1,
    )
    normed_part = jnp.einsum("ne,de->nd", qkv_grad, qkv_full, preferred_element_type=single)
    gain_one_part = jnp.sum(normed_part * gathered.astype(single), axis=0) / gain_one
    normed_sums = rows_scatter(to_relative(normed_part.astype(bfloat)))
    grad_tokens = []
    for token_part, sum_part, grad_part in zip(
        halves_of(token_values), normed_sums, grad_residual
    ):
        back, _ = rms_back(token_part, gain_one, sum_part)
        grad_tokens.append((grad_part + back).astype(bfloat))
    grad_tokens = mix(jnp.concatenate(grad_tokens, axis=0))

    grad_qkv = weight_scatter(sum_dots([gathered], [qkv_grad]), 0)
    grad_out = weight_scatter(sum_dots([context_low], [gathered_grad]), 1)
    gain_sums = butterfly_sum(
        jnp.concatenate(
            [
                mix_vector(gain_one_part),
                mix_vector(gain_two_parts[0] + gain_two_parts[1]),
                grad_query_norm,
                grad_key_norm,
            ]
        )
    )
    return (
        block_out,
        grad_tokens,
        grad_qkv[:, :query_cols],
        grad_qkv[:, query_cols : query_cols + key_cols],
        grad_qkv[:, query_cols + key_cols :],
        grad_out,
        grad_gate_up[:, :hidden_cols],
        grad_gate_up[:, hidden_cols:],
        grad_down,
        gain_sums[:width],
        gain_sums[width : 2 * width],
        gain_sums[2 * width : 2 * width + head_dim],
        gain_sums[2 * width + head_dim :],
    )


def solution(mesh):
    in_specs = (
        P(("dp", "tensor"), None),
        P("dp"),
        P(("dp", "tensor"), None),
        P("dp", "tensor"),
        P("dp", "tensor"),
        P("dp", "tensor"),
        P("tensor", "dp"),
        P("dp", "tensor"),
        P("dp", "tensor"),
        P("tensor", "dp"),
        P(),
        P(),
        P(),
        P(),
    )
    out_specs = (
        P(("dp", "tensor"), None),
        P(("dp", "tensor"), None),
        P("dp", "tensor"),
        P("dp", "tensor"),
        P("dp", "tensor"),
        P("tensor", "dp"),
        P("dp", "tensor"),
        P("dp", "tensor"),
        P("tensor", "dp"),
        P(),
        P(),
        P(),
        P(),
    )
    return jax.shard_map(
        on_device, mesh=mesh, in_specs=in_specs, out_specs=out_specs, check_vma=False
    )
```

```python
from functools import partial
import math

import jax
import jax.numpy as jnp
from jax import lax
from jax.sharding import PartitionSpec as P

LEN = 1024
BLOCK = 512


EPSILON = 1e-05
THETA = 1000000.0
MASKED = -1e30


def rms_scale(values, gain):
    return values * lax.rsqrt(jnp.mean(values * values, axis=-1, keepdims=True) + EPSILON) * gain


def doc_positions(seg_row):
    row_order = jnp.arange(seg_row.shape[0], dtype=jnp.int32)
    starting = jnp.concatenate([jnp.ones((1,), jnp.bool_), seg_row[1:] != seg_row[:-1]])
    starts = lax.cummax(jnp.where(starting, row_order, 0), axis=0)
    return row_order - starts


def rope_tables(positions, half_dim):
    step_index = jnp.arange(half_dim, dtype=jnp.float32)
    inverse = jnp.exp(step_index * (-math.log(THETA) / half_dim))
    angles = positions.astype(jnp.float32)[:, None] * inverse[None, :]
    return (jnp.cos(angles), jnp.sin(angles))


def rotate(values, cosine, sine_table):
    half_dim = values.shape[-1] // 2
    first_half = values[..., :half_dim]
    second = values[..., half_dim:]
    cosine = cosine[:, None, :]
    sine_table = sine_table[:, None, :]
    return jnp.concatenate(
        [first_half * cosine - second * sine_table, second * cosine + first_half * sine_table],
        axis=-1,
    )


def prepare_heads(cosine, sine_table, raw_rows, gain):
    row_total = raw_rows.shape[0]
    return rotate(
        rms_scale(raw_rows.reshape(row_total, -1, gain.shape[0]), gain), cosine, sine_table
    )


def swiglu(gate_proj, upward):
    return jax.nn.silu(gate_proj) * upward


def masked_scores(query_block, key_block, seg_query, seg_key, row_start, scale):
    scores = (
        jnp.einsum("qcgd,kcd->cgqk", query_block, key_block, preferred_element_type=jnp.float32)
        * scale
    )
    query_pos = row_start + jnp.arange(query_block.shape[0], dtype=jnp.int32)
    key_pos = jnp.arange(key_block.shape[0], dtype=jnp.int32)
    allowed = (seg_query[:, None] == seg_key[None, :]) & (key_pos[None, :] <= query_pos[:, None])
    return jnp.where(allowed, scores, MASKED)


def attention_forward(query_low, key_low, value_low, seg_row, scale):
    outputs = []
    totals = []
    for block_index in range(query_low.shape[0] // BLOCK):
        row_start = block_index * BLOCK
        row_stop = row_start + BLOCK
        scores = masked_scores(
            query_low[row_start:row_stop],
            key_low[:row_stop],
            seg_row[row_start:row_stop],
            seg_row[:row_stop],
            row_start,
            scale,
        )
        row_peak = jnp.max(scores, axis=-1, keepdims=True)
        log_total = row_peak + jnp.log(jnp.sum(jnp.exp(scores - row_peak), axis=-1, keepdims=True))
        probs_low = jnp.exp(scores - log_total).astype(jnp.bfloat16)
        outputs.append(
            jnp.einsum(
                "cgqk,kcd->qcgd",
                probs_low,
                value_low[:row_stop],
                preferred_element_type=jnp.float32,
            )
        )
        totals.append(log_total)
    return (jnp.concatenate(outputs, axis=0), jnp.concatenate(totals, axis=2))


def attention_backward(query_low, key_low, value_low, seg_row, log_totals, grad_low, scale):
    query_parts = []
    grad_keys = jnp.zeros(key_low.shape, jnp.float32)
    grad_values = jnp.zeros(value_low.shape, jnp.float32)
    for block_index in range(query_low.shape[0] // BLOCK):
        row_start = block_index * BLOCK
        row_stop = row_start + BLOCK
        query_block = query_low[row_start:row_stop]
        scores = masked_scores(
            query_block,
            key_low[:row_stop],
            seg_row[row_start:row_stop],
            seg_row[:row_stop],
            row_start,
            scale,
        )
        probs = jnp.exp(scores - log_totals[:, :, row_start:row_stop])
        probs_low = probs.astype(jnp.bfloat16)
        grad_rows = grad_low[row_start:row_stop]
        grad_probs = jnp.einsum(
            "qcgd,kcd->cgqk", grad_rows, value_low[:row_stop], preferred_element_type=jnp.float32
        )
        grad_values = grad_values.at[:row_stop].add(
            jnp.einsum("cgqk,qcgd->kcd", probs_low, grad_rows, preferred_element_type=jnp.float32)
        )
        grad_scores = (
            probs * (grad_probs - jnp.sum(probs * grad_probs, axis=-1, keepdims=True))
        ).astype(jnp.bfloat16)
        query_parts.append(
            jnp.einsum(
                "cgqk,kcd->qcgd",
                grad_scores,
                key_low[:row_stop],
                preferred_element_type=jnp.float32,
            )
            * scale
        )
        grad_keys = grad_keys.at[:row_stop].add(
            jnp.einsum(
                "cgqk,qcgd->kcd", grad_scores, query_block, preferred_element_type=jnp.float32
            )
            * scale
        )
    return (jnp.concatenate(query_parts, axis=0), grad_keys, grad_values)


def swap(value, axis, bit):
    size = lax.axis_size(axis)
    return lax.ppermute(value, axis, [(i, i ^ bit) for i in range(size)])


def axis_bits(axis):
    return [1 << k for k in range(lax.axis_size(axis).bit_length() - 1)]


def after(value, *earlier):
    return lax.optimization_barrier((value, *earlier))[0]


def gather_steps(value, axis, bits):
    steps = []
    for bit in bits:
        value = jnp.concatenate([value, swap(value, axis, bit)], axis=0)
        steps.append(value)
    return steps


def block_order(bits):
    order = [0]
    for bit in bits:
        order = order + [r ^ bit for r in order]
    return order


def scatter_steps(value, axis, bits):
    steps = []
    for bit in bits[::-1]:
        rows = value.shape[0] // 2
        total = value[:rows].astype(jnp.float32) + swap(value[rows:], axis, bit).astype(jnp.float32)
        steps.append(total)
        value = total.astype(jnp.bfloat16)
    return steps


def butterfly_sum(value):
    for axis in ("dp", "tensor"):
        for bit in axis_bits(axis):
            value = value + swap(value, axis, bit)
    return value


def rms_back(values, gain, grad):
    ratio = lax.rsqrt(jnp.mean(values * values, axis=-1, keepdims=True) + EPSILON)
    scaled = grad * gain
    inner = jnp.mean(scaled * values, axis=-1, keepdims=True)
    return ratio * scaled - values * (ratio * ratio * ratio * inner), grad * values * ratio


def on_device(
    tokens,
    segments,
    cotangent,
    query_weight,
    key_weight,
    value_weight,
    out_weight,
    gate_weight,
    up_weight,
    down_weight,
    attention_gain,
    feedfwd_gain,
    query_gain,
    key_gain,
):
    bfloat = jnp.bfloat16
    single = jnp.float32
    head_dim = query_gain.shape[0]
    local_rows, width = tokens.shape
    half_rows = local_rows // 2
    tensor_size, here = lax.axis_size("tensor"), lax.axis_index("tensor")
    tensor_bits = axis_bits("tensor")
    scale = head_dim ** (-0.5)
    half_bits = (tensor_bits, tensor_bits[::-1])
    half_order = [block_order(bits) for bits in half_bits]

    def rows_gather(halves):
        return [
            gather_steps(part, "tensor", bits)[-1] for part, bits in zip(halves, half_bits)
        ]

    def rows_scatter(halves):
        return [
            scatter_steps(part, "tensor", bits)[-1] for part, bits in zip(halves, half_bits)
        ]

    def halves_of(value):
        return [value[:half_rows], value[half_rows:]]

    def to_natural(halves):
        blocks = [part.reshape(tensor_size, half_rows, -1) for part in halves]
        places = [jnp.array([order.index(r) for r in range(tensor_size)]) for order in half_order]
        return jnp.concatenate(
            [
                lax.dynamic_index_in_dim(part, place_of[here ^ j], 0, keepdims=False)
                for j in range(tensor_size)
                for part, place_of in zip(blocks, places)
            ],
            axis=0,
        )

    def to_relative(value):
        blocks = value.reshape(tensor_size, 2, half_rows, -1)
        return [
            jnp.concatenate(
                [
                    lax.dynamic_index_in_dim(blocks, here ^ r, 0, keepdims=False)[c]
                    for r in half_order[c]
                ],
                axis=0,
            )
            for c in range(2)
        ]

    gain_one, gain_two = attention_gain, feedfwd_gain
    token_values = tokens.astype(single)
    normed = rms_scale(token_values, gain_one).astype(bfloat)
    gathered_halves = rows_gather(halves_of(normed))
    attention_full = lax.all_gather(
        jnp.concatenate([query_weight, key_weight, value_weight, out_weight.T], axis=1),
        "dp",
        axis=0,
        tiled=True,
    )
    feedfwd_full = lax.all_gather(
        jnp.concatenate([gate_weight, up_weight, down_weight.T], axis=1), "dp", axis=0, tiled=True
    )
    hidden_cols = gate_weight.shape[1]
    query_cols, key_cols = query_weight.shape[1], key_weight.shape[1]
    qkv_cols = query_cols + 2 * key_cols
    qkv_full, out_full = attention_full[:, :qkv_cols], attention_full[:, qkv_cols:]
    gate_up_full = feedfwd_full[:, : 2 * hidden_cols]
    down_full = feedfwd_full[:, 2 * hidden_cols :]
    cot_low = after(cotangent, *gathered_halves)
    cot_halves = rows_gather(halves_of(cot_low))
    grad_hidden = [
        lax.optimization_barrier(
            jnp.einsum("nd,df->nf", part, down_full, preferred_element_type=single)
        )
        for part in cot_halves
    ]

    seg_rows = segments.reshape(-1, LEN)
    sequences = seg_rows.shape[0]
    key_heads = key_cols // head_dim
    group_size = query_cols // key_cols
    gathered = to_natural(gathered_halves)
    total_rows = gathered.shape[0]
    qkv_raw = jnp.dot(gathered, qkv_full, preferred_element_type=single)
    query_raw = qkv_raw[:, :query_cols]
    key_raw = qkv_raw[:, query_cols : query_cols + key_cols]
    value_low = qkv_raw[:, query_cols + key_cols :].astype(bfloat)
    positions = jax.vmap(doc_positions)(seg_rows).reshape(-1)
    cosine, sine_table = rope_tables(positions, head_dim // 2)
    queries, query_back = jax.vjp(partial(prepare_heads, cosine, sine_table), query_raw, query_gain)
    key_rows, key_back = jax.vjp(partial(prepare_heads, cosine, sine_table), key_raw, key_gain)
    query_low = queries.astype(bfloat).reshape(sequences, LEN, key_heads, group_size, head_dim)
    key_low = key_rows.astype(bfloat).reshape(sequences, LEN, key_heads, head_dim)
    value_seq = value_low.reshape(sequences, LEN, key_heads, head_dim)

    def forward_sequence(inputs_one):
        return attention_forward(inputs_one[0], inputs_one[1], inputs_one[2], inputs_one[3], scale)

    attended, log_totals = lax.map(forward_sequence, (query_low, key_low, value_seq, seg_rows))
    context_low = attended.reshape(total_rows, -1).astype(bfloat)
    out_part = jnp.einsum("ne,de->nd", context_low, out_full, preferred_element_type=single).astype(
        bfloat
    )
    attended_sums = rows_scatter(to_relative(out_part))

    residuals, normed_two = [], []
    for token_part, sum_part in zip(halves_of(token_values), attended_sums):
        residuals.append(token_part + sum_part)
        normed_two.append(rms_scale(residuals[-1], gain_two).astype(bfloat))
    two_halves = rows_gather(normed_two)

    hidden_low, gate_up_grad = [], []
    for part, grad_part in zip(two_halves, grad_hidden):
        gate_up = jnp.dot(part, gate_up_full, preferred_element_type=single)
        gate_proj, upward = gate_up[:, :hidden_cols], gate_up[:, hidden_cols:]
        sigmoid = 1.0 / (1.0 + jnp.exp(-gate_proj))
        active = gate_proj * sigmoid
        hidden_low.append((active * upward).astype(bfloat))
        gate_grad = grad_part * upward * (sigmoid * (1.0 + gate_proj * (1.0 - sigmoid)))
        gate_up_grad.append(
            jnp.concatenate(
                [gate_grad.astype(bfloat), (grad_part * active).astype(bfloat)], axis=1
            )
        )
    two_parts = [
        jnp.einsum("nf,df->nd", part, gate_up_full, preferred_element_type=single).astype(bfloat)
        for part in gate_up_grad
    ]
    two_sums = rows_scatter(two_parts)
    hidden_low[0] = after(hidden_low[0], two_parts[1])
    gate_up_grad[0] = after(gate_up_grad[0], two_parts[1])
    down_sums = rows_scatter(
        [
            jnp.einsum("nf,df->nd", part, down_full, preferred_element_type=single).astype(bfloat)
            for part in hidden_low
        ]
    )
    grad_residual, gain_two_parts = [], []
    for residual_part, sum_part, cot_part in zip(residuals, two_sums, halves_of(cot_low)):
        back, gain_part = rms_back(residual_part, gain_two, sum_part)
        grad_residual.append(cot_part.astype(single) + back)
        gain_two_parts.append(jnp.sum(gain_part, axis=0))
    residual_halves = rows_gather([part.astype(bfloat) for part in grad_residual])
    block_out = jnp.concatenate(
        [(res + part).astype(bfloat) for res, part in zip(residuals, down_sums)], axis=0
    )

    def sum_dots(left_parts, right_parts):
        total = 0.0
        for left, right in zip(left_parts, right_parts):
            total = total + jnp.einsum("nd,ne->de", left, right, preferred_element_type=single)
        return total.astype(bfloat)

    def weight_scatter(value):
        return lax.psum_scatter(value, "dp", scatter_dimension=0, tiled=True).astype(single)

    down_part = sum_dots(cot_halves, hidden_low)
    gate_up_part = sum_dots(two_halves, gate_up_grad)
    grad_down = weight_scatter(down_part)
    gathered_grad = after(to_natural(residual_halves), gate_up_part, down_part)
    grad_gate_up = weight_scatter(gate_up_part)
    grad_context = jnp.einsum(
        "nd,de->ne", gathered_grad, out_full, preferred_element_type=single
    ).astype(bfloat)
    grad_context_seq = grad_context.reshape(sequences, LEN, key_heads, group_size, head_dim)

    def backward_sequence(inputs_one):
        query_one, key_one, value_one, seg_one, totals_one, grad_one = inputs_one
        return attention_backward(
            query_one, key_one, value_one, seg_one, totals_one, grad_one, scale
        )

    grad_queries, grad_keys, grad_values = lax.map(
        backward_sequence, (query_low, key_low, value_seq, seg_rows, log_totals, grad_context_seq)
    )
    grad_query_raw, grad_query_norm = query_back(grad_queries.reshape(total_rows, -1, head_dim))
    grad_key_raw, grad_key_norm = key_back(grad_keys.reshape(total_rows, -1, head_dim))
    qkv_grad = jnp.concatenate(
        [
            grad_query_raw.astype(bfloat),
            grad_key_raw.astype(bfloat),
            grad_values.reshape(total_rows, -1).astype(bfloat),
        ],
        axis=1,
    )
    normed_part = jnp.einsum("ne,de->nd", qkv_grad, qkv_full, preferred_element_type=single)
    gain_one_part = jnp.sum(normed_part * gathered.astype(single), axis=0) / gain_one
    normed_sums = rows_scatter(to_relative(normed_part.astype(bfloat)))
    grad_tokens = []
    for token_part, sum_part, grad_part in zip(
        halves_of(token_values), normed_sums, grad_residual
    ):
        back, _ = rms_back(token_part, gain_one, sum_part)
        grad_tokens.append((grad_part + back).astype(bfloat))
    grad_tokens = jnp.concatenate(grad_tokens, axis=0)

    attention_part = jnp.concatenate(
        [sum_dots([gathered], [qkv_grad]), sum_dots([gathered_grad], [context_low])], axis=1
    )
    grad_attention = weight_scatter(after(attention_part, grad_gate_up, grad_down))
    gain_sums = butterfly_sum(
        jnp.concatenate(
            [
                gain_one_part,
                gain_two_parts[0] + gain_two_parts[1],
                grad_query_norm,
                grad_key_norm,
            ]
        )
    )
    return (
        block_out,
        grad_tokens,
        grad_attention[:, :query_cols],
        grad_attention[:, query_cols : query_cols + key_cols],
        grad_attention[:, query_cols + key_cols : qkv_cols],
        grad_attention[:, qkv_cols:].T,
        grad_gate_up[:, :hidden_cols],
        grad_gate_up[:, hidden_cols:],
        grad_down.T,
        gain_sums[:width],
        gain_sums[width : 2 * width],
        gain_sums[2 * width : 2 * width + head_dim],
        gain_sums[2 * width + head_dim :],
    )


def solution(mesh):
    in_specs = (
        P(("dp", "tensor"), None),
        P("dp"),
        P(("dp", "tensor"), None),
        P("dp", "tensor"),
        P("dp", "tensor"),
        P("dp", "tensor"),
        P("tensor", "dp"),
        P("dp", "tensor"),
        P("dp", "tensor"),
        P("tensor", "dp"),
        P(),
        P(),
        P(),
        P(),
    )
    out_specs = (
        P(("dp", "tensor"), None),
        P(("dp", "tensor"), None),
        P("dp", "tensor"),
        P("dp", "tensor"),
        P("dp", "tensor"),
        P("tensor", "dp"),
        P("dp", "tensor"),
        P("dp", "tensor"),
        P("tensor", "dp"),
        P(),
        P(),
        P(),
        P(),
    )
    return jax.shard_map(
        on_device, mesh=mesh, in_specs=in_specs, out_specs=out_specs, check_vma=False
    )
```

```python
from functools import partial
import math

import jax
import jax.numpy as jnp
from jax import lax
from jax.experimental import pallas as pl
from jax.experimental.pallas import tpu as pltpu
from jax.sharding import PartitionSpec as P

LEN = 1024


EPSILON = 1e-05
THETA = 1000000.0
MASKED = -1e30
DOCUMENTS = 3
SHORTEST = 204
TILE = 256
LOG2E = math.log2(math.e)
VMEM_LIMIT = 56 * 2**20
HEAVY, LIGHT = 16 * 10**9, 10**9
BFLOAT, SINGLE = jnp.bfloat16, jnp.float32


def call_kernel(kernel, name, weight, shapes, scalars, arrays, scratch=(), earlier=(), **grid):
    whole = pl.BlockSpec(memory_space=pltpu.VMEM)
    specs = [pl.BlockSpec(memory_space=pltpu.SMEM)] * len(scalars) + [whole] * len(arrays)
    return pl.pallas_call(
        kernel,
        out_shape=[jax.ShapeDtypeStruct(*shape) for shape in shapes],
        in_specs=specs + [pl.BlockSpec(memory_space=pl.ANY)] * len(earlier),
        out_specs=[whole] * len(shapes),
        scratch_shapes=[pltpu.VMEM(*shape) for shape in scratch],
        compiler_params=pltpu.CompilerParams(vmem_limit_bytes=VMEM_LIMIT),
        cost_estimate=pl.CostEstimate(flops=weight, bytes_accessed=2**20, transcendentals=0),
        name=name,
    )(*scalars, *arrays, *earlier)


def dot(left, right):
    return jnp.dot(left, right, preferred_element_type=SINGLE)


def dot_last(left, right):
    return lax.dot_general(left, right, (((1,), (1,)), ((), ())), preferred_element_type=SINGLE)


def key_span(start):
    reach = LEN - (DOCUMENTS - 1) * SHORTEST - 1
    return max(0, (start - reach) // 128 * 128), start + TILE


def mask_bias(begin_ref, start, low, high):
    shape = (high - low, TILE)
    key_pos = low + lax.broadcasted_iota(jnp.int32, shape, 0)
    query_pos = start + lax.broadcasted_iota(jnp.int32, shape, 1)
    counts = (key_pos >= begin_ref[:, start : start + TILE]) & (key_pos <= query_pos)
    return jnp.where(counts, 0.0, MASKED)


def head_ratio(values):
    return lax.rsqrt(jnp.mean(values * values, axis=0, keepdims=True) + EPSILON)


def turn(values, cosine, sine):
    half_dim = values.shape[0] // 2
    first, second = values[:half_dim], values[half_dim:]
    return jnp.concatenate([first * cosine - second * sine, second * cosine + first * sine], axis=0)


def gain_columns(gain_ref, head_dim):
    turned = jnp.broadcast_to(gain_ref[...], (8, gain_ref.shape[1])).T
    return turned[:head_dim, :1], turned[head_dim : 2 * head_dim, :1]


def spread(place_ref, natural, out_ref):
    rows = LEN // place_ref.shape[0]
    for block in range(place_ref.shape[0]):
        start = pl.multiple_of(place_ref[block], rows)
        out_ref[pl.ds(start, rows), :] = natural[block * rows : (block + 1) * rows, :]


def collect(place_ref, value_ref, natural):
    rows = LEN // place_ref.shape[0]
    for block in range(place_ref.shape[0]):
        start = pl.multiple_of(place_ref[block], rows)
        natural[block * rows : (block + 1) * rows, :] = value_ref[pl.ds(start, rows), :]


def attend_kernel(
    sizes,
    place_ref,
    rows_a_ref,
    rows_b_ref,
    rows_c_ref,
    rows_d_ref,
    weight_ref,
    gain_ref,
    segment_ref,
    raw_ref,
    query_ref,
    key_ref,
    query_row_ref,
    key_row_ref,
    value_row_ref,
    total_ref,
    attended_ref,
    cosine_ref,
    sine_ref,
    begin_ref,
    context_ref,
    part_a_ref,
    part_b_ref,
    part_c_ref,
    part_d_ref,
    mixed,
    natural,
    extended,
    bias,
    context,
):
    query_heads, key_heads, head_dim = sizes
    group_size = query_heads // key_heads
    heads = query_heads + key_heads
    columns = natural.shape[1]
    quarter = rows_a_ref.shape[0]
    weight = weight_ref[:, :columns]
    for q, rows_ref in enumerate((rows_a_ref, rows_b_ref, rows_c_ref, rows_d_ref)):
        mixed[q * quarter : (q + 1) * quarter, :] = dot(rows_ref[...], weight)
    collect(place_ref, mixed, natural)
    for start in range(0, LEN, 128):
        raw_ref[:, start : start + 128] = natural[start : start + 128, :].T

    segment = segment_ref[...]
    first_count = jnp.sum((segment == 0).astype(SINGLE), axis=1, keepdims=True)
    second_count = jnp.sum((segment == 1).astype(SINGLE), axis=1, keepdims=True)
    begin = jnp.where(
        segment == 0, 0.0, jnp.where(segment == 1, first_count, first_count + second_count)
    )
    begin_ref[...] = begin.astype(jnp.int32)
    half_dim = head_dim // 2
    shape = (half_dim, LEN)
    steps = lax.broadcasted_iota(jnp.int32, shape, 0).astype(SINGLE)
    order = lax.broadcasted_iota(jnp.int32, shape, 1).astype(SINGLE)
    angles = (order - begin) * jnp.exp(steps * (-math.log(THETA) / half_dim))
    cosine, sine = jnp.cos(angles), jnp.sin(angles)
    cosine_ref[...] = cosine
    sine_ref[...] = sine

    gains = gain_columns(gain_ref, head_dim)
    for head in range(heads):
        values = raw_ref[head * head_dim : (head + 1) * head_dim, :]
        gain = gains[0] if head < query_heads else gains[1]
        turned = turn(values * head_ratio(values) * gain, cosine, sine)
        if head < query_heads:
            query_ref[head] = turned.astype(BFLOAT)
            query_row_ref[head] = turned.T.astype(BFLOAT)
        else:
            key_ref[head - query_heads] = turned.astype(BFLOAT)
            key_row_ref[head - query_heads] = turned.T.astype(BFLOAT)
    for head in range(key_heads):
        first = (heads + head) * head_dim
        extended[head, :head_dim, :] = raw_ref[first : first + head_dim, :].astype(BFLOAT)
        extended[head, head_dim:, :] = jnp.ones((extended.shape[1] - head_dim, LEN), BFLOAT)
        value_row_ref[head] = natural[:, first : first + head_dim].astype(BFLOAT)
    factor = LOG2E * head_dim ** (-0.5)
    for start in range(0, LEN, TILE):
        low, high = key_span(start)
        span, tile = slice(low, high), slice(start, start + TILE)
        bias[: high - low, :] = mask_bias(begin_ref, start, low, high)

        def one_head(head, carry):
            key_head = head // group_size
            scores = dot(key_row_ref[key_head, span, :], query_ref[head, :, tile])
            powers = jnp.exp2(scores * factor + bias[: high - low, :])
            summed = dot(extended[key_head, :, span], powers.astype(BFLOAT))
            total = summed[head_dim : head_dim + 1, :]
            total_ref[head, :, tile] = jnp.log2(total)
            attended_ref[head, :, tile] = summed[:head_dim, :] / total
            return carry

        lax.fori_loop(0, query_heads, one_head, 0)
    for head in range(query_heads):
        context[:, head * head_dim : (head + 1) * head_dim] = attended_ref[head].T.astype(BFLOAT)
    spread(place_ref, context, context_ref)
    out_weight = weight_ref[:, columns:]
    for q, part_ref in enumerate((part_a_ref, part_b_ref, part_c_ref, part_d_ref)):
        rows = context_ref[q * quarter : (q + 1) * quarter, :]
        part_ref[...] = dot_last(rows, out_weight).astype(BFLOAT)


def attend(sizes, place, quarters, weight, gains, segments):
    query_heads, key_heads, head_dim = sizes
    columns = (query_heads + 2 * key_heads) * head_dim
    quarter, width = quarters[0].shape
    shapes = [
        ((columns, LEN), SINGLE),
        ((query_heads, head_dim, LEN), BFLOAT),
        ((key_heads, head_dim, LEN), BFLOAT),
        ((query_heads, LEN, head_dim), BFLOAT),
        ((key_heads, LEN, head_dim), BFLOAT),
        ((key_heads, LEN, head_dim), BFLOAT),
        ((query_heads, 1, LEN), SINGLE),
        ((query_heads, head_dim, LEN), SINGLE),
        ((head_dim // 2, LEN), SINGLE),
        ((head_dim // 2, LEN), SINGLE),
        ((1, LEN), jnp.int32),
        ((LEN, query_heads * head_dim), BFLOAT),
    ] + [((quarter, width), BFLOAT)] * 4
    scratch = [
        ((LEN, columns), SINGLE),
        ((LEN, columns), SINGLE),
        ((key_heads, head_dim + 16, LEN), BFLOAT),
        ((LEN, TILE), SINGLE),
        ((LEN, query_heads * head_dim), BFLOAT),
    ]
    arrays = (*quarters, weight, gains, segments)
    outs = call_kernel(
        partial(attend_kernel, sizes), "attend", HEAVY, shapes, (place,), arrays, scratch
    )
    return outs[:11], outs[11], outs[12:]


def attend_back_kernel(
    sizes,
    place_ref,
    grad_a_ref,
    grad_b_ref,
    grad_c_ref,
    grad_d_ref,
    rows_a_ref,
    rows_b_ref,
    rows_c_ref,
    rows_d_ref,
    weight_ref,
    gain_ref,
    raw_ref,
    query_ref,
    key_ref,
    query_row_ref,
    key_row_ref,
    value_row_ref,
    total_ref,
    attended_ref,
    cosine_ref,
    sine_ref,
    begin_ref,
    out_ref,
    head_gain_ref,
    row_gain_ref,
    part_a_ref,
    part_b_ref,
    part_c_ref,
    part_d_ref,
    mixed,
    context,
    grad_row,
    grad_col,
    query_grad,
    key_grad,
    value_grad,
    joined,
    natural,
    bias,
):
    query_heads, key_heads, head_dim = sizes
    group_size = query_heads // key_heads
    heads = query_heads + key_heads
    columns = natural.shape[1]
    quarter = grad_a_ref.shape[0]
    out_weight = weight_ref[:, columns:]
    for q, rows_ref in enumerate((grad_a_ref, grad_b_ref, grad_c_ref, grad_d_ref)):
        mixed[q * quarter : (q + 1) * quarter, :] = dot(rows_ref[...], out_weight).astype(BFLOAT)
    collect(place_ref, mixed, context)
    for head in range(query_heads):
        part = context[:, head * head_dim : (head + 1) * head_dim]
        grad_row[head] = part
        grad_col[head] = part.astype(SINGLE).T
    key_grad[...] = jnp.zeros(key_grad.shape, SINGLE)
    value_grad[...] = jnp.zeros(value_grad.shape, SINGLE)
    scale = head_dim ** (-0.5)
    factor = LOG2E * scale
    for start in range(0, LEN, TILE):
        low, high = key_span(start)
        span, tile = slice(low, high), slice(start, start + TILE)
        bias[: high - low, :] = mask_bias(begin_ref, start, low, high)

        def one_head(head, carry):
            key_head = head // group_size
            scores = dot(key_row_ref[key_head, span, :], query_ref[head, :, tile])
            probs = jnp.exp2(scores * factor + bias[: high - low, :] - total_ref[head, :, tile])
            grads = grad_col[head, :, tile]
            inner = jnp.sum(grads * attended_ref[head, :, tile], axis=0, keepdims=True)
            probs_grad = dot(value_row_ref[key_head, span, :], grads.astype(BFLOAT))
            scores_grad = (probs * (probs_grad - inner)).astype(BFLOAT)
            value_grad[key_head, span, :] += dot(probs.astype(BFLOAT), grad_row[head, tile, :])
            key_grad[key_head, span, :] += dot(scores_grad, query_row_ref[head, tile, :])
            query_grad[head, :, tile] = dot(key_ref[key_head, :, span], scores_grad)
            return carry

        lax.fori_loop(0, query_heads, one_head, 0)
    cosine, sine = cosine_ref[...], sine_ref[...]
    gains = gain_columns(gain_ref, head_dim)
    for kind in range(2):
        head_gain_ref[kind] = jnp.zeros(head_gain_ref.shape[1:], SINGLE)
    for head in range(heads):
        kind = 0 if head < query_heads else 1
        grads = query_grad[head] if kind == 0 else key_grad[head - query_heads].T
        grads = turn(grads * scale, cosine, -sine)
        values = raw_ref[head * head_dim : (head + 1) * head_dim, :]
        ratio = head_ratio(values)
        normed = values * ratio
        weighted = grads * gains[kind]
        inner = jnp.mean(weighted * normed, axis=0, keepdims=True)
        joined[head * head_dim : (head + 1) * head_dim, :] = ratio * (weighted - normed * inner)
        products = grads * normed
        folded = products[:, :128]
        for first in range(128, LEN, 128):
            folded = folded + products[:, first : first + 128]
        head_gain_ref[kind] += folded
    for start in range(0, LEN, 128):
        natural[start : start + 128, : heads * head_dim] = joined[:, start : start + 128].T.astype(
            BFLOAT
        )
    for head in range(key_heads):
        first = (heads + head) * head_dim
        natural[:, first : first + head_dim] = value_grad[head].astype(BFLOAT)
    spread(place_ref, natural, out_ref)
    weight = weight_ref[:, :columns]
    row_gain = jnp.zeros(row_gain_ref.shape, SINGLE)
    rows_refs = (rows_a_ref, rows_b_ref, rows_c_ref, rows_d_ref)
    for q, part_ref in enumerate((part_a_ref, part_b_ref, part_c_ref, part_d_ref)):
        part = dot_last(out_ref[q * quarter : (q + 1) * quarter, :], weight)
        part_ref[...] = part.astype(BFLOAT)
        row_gain += jnp.sum(part * rows_refs[q][...].astype(SINGLE), axis=0, keepdims=True)
    row_gain_ref[...] = row_gain


def attend_back(sizes, place, grads, quarters, weight, gains, saved):
    query_heads, key_heads, head_dim = sizes
    heads = query_heads + key_heads
    columns = (heads + key_heads) * head_dim
    quarter, width = quarters[0].shape
    shapes = [
        ((LEN, columns), BFLOAT),
        ((2, head_dim, 128), SINGLE),
        ((1, width), SINGLE),
    ] + [((quarter, width), BFLOAT)] * 4
    scratch = [
        ((LEN, query_heads * head_dim), BFLOAT),
        ((LEN, query_heads * head_dim), BFLOAT),
        ((query_heads, LEN, head_dim), BFLOAT),
        ((query_heads, head_dim, LEN), SINGLE),
        ((query_heads, head_dim, LEN), SINGLE),
        ((key_heads, LEN, head_dim), SINGLE),
        ((key_heads, LEN, head_dim), SINGLE),
        ((heads * head_dim, LEN), SINGLE),
        ((LEN, columns), BFLOAT),
        ((LEN, TILE), SINGLE),
    ]
    arrays = (*grads, *quarters, weight, gains, *saved)
    outs = call_kernel(
        partial(attend_back_kernel, sizes), "attend_back", HEAVY, shapes, (place,), arrays, scratch
    )
    return outs[0], outs[1], outs[2], outs[3:]


def feedfwd_kernel(
    rows_a_ref,
    rows_b_ref,
    rows_c_ref,
    rows_d_ref,
    cot_a_ref,
    cot_b_ref,
    cot_c_ref,
    cot_d_ref,
    weight_ref,
    hidden_ref,
    grad_ref,
    part_a_ref,
    part_b_ref,
    part_c_ref,
    part_d_ref,
    gate_up,
    grad_hidden,
):
    hidden_cols = hidden_ref.shape[1]
    quarter = rows_a_ref.shape[0]
    step = 384 if hidden_cols % 384 == 0 else hidden_cols
    quarters = (
        (rows_a_ref, cot_a_ref, part_a_ref),
        (rows_b_ref, cot_b_ref, part_b_ref),
        (rows_c_ref, cot_c_ref, part_c_ref),
        (rows_d_ref, cot_d_ref, part_d_ref),
    )
    for q, (rows_ref, cot_ref, part_ref) in enumerate(quarters):
        tile, slot = slice(q * quarter, (q + 1) * quarter), q % 2
        gate_up[slot] = dot(rows_ref[...], weight_ref[:, : 2 * hidden_cols])
        grad_hidden[slot] = dot(cot_ref[...], weight_ref[:, 2 * hidden_cols :])
        for first in range(0, hidden_cols, step):
            cols = slice(first, first + step)
            up_cols = slice(hidden_cols + first, hidden_cols + first + step)
            gate_proj, upward = gate_up[slot, :, cols], gate_up[slot, :, up_cols]
            grads = grad_hidden[slot, :, cols]
            sigmoid = 1.0 / (1.0 + jnp.exp(-gate_proj))
            active = gate_proj * sigmoid
            hidden_ref[tile, cols] = (active * upward).astype(BFLOAT)
            slope = sigmoid * (1.0 + gate_proj * (1.0 - sigmoid))
            grad_ref[tile, cols] = (grads * upward * slope).astype(BFLOAT)
            grad_ref[tile, up_cols] = (grads * active).astype(BFLOAT)
        part_ref[...] = dot_last(grad_ref[tile, :], weight_ref[:, : 2 * hidden_cols]).astype(BFLOAT)


def feedfwd(quarters, cots, weight):
    quarter, width = quarters[0].shape
    hidden_cols = weight.shape[1] // 3
    shapes = [((LEN, hidden_cols), BFLOAT), ((LEN, 2 * hidden_cols), BFLOAT)]
    shapes += [((quarter, width), BFLOAT)] * 4
    scratch = [((2, quarter, 2 * hidden_cols), SINGLE), ((2, quarter, hidden_cols), SINGLE)]
    outs = call_kernel(
        feedfwd_kernel, "feedfwd", HEAVY, shapes, (), (*quarters, *cots, weight), scratch
    )
    return outs[0], outs[1], outs[2:]


def weights_kernel(
    first_tiles,
    first_a_ref,
    first_b_ref,
    first_c_ref,
    first_d_ref,
    second_a_ref,
    second_b_ref,
    second_c_ref,
    second_d_ref,
    first_grad_ref,
    second_grad_ref,
    out_ref,
    turned_ref,
):
    step = pl.program_id(0)
    quarter = first_a_ref.shape[0]

    def turn_over(*refs):
        for q, ref in enumerate(refs):
            turned_ref[:, q * quarter : (q + 1) * quarter] = ref[...].T

    @pl.when(step == 0)
    def _():
        turn_over(first_a_ref, first_b_ref, first_c_ref, first_d_ref)

    @pl.when(step < first_tiles)
    def _():
        out_ref[...] = dot(turned_ref[...], first_grad_ref[...]).astype(BFLOAT)

    @pl.when(step == first_tiles)
    def _():
        turn_over(second_a_ref, second_b_ref, second_c_ref, second_d_ref)

    @pl.when(step >= first_tiles)
    def _():
        out_ref[...] = dot(turned_ref[...], second_grad_ref[...]).astype(BFLOAT)


def weight_parts(firsts, first_grad, seconds, second_grad):
    first_cols, second_cols = first_grad.shape[1], second_grad.shape[1]
    quarter, width = firsts[0].shape
    tiles = [t for t in (1152, 256, 128) if first_cols % t == 0 and second_cols % t == 0]
    if not tiles:
        sums = []
        for lefts, right in ((firsts, first_grad), (seconds, second_grad)):
            left = jnp.concatenate(lefts, axis=0)
            total = jnp.einsum("nd,ne->de", left, right, preferred_element_type=SINGLE)
            sums.append(total.astype(BFLOAT))
        return jnp.concatenate(sums, axis=1)
    tile = tiles[0]
    first_tiles = first_cols // tile
    whole = pl.BlockSpec((quarter, width), lambda j: (0, 0))
    first_spec = pl.BlockSpec((LEN, tile), lambda j: (0, jnp.minimum(j, first_tiles - 1)))
    second_spec = pl.BlockSpec((LEN, tile), lambda j: (0, jnp.maximum(j - first_tiles, 0)))
    columns = first_cols + second_cols
    return pl.pallas_call(
        partial(weights_kernel, first_tiles),
        grid=(columns // tile,),
        out_shape=jax.ShapeDtypeStruct((width, columns), BFLOAT),
        in_specs=[whole] * 8 + [first_spec, second_spec],
        out_specs=pl.BlockSpec((width, tile), lambda j: (0, j)),
        scratch_shapes=[pltpu.VMEM((width, LEN), BFLOAT)],
        compiler_params=pltpu.CompilerParams(vmem_limit_bytes=VMEM_LIMIT),
        cost_estimate=pl.CostEstimate(flops=LIGHT, bytes_accessed=2**20, transcendentals=0),
        name="weight_parts",
    )(*firsts, *seconds, first_grad, second_grad)


def pair_sum_kernel(stay_a_ref, got_a_ref, stay_b_ref, got_b_ref, *refs):
    outs = refs[-4:]
    rows = stay_a_ref.shape[0] // 2
    pairs = ((stay_a_ref, got_a_ref), (stay_b_ref, got_b_ref))
    for half, (stay_ref, got_ref) in enumerate(pairs):
        total = stay_ref[...].astype(SINGLE) + got_ref[...].astype(SINGLE)
        outs[2 * half][...] = total[:rows].astype(outs[2 * half].dtype)
        outs[2 * half + 1][...] = total[rows:].astype(BFLOAT)


def pair_sum(stays, gots, last, earlier):
    rows, width = stays[0].shape
    shapes = [((rows // 2, width), SINGLE if last else BFLOAT), ((rows // 2, width), BFLOAT)] * 2
    arrays = (stays[0], gots[0], stays[1], gots[1])
    outs = call_kernel(
        pair_sum_kernel, "pair_sum", LIGHT, shapes, (), arrays, earlier=earlier
    )
    return outs[0::2], outs[1::2]


def down_kernel(hidden_ref, weight_ref, *refs):
    quarter = hidden_ref.shape[0] // 4
    for q, part_ref in enumerate(refs[-4:]):
        rows = hidden_ref[q * quarter : (q + 1) * quarter, :]
        part_ref[...] = dot_last(rows, weight_ref[...]).astype(BFLOAT)


def down_parts_of(hidden, weight, earlier):
    hidden_cols = hidden.shape[1]
    quarter, width = LEN // 4, weight.shape[0]
    if hidden_cols % 128:
        down = weight[:, 2 * hidden_cols :]
        return [
            dot_last(hidden[q * quarter : (q + 1) * quarter], down).astype(BFLOAT) for q in range(4)
        ]
    part = pl.BlockSpec((quarter, width), lambda i: (0, 0))
    return pl.pallas_call(
        down_kernel,
        grid=(1,),
        out_shape=[jax.ShapeDtypeStruct((quarter, width), BFLOAT)] * 4,
        in_specs=[
            pl.BlockSpec((LEN, hidden_cols), lambda i: (0, 0)),
            pl.BlockSpec((width, hidden_cols), lambda i: (0, 2)),
        ]
        + [pl.BlockSpec(memory_space=pl.ANY)] * len(earlier),
        out_specs=[part] * 4,
        compiler_params=pltpu.CompilerParams(vmem_limit_bytes=VMEM_LIMIT),
        cost_estimate=pl.CostEstimate(flops=LIGHT, bytes_accessed=2**20, transcendentals=0),
        name="down_parts",
    )(hidden, weight, *earlier)


def later(value, earlier):
    anywhere = pl.BlockSpec(memory_space=pl.ANY)
    return pl.pallas_call(
        lambda *refs: None,
        out_shape=jax.ShapeDtypeStruct(value.shape, value.dtype),
        in_specs=[anywhere, anywhere],
        out_specs=anywhere,
        input_output_aliases={0: 0},
        name="later",
    )(value, earlier)


def rms_scale(values, gain):
    return values * lax.rsqrt(jnp.mean(values * values, axis=-1, keepdims=True) + EPSILON) * gain


def swap(value, axis, bit):
    size = lax.axis_size(axis)
    return lax.ppermute(value, axis, [(i, i ^ bit) for i in range(size)])


def axis_bits(axis):
    return [1 << k for k in range(lax.axis_size(axis).bit_length() - 1)]


def block_order(bits):
    order = [0]
    for bit in bits:
        order = order + [r ^ bit for r in order]
    return order


def butterfly_sum(value):
    for axis in ("dp", "tensor"):
        for bit in axis_bits(axis):
            value = value + swap(value, axis, bit)
    return value


def rms_back(values, gain, grad):
    ratio = lax.rsqrt(jnp.mean(values * values, axis=-1, keepdims=True) + EPSILON)
    scaled = grad * gain
    inner = jnp.mean(scaled * values, axis=-1, keepdims=True)
    return ratio * scaled - values * (ratio * ratio * ratio * inner), grad * values * ratio


def on_device(
    tokens,
    segments,
    cotangent,
    query_weight,
    key_weight,
    value_weight,
    out_weight,
    gate_weight,
    up_weight,
    down_weight,
    attention_gain,
    feedfwd_gain,
    query_gain,
    key_gain,
):
    head_dim = query_gain.shape[0]
    local_rows, width = tokens.shape
    half_rows = local_rows // 2
    tensor_size, here = lax.axis_size("tensor"), lax.axis_index("tensor")
    tensor_bits = axis_bits("tensor")
    half_bits = (tensor_bits, tensor_bits[::-1])
    half_order = [block_order(bits) for bits in half_bits]
    place = jnp.stack(
        [
            jnp.array([order.index(r) for r in range(tensor_size)], jnp.int32)[here ^ j] * half_rows
            + c * (LEN // 2)
            for j in range(tensor_size)
            for c, order in enumerate(half_order)
        ]
    )

    def rows_gather(halves):
        for bits in zip(*half_bits):
            pairs = [(part, swap(part, "tensor", bit)) for part, bit in zip(halves, bits)]
            halves = [jnp.concatenate(pair, axis=0) for pair in pairs]
        return [*pairs[0], *pairs[1]]

    def rows_scatter(parts, earlier=()):
        stays, aways = parts[0::2], parts[1::2]
        for step, bits in enumerate(zip(*(bits[::-1] for bits in half_bits))):
            gots = [swap(part, "tensor", bit) for part, bit in zip(aways, bits)]
            if step < len(tensor_bits) - 1:
                last = step == len(tensor_bits) - 2
                stays, aways = pair_sum(stays, gots, last, earlier)
                earlier = ()
        return [stay.astype(SINGLE) + got.astype(SINGLE) for stay, got in zip(stays, gots)]

    def halves_of(value):
        return [value[:half_rows], value[half_rows:]]

    token_values = tokens.astype(SINGLE)
    normed = rms_scale(token_values, attention_gain).astype(BFLOAT)
    gathered = rows_gather(halves_of(normed))
    attention_full = lax.all_gather(
        jnp.concatenate([query_weight, key_weight, value_weight, out_weight.T], axis=1),
        "dp",
        axis=0,
        tiled=True,
    )
    feedfwd_full = lax.all_gather(
        jnp.concatenate([gate_weight, up_weight, down_weight.T], axis=1), "dp", axis=0, tiled=True
    )
    cots = rows_gather(halves_of(cotangent))

    hidden_cols = gate_weight.shape[1]
    query_cols, key_cols = query_weight.shape[1], key_weight.shape[1]
    qkv_cols = query_cols + 2 * key_cols
    sizes = (query_cols // head_dim, key_cols // head_dim, head_dim)
    gains = jnp.concatenate([query_gain, key_gain])[None, :]
    saved, context, attended_parts = attend(
        sizes, place, gathered, attention_full, gains, segments[None, :]
    )
    residuals, normed_two = [], []
    for token_part, sum_part in zip(halves_of(token_values), rows_scatter(attended_parts)):
        residuals.append(token_part + sum_part)
        normed_two.append(rms_scale(residuals[-1], feedfwd_gain).astype(BFLOAT))
    gathered_two = rows_gather(normed_two)

    hidden, gate_up_grad, two_parts = feedfwd(gathered_two, cots, feedfwd_full)
    feedfwd_part = weight_parts(gathered_two, gate_up_grad, cots, hidden)
    grad_feedfwd = lax.psum_scatter(feedfwd_part, "dp", scatter_dimension=0, tiled=True)
    two_sums = rows_scatter(two_parts, (feedfwd_part,))
    grad_residual, gain_two_part = [], 0.0
    for residual_part, sum_part, cot_part in zip(residuals, two_sums, halves_of(cotangent)):
        back, gain_part = rms_back(residual_part, feedfwd_gain, sum_part)
        grad_residual.append(cot_part.astype(SINGLE) + back)
        gain_two_part = gain_two_part + jnp.sum(gain_part, axis=0)
    gathered_grad = rows_gather([part.astype(BFLOAT) for part in grad_residual])

    qkv_grad, head_gains, row_gain, normed_parts = attend_back(
        sizes, place, gathered_grad, gathered, attention_full, gains, saved
    )
    attention_part = weight_parts(gathered, qkv_grad, gathered_grad, context)
    grad_attention = lax.psum_scatter(
        later(attention_part, grad_feedfwd), "dp", scatter_dimension=0, tiled=True
    )
    normed_sums = rows_scatter(normed_parts)
    grad_tokens = []
    for token_part, sum_part, grad_part in zip(
        halves_of(token_values), normed_sums, grad_residual
    ):
        back, _ = rms_back(token_part, attention_gain, sum_part)
        grad_tokens.append((grad_part + back).astype(BFLOAT))

    down_parts = down_parts_of(hidden, feedfwd_full, gathered_grad)
    down_sums = rows_scatter(down_parts)
    block_out = [(res + part).astype(BFLOAT) for res, part in zip(residuals, down_sums)]

    gain_sums = butterfly_sum(
        jnp.concatenate(
            [row_gain[0] / attention_gain, gain_two_part, *jnp.sum(head_gains, axis=2)]
        )
    )
    grad_attention, grad_feedfwd = grad_attention.astype(SINGLE), grad_feedfwd.astype(SINGLE)
    return (
        jnp.concatenate(block_out, axis=0),
        jnp.concatenate(grad_tokens, axis=0),
        grad_attention[:, :query_cols],
        grad_attention[:, query_cols : query_cols + key_cols],
        grad_attention[:, query_cols + key_cols : qkv_cols],
        grad_attention[:, qkv_cols:].T,
        grad_feedfwd[:, :hidden_cols],
        grad_feedfwd[:, hidden_cols : 2 * hidden_cols],
        grad_feedfwd[:, 2 * hidden_cols :].T,
        gain_sums[:width],
        gain_sums[width : 2 * width],
        gain_sums[2 * width : 2 * width + head_dim],
        gain_sums[2 * width + head_dim :],
    )


def solution(mesh):
    in_specs = (
        P(("dp", "tensor"), None),
        P("dp"),
        P(("dp", "tensor"), None),
        P("dp", "tensor"),
        P("dp", "tensor"),
        P("dp", "tensor"),
        P("tensor", "dp"),
        P("dp", "tensor"),
        P("dp", "tensor"),
        P("tensor", "dp"),
        P(),
        P(),
        P(),
        P(),
    )
    out_specs = (
        P(("dp", "tensor"), None),
        P(("dp", "tensor"), None),
        P("dp", "tensor"),
        P("dp", "tensor"),
        P("dp", "tensor"),
        P("tensor", "dp"),
        P("dp", "tensor"),
        P("dp", "tensor"),
        P("tensor", "dp"),
        P(),
        P(),
        P(),
        P(),
    )
    return jax.shard_map(
        on_device, mesh=mesh, in_specs=in_specs, out_specs=out_specs, check_vma=False
    )
```

```python
from functools import partial
import math

import jax
import jax.numpy as jnp
from jax import lax
from jax.experimental import pallas as pl
from jax.experimental.pallas import tpu as pltpu
from jax.sharding import PartitionSpec as P

LEN = 1024


EPSILON = 1e-05
THETA = 1000000.0
MASKED = -1e30
DOCUMENTS = 3
SHORTEST = 204
TILE = 256
LOG2E = math.log2(math.e)
MIB = 2**20
HEAVY, LIGHT = 16 * 10**9, 10**9
BFLOAT, SINGLE = jnp.bfloat16, jnp.float32


def call_kernel(kernel, name, weight, limit, shapes, scalars, arrays, scratch=(), earlier=()):
    whole = pl.BlockSpec(memory_space=pltpu.VMEM)
    specs = [pl.BlockSpec(memory_space=pltpu.SMEM)] * len(scalars) + [whole] * len(arrays)
    return pl.pallas_call(
        kernel,
        out_shape=[jax.ShapeDtypeStruct(*shape) for shape in shapes],
        in_specs=specs + [pl.BlockSpec(memory_space=pl.ANY)] * len(earlier),
        out_specs=[whole] * len(shapes),
        scratch_shapes=[pltpu.VMEM(*shape) for shape in scratch],
        compiler_params=pltpu.CompilerParams(vmem_limit_bytes=limit * MIB),
        cost_estimate=pl.CostEstimate(flops=weight, bytes_accessed=2**20, transcendentals=0),
        name=name,
    )(*scalars, *arrays, *earlier)


def dot(left, right):
    return jnp.dot(left, right, preferred_element_type=SINGLE)


def dot_last(left, right):
    return lax.dot_general(left, right, (((1,), (1,)), ((), ())), preferred_element_type=SINGLE)


def key_span(start):
    reach = LEN - (DOCUMENTS - 1) * SHORTEST - 1
    return max(0, (start - reach) // 128 * 128), start + TILE


def mask_bias(begin_ref, start, low, high):
    shape = (high - low, TILE)
    key_pos = low + lax.broadcasted_iota(jnp.int32, shape, 0)
    query_pos = start + lax.broadcasted_iota(jnp.int32, shape, 1)
    counts = (key_pos >= begin_ref[:, start : start + TILE]) & (key_pos <= query_pos)
    return jnp.where(counts, 0.0, MASKED)


def head_ratio(values):
    return lax.rsqrt(jnp.mean(values * values, axis=0, keepdims=True) + EPSILON)


def turn(values, cosine, sine):
    half_dim = values.shape[0] // 2
    first, second = values[:half_dim], values[half_dim:]
    return jnp.concatenate([first * cosine - second * sine, second * cosine + first * sine], axis=0)


def gain_columns(gain_ref, head_dim):
    turned = jnp.broadcast_to(gain_ref[...], (8, gain_ref.shape[1])).T
    return turned[:head_dim, :1], turned[head_dim : 2 * head_dim, :1]


def spread(place_ref, natural, out_ref):
    rows = LEN // place_ref.shape[0]
    for block in range(place_ref.shape[0]):
        start = pl.multiple_of(place_ref[block], rows)
        out_ref[pl.ds(start, rows), :] = natural[block * rows : (block + 1) * rows, :]


def collect(place_ref, value_ref, natural):
    rows = LEN // place_ref.shape[0]
    for block in range(place_ref.shape[0]):
        start = pl.multiple_of(place_ref[block], rows)
        natural[block * rows : (block + 1) * rows, :] = value_ref[pl.ds(start, rows), :]


def attend_kernel(
    sizes,
    place_ref,
    rows_a_ref,
    rows_b_ref,
    rows_c_ref,
    rows_d_ref,
    weight_ref,
    gain_ref,
    segment_ref,
    raw_ref,
    query_ref,
    key_ref,
    query_row_ref,
    key_row_ref,
    value_row_ref,
    total_ref,
    attended_ref,
    cosine_ref,
    sine_ref,
    begin_ref,
    context_ref,
    part_a_ref,
    part_b_ref,
    part_c_ref,
    part_d_ref,
    mixed,
    natural,
    extended,
    bias,
    context,
):
    query_heads, key_heads, head_dim = sizes
    group_size = query_heads // key_heads
    heads = query_heads + key_heads
    columns = natural.shape[1]
    quarter = rows_a_ref.shape[0]
    weight = weight_ref[:, :columns]
    for q, rows_ref in enumerate((rows_a_ref, rows_b_ref, rows_c_ref, rows_d_ref)):
        mixed[q * quarter : (q + 1) * quarter, :] = dot(rows_ref[...], weight)
    collect(place_ref, mixed, natural)
    for start in range(0, LEN, 128):
        raw_ref[:, start : start + 128] = natural[start : start + 128, :].T

    segment = segment_ref[...]
    first_count = jnp.sum((segment == 0).astype(SINGLE), axis=1, keepdims=True)
    second_count = jnp.sum((segment == 1).astype(SINGLE), axis=1, keepdims=True)
    begin = jnp.where(
        segment == 0, 0.0, jnp.where(segment == 1, first_count, first_count + second_count)
    )
    begin_ref[...] = begin.astype(jnp.int32)
    half_dim = head_dim // 2
    shape = (half_dim, LEN)
    steps = lax.broadcasted_iota(jnp.int32, shape, 0).astype(SINGLE)
    order = lax.broadcasted_iota(jnp.int32, shape, 1).astype(SINGLE)
    angles = (order - begin) * jnp.exp(steps * (-math.log(THETA) / half_dim))
    cosine, sine = jnp.cos(angles), jnp.sin(angles)
    cosine_ref[...] = cosine
    sine_ref[...] = sine

    gains = gain_columns(gain_ref, head_dim)
    for head in range(heads):
        values = raw_ref[head * head_dim : (head + 1) * head_dim, :]
        gain = gains[0] if head < query_heads else gains[1]
        turned = turn(values * head_ratio(values) * gain, cosine, sine)
        if head < query_heads:
            query_ref[head] = turned.astype(BFLOAT)
            query_row_ref[head] = turned.T.astype(BFLOAT)
        else:
            key_ref[head - query_heads] = turned.astype(BFLOAT)
            key_row_ref[head - query_heads] = turned.T.astype(BFLOAT)
    for head in range(key_heads):
        first = (heads + head) * head_dim
        extended[head, :head_dim, :] = raw_ref[first : first + head_dim, :].astype(BFLOAT)
        extended[head, head_dim:, :] = jnp.ones((extended.shape[1] - head_dim, LEN), BFLOAT)
        value_row_ref[head] = natural[:, first : first + head_dim].astype(BFLOAT)
    factor = LOG2E * head_dim ** (-0.5)
    for start in range(0, LEN, TILE):
        low, high = key_span(start)
        span, tile = slice(low, high), slice(start, start + TILE)
        bias[: high - low, :] = mask_bias(begin_ref, start, low, high)

        def one_head(head, carry):
            key_head = head // group_size
            scores = dot(key_row_ref[key_head, span, :], query_ref[head, :, tile])
            powers = jnp.exp2(scores * factor + bias[: high - low, :])
            summed = dot(extended[key_head, :, span], powers.astype(BFLOAT))
            total = summed[head_dim : head_dim + 1, :]
            total_ref[head, :, tile] = jnp.log2(total)
            attended_ref[head, :, tile] = summed[:head_dim, :] / total
            return carry

        lax.fori_loop(0, query_heads, one_head, 0)
    for head in range(query_heads):
        context[:, head * head_dim : (head + 1) * head_dim] = attended_ref[head].T.astype(BFLOAT)
    spread(place_ref, context, context_ref)
    out_weight = weight_ref[:, columns:]
    for q, part_ref in enumerate((part_a_ref, part_b_ref, part_c_ref, part_d_ref)):
        rows = context_ref[q * quarter : (q + 1) * quarter, :]
        part_ref[...] = dot_last(rows, out_weight).astype(BFLOAT)


def attend(sizes, place, quarters, weight, gains, segments):
    query_heads, key_heads, head_dim = sizes
    columns = (query_heads + 2 * key_heads) * head_dim
    quarter, width = quarters[0].shape
    shapes = [
        ((columns, LEN), SINGLE),
        ((query_heads, head_dim, LEN), BFLOAT),
        ((key_heads, head_dim, LEN), BFLOAT),
        ((query_heads, LEN, head_dim), BFLOAT),
        ((key_heads, LEN, head_dim), BFLOAT),
        ((key_heads, LEN, head_dim), BFLOAT),
        ((query_heads, 1, LEN), SINGLE),
        ((query_heads, head_dim, LEN), SINGLE),
        ((head_dim // 2, LEN), SINGLE),
        ((head_dim // 2, LEN), SINGLE),
        ((1, LEN), jnp.int32),
        ((LEN, query_heads * head_dim), BFLOAT),
    ] + [((quarter, width), BFLOAT)] * 4
    scratch = [
        ((LEN, columns), SINGLE),
        ((LEN, columns), SINGLE),
        ((key_heads, head_dim + 16, LEN), BFLOAT),
        ((LEN, TILE), SINGLE),
        ((LEN, query_heads * head_dim), BFLOAT),
    ]
    arrays = (*quarters, weight, gains, segments)
    outs = call_kernel(
        partial(attend_kernel, sizes), "attend", HEAVY, 56, shapes, (place,), arrays, scratch
    )
    return outs[:11], outs[11], outs[12:]


def attend_back_kernel(
    sizes,
    place_ref,
    grad_a_ref,
    grad_b_ref,
    grad_c_ref,
    grad_d_ref,
    rows_a_ref,
    rows_b_ref,
    rows_c_ref,
    rows_d_ref,
    weight_ref,
    gain_ref,
    raw_ref,
    query_ref,
    key_ref,
    query_row_ref,
    key_row_ref,
    value_row_ref,
    total_ref,
    attended_ref,
    cosine_ref,
    sine_ref,
    begin_ref,
    earlier_ref,
    out_ref,
    head_gain_ref,
    row_gain_ref,
    part_a_ref,
    part_b_ref,
    part_c_ref,
    part_d_ref,
    mixed,
    context,
    grad_row,
    grad_col,
    query_grad,
    key_grad,
    value_grad,
    joined,
    natural,
    bias,
):
    query_heads, key_heads, head_dim = sizes
    group_size = query_heads // key_heads
    heads = query_heads + key_heads
    columns = natural.shape[1]
    quarter = grad_a_ref.shape[0]
    out_weight = weight_ref[:, columns:]
    for q, rows_ref in enumerate((grad_a_ref, grad_b_ref, grad_c_ref, grad_d_ref)):
        mixed[q * quarter : (q + 1) * quarter, :] = dot(rows_ref[...], out_weight).astype(BFLOAT)
    collect(place_ref, mixed, context)
    for head in range(query_heads):
        part = context[:, head * head_dim : (head + 1) * head_dim]
        grad_row[head] = part
        grad_col[head] = part.astype(SINGLE).T
    key_grad[...] = jnp.zeros(key_grad.shape, SINGLE)
    value_grad[...] = jnp.zeros(value_grad.shape, SINGLE)
    scale = head_dim ** (-0.5)
    factor = LOG2E * scale
    for start in range(0, LEN, TILE):
        low, high = key_span(start)
        span, tile = slice(low, high), slice(start, start + TILE)
        bias[: high - low, :] = mask_bias(begin_ref, start, low, high)

        def one_head(head, carry):
            key_head = head // group_size
            scores = dot(key_row_ref[key_head, span, :], query_ref[head, :, tile])
            probs = jnp.exp2(scores * factor + bias[: high - low, :] - total_ref[head, :, tile])
            grads = grad_col[head, :, tile]
            inner = jnp.sum(grads * attended_ref[head, :, tile], axis=0, keepdims=True)
            probs_grad = dot(value_row_ref[key_head, span, :], grads.astype(BFLOAT))
            scores_grad = (probs * (probs_grad - inner)).astype(BFLOAT)
            value_grad[key_head, span, :] += dot(probs.astype(BFLOAT), grad_row[head, tile, :])
            key_grad[key_head, span, :] += dot(scores_grad, query_row_ref[head, tile, :])
            query_grad[head, :, tile] = dot(key_ref[key_head, :, span], scores_grad)
            return carry

        lax.fori_loop(0, query_heads, one_head, 0)
    cosine, sine = cosine_ref[...], sine_ref[...]
    gains = gain_columns(gain_ref, head_dim)
    for kind in range(2):
        head_gain_ref[kind] = jnp.zeros(head_gain_ref.shape[1:], SINGLE)
    for head in range(heads):
        kind = 0 if head < query_heads else 1
        grads = query_grad[head] if kind == 0 else key_grad[head - query_heads].T
        grads = turn(grads * scale, cosine, -sine)
        values = raw_ref[head * head_dim : (head + 1) * head_dim, :]
        ratio = head_ratio(values)
        normed = values * ratio
        weighted = grads * gains[kind]
        inner = jnp.mean(weighted * normed, axis=0, keepdims=True)
        joined[head * head_dim : (head + 1) * head_dim, :] = ratio * (weighted - normed * inner)
        products = grads * normed
        folded = products[:, :128]
        for first in range(128, LEN, 128):
            folded = folded + products[:, first : first + 128]
        head_gain_ref[kind] += folded
    for start in range(0, LEN, 128):
        natural[start : start + 128, : heads * head_dim] = joined[:, start : start + 128].T.astype(
            BFLOAT
        )
    for head in range(key_heads):
        first = (heads + head) * head_dim
        natural[:, first : first + head_dim] = value_grad[head].astype(BFLOAT)
    spread(place_ref, natural, out_ref)
    weight = weight_ref[:, :columns]
    row_gain = jnp.zeros(row_gain_ref.shape, SINGLE)
    rows_refs = (rows_a_ref, rows_b_ref, rows_c_ref, rows_d_ref)
    for q, part_ref in enumerate((part_a_ref, part_b_ref, part_c_ref, part_d_ref)):
        part = dot_last(out_ref[q * quarter : (q + 1) * quarter, :], weight)
        part_ref[...] = part.astype(BFLOAT)
        row_gain += jnp.sum(part * rows_refs[q][...].astype(SINGLE), axis=0, keepdims=True)
    row_gain_ref[...] = row_gain


def attend_back(sizes, place, grads, quarters, weight, gains, saved, earlier):
    query_heads, key_heads, head_dim = sizes
    heads = query_heads + key_heads
    columns = (heads + key_heads) * head_dim
    quarter, width = quarters[0].shape
    shapes = [
        ((LEN, columns), BFLOAT),
        ((2, head_dim, 128), SINGLE),
        ((1, width), SINGLE),
    ] + [((quarter, width), BFLOAT)] * 4
    scratch = [
        ((LEN, query_heads * head_dim), BFLOAT),
        ((LEN, query_heads * head_dim), BFLOAT),
        ((query_heads, LEN, head_dim), BFLOAT),
        ((query_heads, head_dim, LEN), SINGLE),
        ((query_heads, head_dim, LEN), SINGLE),
        ((key_heads, LEN, head_dim), SINGLE),
        ((key_heads, LEN, head_dim), SINGLE),
        ((heads * head_dim, LEN), SINGLE),
        ((LEN, columns), BFLOAT),
        ((LEN, TILE), SINGLE),
    ]
    arrays = (*grads, *quarters, weight, gains, *saved)
    kernel = partial(attend_back_kernel, sizes)
    outs = call_kernel(
        kernel, "attend_back", HEAVY, 56, shapes, (place,), arrays, scratch, (earlier,)
    )
    return outs[0], outs[1], outs[2], outs[3:]


def feedfwd_kernel(
    rows_a_ref,
    rows_b_ref,
    rows_c_ref,
    rows_d_ref,
    cot_a_ref,
    cot_b_ref,
    cot_c_ref,
    cot_d_ref,
    weight_ref,
    hidden_ref,
    out_ref,
    part_a_ref,
    part_b_ref,
    part_c_ref,
    part_d_ref,
    rows_turned,
    cot_turned,
    gate_up_grad,
    total,
):
    step = pl.program_id(0)
    quarter = rows_a_ref.shape[0]
    cols = hidden_ref.shape[1]
    rows_refs = (rows_a_ref, rows_b_ref, rows_c_ref, rows_d_ref)
    cot_refs = (cot_a_ref, cot_b_ref, cot_c_ref, cot_d_ref)
    part_refs = (part_a_ref, part_b_ref, part_c_ref, part_d_ref)

    @pl.when(step == 0)
    def _():
        for q in range(4):
            rows_turned[:, q * quarter : (q + 1) * quarter] = rows_refs[q][...].T
            cot_turned[:, q * quarter : (q + 1) * quarter] = cot_refs[q][...].T
        total[...] = jnp.zeros(total.shape, SINGLE)

    for q in range(4):
        tile = slice(q * quarter, (q + 1) * quarter)
        gate_up = dot(rows_refs[q][...], weight_ref[:, : 2 * cols])
        gate_proj, upward = gate_up[:, :cols], gate_up[:, cols:]
        grad_hidden = dot(cot_refs[q][...], weight_ref[:, 2 * cols :])
        sigmoid = 0.5 * jnp.tanh(0.5 * gate_proj) + 0.5
        active = gate_proj * sigmoid
        hidden_ref[tile, :] = (active * upward).astype(BFLOAT)
        slope = sigmoid + active * (1.0 - sigmoid)
        gate_up_grad[tile, :cols] = (grad_hidden * upward * slope).astype(BFLOAT)
        gate_up_grad[tile, cols:] = (grad_hidden * active).astype(BFLOAT)
        total[tile, :] += dot_last(gate_up_grad[tile, :], weight_ref[:, : 2 * cols])
    out_ref[:, : 2 * cols] = dot(rows_turned[...], gate_up_grad[...]).astype(BFLOAT)
    out_ref[:, 2 * cols :] = dot(cot_turned[...], hidden_ref[...]).astype(BFLOAT)

    @pl.when(step == pl.num_programs(0) - 1)
    def _():
        for q in range(4):
            part_refs[q][...] = total[q * quarter : (q + 1) * quarter, :].astype(BFLOAT)


def tile_of(hidden_cols):
    return 384 if hidden_cols % 384 == 0 else hidden_cols


def interleave(gate, up, down):
    tile = tile_of(gate.shape[1])
    pieces = []
    for first in range(0, gate.shape[1], tile):
        pieces += [value[:, first : first + tile] for value in (gate, up, down)]
    return jnp.concatenate(pieces, axis=1)


def part_of(value, kind):
    tile = tile_of(value.shape[1] // 3)
    starts = range(kind * tile, value.shape[1], 3 * tile)
    return jnp.concatenate([value[:, first : first + tile] for first in starts], axis=1)


def feedfwd(quarters, cots, weight):
    quarter, width = quarters[0].shape
    hidden_cols = weight.shape[1] // 3
    cols = tile_of(hidden_cols)
    whole = pl.BlockSpec((quarter, width), lambda j: (0, 0))
    block = pl.BlockSpec((width, 3 * cols), lambda j: (0, j))
    outs = pl.pallas_call(
        feedfwd_kernel,
        grid=(hidden_cols // cols,),
        out_shape=[
            jax.ShapeDtypeStruct((LEN, hidden_cols), BFLOAT),
            jax.ShapeDtypeStruct((width, 3 * hidden_cols), BFLOAT),
        ]
        + [jax.ShapeDtypeStruct((quarter, width), BFLOAT)] * 4,
        in_specs=[whole] * 8 + [block],
        out_specs=[pl.BlockSpec((LEN, cols), lambda j: (0, j)), block] + [whole] * 4,
        scratch_shapes=[
            pltpu.VMEM((width, LEN), BFLOAT),
            pltpu.VMEM((width, LEN), BFLOAT),
            pltpu.VMEM((LEN, 2 * cols), BFLOAT),
            pltpu.VMEM((LEN, width), SINGLE),
        ],
        compiler_params=pltpu.CompilerParams(vmem_limit_bytes=56 * MIB),
        cost_estimate=pl.CostEstimate(flops=HEAVY, bytes_accessed=2**20, transcendentals=0),
        name="feedfwd",
    )(*quarters, *cots, weight)
    return outs[0], outs[1], outs[2:]


def weights_kernel(
    first_tiles,
    first_a_ref,
    first_b_ref,
    first_c_ref,
    first_d_ref,
    second_a_ref,
    second_b_ref,
    second_c_ref,
    second_d_ref,
    first_grad_ref,
    second_grad_ref,
    earlier_ref,
    out_ref,
    turned_ref,
):
    step = pl.program_id(0)
    quarter = first_a_ref.shape[0]

    def turn_over(*refs):
        for q, ref in enumerate(refs):
            turned_ref[:, q * quarter : (q + 1) * quarter] = ref[...].T

    @pl.when(step == 0)
    def _():
        turn_over(first_a_ref, first_b_ref, first_c_ref, first_d_ref)

    @pl.when(step < first_tiles)
    def _():
        out_ref[...] = dot(turned_ref[...], first_grad_ref[...]).astype(BFLOAT)

    @pl.when(step == first_tiles)
    def _():
        turn_over(second_a_ref, second_b_ref, second_c_ref, second_d_ref)

    @pl.when(step >= first_tiles)
    def _():
        out_ref[...] = dot(turned_ref[...], second_grad_ref[...]).astype(BFLOAT)


def weight_parts(firsts, first_grad, seconds, second_grad, earlier):
    first_cols, second_cols = first_grad.shape[1], second_grad.shape[1]
    quarter, width = firsts[0].shape
    tiles = [t for t in (256, 128) if first_cols % t == 0 and second_cols % t == 0]
    if not tiles:
        sums = []
        for lefts, right in ((firsts, first_grad), (seconds, second_grad)):
            left = jnp.concatenate(lefts, axis=0)
            total = jnp.einsum("nd,ne->de", left, right, preferred_element_type=SINGLE)
            sums.append(total.astype(BFLOAT))
        return jnp.concatenate(sums, axis=1)
    tile = tiles[0]
    first_tiles = first_cols // tile
    whole = pl.BlockSpec((quarter, width), lambda j: (0, 0))
    first_spec = pl.BlockSpec((LEN, tile), lambda j: (0, jnp.minimum(j, first_tiles - 1)))
    second_spec = pl.BlockSpec((LEN, tile), lambda j: (0, jnp.maximum(j - first_tiles, 0)))
    columns = first_cols + second_cols
    return pl.pallas_call(
        partial(weights_kernel, first_tiles),
        grid=(columns // tile,),
        out_shape=jax.ShapeDtypeStruct((width, columns), BFLOAT),
        in_specs=[whole] * 8 + [first_spec, second_spec, pl.BlockSpec(memory_space=pl.ANY)],
        out_specs=pl.BlockSpec((width, tile), lambda j: (0, j)),
        scratch_shapes=[pltpu.VMEM((width, LEN), BFLOAT)],
        compiler_params=pltpu.CompilerParams(vmem_limit_bytes=56 * MIB),
        cost_estimate=pl.CostEstimate(flops=LIGHT, bytes_accessed=2**20, transcendentals=0),
        name="weight_parts",
    )(*firsts, *seconds, first_grad, second_grad, earlier)


def pair_sum_kernel(stay_a_ref, got_a_ref, stay_b_ref, got_b_ref, *refs):
    outs = refs[-4:]
    rows = stay_a_ref.shape[0] // 2
    pairs = ((stay_a_ref, got_a_ref), (stay_b_ref, got_b_ref))
    for half, (stay_ref, got_ref) in enumerate(pairs):
        total = stay_ref[...].astype(SINGLE) + got_ref[...].astype(SINGLE)
        outs[2 * half][...] = total[:rows].astype(outs[2 * half].dtype)
        outs[2 * half + 1][...] = total[rows:].astype(BFLOAT)


def pair_sum(stays, gots, last, earlier):
    rows, width = stays[0].shape
    shapes = [((rows // 2, width), SINGLE if last else BFLOAT), ((rows // 2, width), BFLOAT)] * 2
    arrays = (stays[0], gots[0], stays[1], gots[1])
    outs = call_kernel(pair_sum_kernel, "pair_sum", LIGHT, 8, shapes, (), arrays, earlier=earlier)
    return outs[0::2], outs[1::2]


def down_kernel(hidden_ref, weight_ref, *refs):
    outs, total = refs[-5:-1], refs[-1]
    step = pl.program_id(0)
    product = dot_last(hidden_ref[...], weight_ref[...])

    @pl.when(step == 0)
    def _():
        total[...] = product

    @pl.when(step > 0)
    def _():
        total[...] += product

    @pl.when(step == pl.num_programs(0) - 1)
    def _():
        quarter = total.shape[0] // 4
        for q, part_ref in enumerate(outs):
            part_ref[...] = total[q * quarter : (q + 1) * quarter, :].astype(BFLOAT)


def down_parts_of(hidden, weight, earlier):
    hidden_cols = hidden.shape[1]
    quarter, width = LEN // 4, weight.shape[0]
    cols = tile_of(hidden_cols)
    if cols % 128:
        down = part_of(weight, 2)
        return [
            dot_last(hidden[q * quarter : (q + 1) * quarter], down).astype(BFLOAT) for q in range(4)
        ]
    part = pl.BlockSpec((quarter, width), lambda i: (0, 0))
    return pl.pallas_call(
        down_kernel,
        grid=(hidden_cols // cols,),
        out_shape=[jax.ShapeDtypeStruct((quarter, width), BFLOAT)] * 4,
        in_specs=[
            pl.BlockSpec((LEN, cols), lambda i: (0, i)),
            pl.BlockSpec((width, cols), lambda i: (0, 3 * i + 2)),
        ]
        + [pl.BlockSpec(memory_space=pl.ANY)] * len(earlier),
        out_specs=[part] * 4,
        scratch_shapes=[pltpu.VMEM((LEN, width), SINGLE)],
        compiler_params=pltpu.CompilerParams(vmem_limit_bytes=56 * MIB),
        cost_estimate=pl.CostEstimate(flops=LIGHT, bytes_accessed=2**20, transcendentals=0),
        name="down_parts",
    )(hidden, weight, *earlier)


def split_kernel(value_ref, query_ref, key_ref, value_out_ref, out_ref):
    first = 0
    for ref in (query_ref, key_ref, value_out_ref):
        ref[...] = value_ref[:, first : first + ref.shape[1]].astype(SINGLE)
        first += ref.shape[1]
    out_ref[...] = value_ref[:, first:].astype(SINGLE).T


def split_weights(value, shapes):
    kinds = [(shape, SINGLE) for shape in shapes]
    return call_kernel(split_kernel, "split_weights", LIGHT, 56, kinds, (), (value,))


def pack_kernel(query_ref, key_ref, value_ref, out_ref, packed_ref):
    first = 0
    for ref in (query_ref, key_ref, value_ref):
        packed_ref[:, first : first + ref.shape[1]] = ref[...]
        first += ref.shape[1]
    packed_ref[:, first:] = out_ref[...].astype(SINGLE).T.astype(BFLOAT)


def pack_weights(*values):
    columns = sum(value.shape[1] for value in values[:3]) + values[3].shape[0]
    kinds = [((values[0].shape[0], columns), BFLOAT)]
    return call_kernel(pack_kernel, "pack_weights", LIGHT, 56, kinds, (), values)[0]


def later(value, *earlier):
    anywhere = pl.BlockSpec(memory_space=pl.ANY)
    return pl.pallas_call(
        lambda *refs: None,
        out_shape=jax.ShapeDtypeStruct(value.shape, value.dtype),
        in_specs=[anywhere] * (1 + len(earlier)),
        out_specs=anywhere,
        input_output_aliases={0: 0},
        name="later",
    )(value, *earlier)


def wait_aways(parts, *earlier):
    return [later(part, *earlier) if q % 2 else part for q, part in enumerate(parts)]


def rms_scale(values, gain):
    return values * lax.rsqrt(jnp.mean(values * values, axis=-1, keepdims=True) + EPSILON) * gain


def swap(value, axis, bit):
    size = lax.axis_size(axis)
    return lax.ppermute(value, axis, [(i, i ^ bit) for i in range(size)])


def axis_bits(axis):
    return [1 << k for k in range(lax.axis_size(axis).bit_length() - 1)]


def block_order(bits):
    order = [0]
    for bit in bits:
        order = order + [r ^ bit for r in order]
    return order


def butterfly_sum(value):
    for axis in ("dp", "tensor"):
        for bit in axis_bits(axis):
            value = value + swap(value, axis, bit)
    return value


def rms_back(values, gain, grad):
    ratio = lax.rsqrt(jnp.mean(values * values, axis=-1, keepdims=True) + EPSILON)
    scaled = grad * gain
    inner = jnp.mean(scaled * values, axis=-1, keepdims=True)
    return ratio * scaled - values * (ratio * ratio * ratio * inner), grad * values * ratio


def on_device(
    tokens,
    segments,
    cotangent,
    query_weight,
    key_weight,
    value_weight,
    out_weight,
    gate_weight,
    up_weight,
    down_weight,
    attention_gain,
    feedfwd_gain,
    query_gain,
    key_gain,
):
    head_dim = query_gain.shape[0]
    local_rows, width = tokens.shape
    half_rows = local_rows // 2
    tensor_size, here = lax.axis_size("tensor"), lax.axis_index("tensor")
    tensor_bits = axis_bits("tensor")
    half_bits = (tensor_bits, tensor_bits[::-1])
    half_order = [block_order(bits) for bits in half_bits]
    place = jnp.stack(
        [
            jnp.array([order.index(r) for r in range(tensor_size)], jnp.int32)[here ^ j] * half_rows
            + c * (LEN // 2)
            for j in range(tensor_size)
            for c, order in enumerate(half_order)
        ]
    )

    def rows_gather(halves):
        for bits in zip(*half_bits):
            pairs = [(part, swap(part, "tensor", bit)) for part, bit in zip(halves, bits)]
            halves = [jnp.concatenate(pair, axis=0) for pair in pairs]
        return [*pairs[0], *pairs[1]]

    def rows_scatter(parts, earlier=()):
        stays, aways = parts[0::2], parts[1::2]
        for step, bits in enumerate(zip(*(bits[::-1] for bits in half_bits))):
            gots = [swap(part, "tensor", bit) for part, bit in zip(aways, bits)]
            if step < len(tensor_bits) - 1:
                last = step == len(tensor_bits) - 2
                stays, aways = pair_sum(stays, gots, last, earlier)
                earlier = ()
        return [stay.astype(SINGLE) + got.astype(SINGLE) for stay, got in zip(stays, gots)], stays

    def halves_of(value):
        return [value[:half_rows], value[half_rows:]]

    token_values = tokens.astype(SINGLE)
    normed = rms_scale(token_values, attention_gain).astype(BFLOAT)
    gathered = rows_gather(halves_of(normed))
    attention_full = lax.all_gather(
        pack_weights(query_weight, key_weight, value_weight, out_weight),
        "dp",
        axis=0,
        tiled=True,
    )
    feedfwd_full = lax.all_gather(
        interleave(gate_weight, up_weight, down_weight.T), "dp", axis=0, tiled=True
    )
    cots = rows_gather(halves_of(cotangent))

    query_cols, key_cols = query_weight.shape[1], key_weight.shape[1]
    sizes = (query_cols // head_dim, key_cols // head_dim, head_dim)
    gains = jnp.concatenate([query_gain, key_gain])[None, :]
    saved, context, attended_parts = attend(
        sizes, place, gathered, attention_full, gains, segments[None, :]
    )
    attended_parts = wait_aways(attended_parts, cots[1], cots[3])
    residuals, normed_two = [], []
    for token_part, sum_part in zip(halves_of(token_values), rows_scatter(attended_parts)[0]):
        residuals.append(token_part + sum_part)
        normed_two.append(rms_scale(residuals[-1], feedfwd_gain).astype(BFLOAT))
    gathered_two = rows_gather(normed_two)

    hidden, feedfwd_part, two_parts = feedfwd(gathered_two, cots, feedfwd_full)
    grad_feedfwd = lax.psum_scatter(feedfwd_part, "dp", scatter_dimension=0, tiled=True)
    two_sums, _ = rows_scatter(two_parts)
    grad_residual, gain_two_part = [], 0.0
    for residual_part, sum_part, cot_part in zip(residuals, two_sums, halves_of(cotangent)):
        back, gain_part = rms_back(residual_part, feedfwd_gain, sum_part)
        grad_residual.append(cot_part.astype(SINGLE) + back)
        gain_two_part = gain_two_part + jnp.sum(gain_part, axis=0)
    grad_low = [part.astype(BFLOAT) for part in grad_residual]
    down_parts = down_parts_of(hidden, feedfwd_full, grad_low)
    gathered_grad = rows_gather(grad_low)

    qkv_grad, head_gains, row_gain, normed_parts = attend_back(
        sizes, place, gathered_grad, gathered, attention_full, gains, saved, down_parts[0]
    )
    down_sums, down_stays = rows_scatter(
        wait_aways(down_parts, gathered_grad[1], gathered_grad[3])
    )
    attention_part = weight_parts(gathered, qkv_grad, gathered_grad, context, down_stays[0])
    attention_part = later(attention_part, grad_feedfwd)
    grad_attention = lax.psum_scatter(attention_part, "dp", scatter_dimension=0, tiled=True)
    normed_sums, normed_stays = rows_scatter(normed_parts, (attention_part,))
    grad_tokens = []
    for token_part, sum_part, grad_part in zip(
        halves_of(token_values), normed_sums, grad_residual
    ):
        back, _ = rms_back(token_part, attention_gain, sum_part)
        grad_tokens.append((grad_part + back).astype(BFLOAT))

    block_out = [(res + part).astype(BFLOAT) for res, part in zip(residuals, down_sums)]

    gain_parts = jnp.concatenate(
        [row_gain[0] / attention_gain, gain_two_part, *jnp.sum(head_gains, axis=2)]
    )
    gain_sums = butterfly_sum(gain_parts + 0.0 * normed_stays[0][0, 0].astype(SINGLE))
    grad_feedfwd = grad_feedfwd.astype(SINGLE)
    shapes = [value.shape for value in (query_weight, key_weight, value_weight, out_weight)]
    return (
        jnp.concatenate(block_out, axis=0),
        jnp.concatenate(grad_tokens, axis=0),
        *split_weights(grad_attention, shapes),
        part_of(grad_feedfwd, 0),
        part_of(grad_feedfwd, 1),
        part_of(grad_feedfwd, 2).T,
        gain_sums[:width],
        gain_sums[width : 2 * width],
        gain_sums[2 * width : 2 * width + head_dim],
        gain_sums[2 * width + head_dim :],
    )


def solution(mesh):
    in_specs = (
        P(("dp", "tensor"), None),
        P("dp"),
        P(("dp", "tensor"), None),
        P("dp", "tensor"),
        P("dp", "tensor"),
        P("dp", "tensor"),
        P("tensor", "dp"),
        P("dp", "tensor"),
        P("dp", "tensor"),
        P("tensor", "dp"),
        P(),
        P(),
        P(),
        P(),
    )
    out_specs = (
        P(("dp", "tensor"), None),
        P(("dp", "tensor"), None),
        P("dp", "tensor"),
        P("dp", "tensor"),
        P("dp", "tensor"),
        P("tensor", "dp"),
        P("dp", "tensor"),
        P("dp", "tensor"),
        P("tensor", "dp"),
        P(),
        P(),
        P(),
        P(),
    )
    return jax.shard_map(
        on_device, mesh=mesh, in_specs=in_specs, out_specs=out_specs, check_vma=False
    )
```

```python
from functools import partial
import math

import jax
import jax.numpy as jnp
from jax import lax
from jax.experimental import pallas as pl
from jax.experimental.pallas import tpu as pltpu
from jax.sharding import PartitionSpec as P

LEN = 1024


EPSILON = 1e-05
THETA = 1000000.0
MASKED = -1e30
DOCUMENTS = 3
SHORTEST = 204
TILE = 256
LOG2E = math.log2(math.e)
MIB = 2**20
HEAVY, LIGHT = 16 * 10**9, 10**9
BFLOAT, SINGLE = jnp.bfloat16, jnp.float32


def call_kernel(kernel, name, weight, limit, shapes, scalars, arrays, scratch=(), earlier=()):
    whole = pl.BlockSpec(memory_space=pltpu.VMEM)
    specs = [pl.BlockSpec(memory_space=pltpu.SMEM)] * len(scalars) + [whole] * len(arrays)
    return pl.pallas_call(
        kernel,
        out_shape=[jax.ShapeDtypeStruct(*shape) for shape in shapes],
        in_specs=specs + [pl.BlockSpec(memory_space=pl.ANY)] * len(earlier),
        out_specs=[whole] * len(shapes),
        scratch_shapes=[pltpu.VMEM(*shape) for shape in scratch],
        compiler_params=pltpu.CompilerParams(vmem_limit_bytes=limit * MIB),
        cost_estimate=pl.CostEstimate(flops=weight, bytes_accessed=2**20, transcendentals=0),
        name=name,
    )(*scalars, *arrays, *earlier)


def dot(left, right):
    return jnp.dot(left, right, preferred_element_type=SINGLE)


def dot_last(left, right):
    return lax.dot_general(left, right, (((1,), (1,)), ((), ())), preferred_element_type=SINGLE)


def key_span(start):
    reach = LEN - (DOCUMENTS - 1) * SHORTEST - 1
    return max(0, (start - reach) // 128 * 128), start + TILE


def mask_bias(begin_ref, start, low, high):
    shape = (high - low, TILE)
    key_pos = low + lax.broadcasted_iota(jnp.int32, shape, 0)
    query_pos = start + lax.broadcasted_iota(jnp.int32, shape, 1)
    counts = (key_pos >= begin_ref[:, start : start + TILE]) & (key_pos <= query_pos)
    return jnp.where(counts, 0.0, MASKED)


def head_ratio(values):
    return lax.rsqrt(jnp.mean(values * values, axis=0, keepdims=True) + EPSILON)


def turn(values, cosine, sine):
    half_dim = values.shape[0] // 2
    first, second = values[:half_dim], values[half_dim:]
    return jnp.concatenate([first * cosine - second * sine, second * cosine + first * sine], axis=0)


def gain_columns(gain_ref, head_dim):
    turned = jnp.broadcast_to(gain_ref[...], (8, gain_ref.shape[1])).T
    return turned[:head_dim, :1], turned[head_dim : 2 * head_dim, :1]


def spread(place_ref, natural, out_ref):
    rows = LEN // place_ref.shape[0]
    for block in range(place_ref.shape[0]):
        start = pl.multiple_of(place_ref[block], rows)
        out_ref[pl.ds(start, rows), :] = natural[block * rows : (block + 1) * rows, :]


def collect(place_ref, value_ref, natural):
    rows = LEN // place_ref.shape[0]
    for block in range(place_ref.shape[0]):
        start = pl.multiple_of(place_ref[block], rows)
        natural[block * rows : (block + 1) * rows, :] = value_ref[pl.ds(start, rows), :]


def attend_kernel(
    sizes,
    place_ref,
    rows_a_ref,
    rows_b_ref,
    rows_c_ref,
    rows_d_ref,
    weight_ref,
    gain_ref,
    segment_ref,
    raw_ref,
    query_ref,
    key_ref,
    query_row_ref,
    key_row_ref,
    value_row_ref,
    total_ref,
    attended_ref,
    cosine_ref,
    sine_ref,
    begin_ref,
    context_ref,
    part_a_ref,
    part_b_ref,
    part_c_ref,
    part_d_ref,
    mixed,
    natural,
    extended,
    bias,
    context,
):
    query_heads, key_heads, head_dim = sizes
    group_size = query_heads // key_heads
    heads = query_heads + key_heads
    columns = natural.shape[1]
    quarter = rows_a_ref.shape[0]
    weight = weight_ref[:, :columns]
    for q, rows_ref in enumerate((rows_a_ref, rows_b_ref, rows_c_ref, rows_d_ref)):
        mixed[q * quarter : (q + 1) * quarter, :] = dot(rows_ref[...], weight)
    collect(place_ref, mixed, natural)
    for start in range(0, LEN, 128):
        raw_ref[:, start : start + 128] = natural[start : start + 128, :].T

    segment = segment_ref[...]
    first_count = jnp.sum((segment == 0).astype(SINGLE), axis=1, keepdims=True)
    second_count = jnp.sum((segment == 1).astype(SINGLE), axis=1, keepdims=True)
    begin = jnp.where(
        segment == 0, 0.0, jnp.where(segment == 1, first_count, first_count + second_count)
    )
    begin_ref[...] = begin.astype(jnp.int32)
    half_dim = head_dim // 2
    shape = (half_dim, LEN)
    steps = lax.broadcasted_iota(jnp.int32, shape, 0).astype(SINGLE)
    order = lax.broadcasted_iota(jnp.int32, shape, 1).astype(SINGLE)
    angles = (order - begin) * jnp.exp(steps * (-math.log(THETA) / half_dim))
    cosine, sine = jnp.cos(angles), jnp.sin(angles)
    cosine_ref[...] = cosine
    sine_ref[...] = sine

    gains = gain_columns(gain_ref, head_dim)
    for head in range(heads):
        values = raw_ref[head * head_dim : (head + 1) * head_dim, :]
        gain = gains[0] if head < query_heads else gains[1]
        turned = turn(values * head_ratio(values) * gain, cosine, sine)
        if head < query_heads:
            query_ref[head] = turned.astype(BFLOAT)
            query_row_ref[head] = turned.T.astype(BFLOAT)
        else:
            key_ref[head - query_heads] = turned.astype(BFLOAT)
            key_row_ref[head - query_heads] = turned.T.astype(BFLOAT)
    for head in range(key_heads):
        first = (heads + head) * head_dim
        extended[head, :head_dim, :] = raw_ref[first : first + head_dim, :].astype(BFLOAT)
        extended[head, head_dim:, :] = jnp.ones((extended.shape[1] - head_dim, LEN), BFLOAT)
        value_row_ref[head] = natural[:, first : first + head_dim].astype(BFLOAT)
    factor = LOG2E * head_dim ** (-0.5)
    for start in range(0, LEN, TILE):
        low, high = key_span(start)
        span, tile = slice(low, high), slice(start, start + TILE)
        bias[: high - low, :] = mask_bias(begin_ref, start, low, high)

        def one_head(head, carry):
            key_head = head // group_size
            scores = dot(key_row_ref[key_head, span, :], query_ref[head, :, tile])
            powers = jnp.exp2(scores * factor + bias[: high - low, :])
            summed = dot(extended[key_head, :, span], powers.astype(BFLOAT))
            total = summed[head_dim : head_dim + 1, :]
            total_ref[head, :, tile] = jnp.log2(total)
            attended_ref[head, :, tile] = summed[:head_dim, :] / total
            return carry

        lax.fori_loop(0, query_heads, one_head, 0)
    for head in range(query_heads):
        context[:, head * head_dim : (head + 1) * head_dim] = attended_ref[head].T.astype(BFLOAT)
    spread(place_ref, context, context_ref)
    out_weight = weight_ref[:, columns:]
    for q, part_ref in enumerate((part_a_ref, part_b_ref, part_c_ref, part_d_ref)):
        rows = context_ref[q * quarter : (q + 1) * quarter, :]
        part_ref[...] = dot_last(rows, out_weight).astype(BFLOAT)


def attend(sizes, place, quarters, weight, gains, segments):
    query_heads, key_heads, head_dim = sizes
    columns = (query_heads + 2 * key_heads) * head_dim
    quarter, width = quarters[0].shape
    shapes = [
        ((columns, LEN), SINGLE),
        ((query_heads, head_dim, LEN), BFLOAT),
        ((key_heads, head_dim, LEN), BFLOAT),
        ((query_heads, LEN, head_dim), BFLOAT),
        ((key_heads, LEN, head_dim), BFLOAT),
        ((key_heads, LEN, head_dim), BFLOAT),
        ((query_heads, 1, LEN), SINGLE),
        ((query_heads, head_dim, LEN), SINGLE),
        ((head_dim // 2, LEN), SINGLE),
        ((head_dim // 2, LEN), SINGLE),
        ((1, LEN), jnp.int32),
        ((LEN, query_heads * head_dim), BFLOAT),
    ] + [((quarter, width), BFLOAT)] * 4
    scratch = [
        ((LEN, columns), SINGLE),
        ((LEN, columns), SINGLE),
        ((key_heads, head_dim + 16, LEN), BFLOAT),
        ((LEN, TILE), SINGLE),
        ((LEN, query_heads * head_dim), BFLOAT),
    ]
    arrays = (*quarters, weight, gains, segments)
    outs = call_kernel(
        partial(attend_kernel, sizes), "attend", HEAVY, 56, shapes, (place,), arrays, scratch
    )
    return outs[:11], outs[11], outs[12:]


def attend_back_kernel(
    sizes,
    place_ref,
    grad_a_ref,
    grad_b_ref,
    grad_c_ref,
    grad_d_ref,
    rows_a_ref,
    rows_b_ref,
    rows_c_ref,
    rows_d_ref,
    weight_ref,
    gain_ref,
    raw_ref,
    query_ref,
    key_ref,
    query_row_ref,
    key_row_ref,
    value_row_ref,
    total_ref,
    attended_ref,
    cosine_ref,
    sine_ref,
    begin_ref,
    context_ref,
    earlier_ref,
    weight_grad_ref,
    head_gain_ref,
    row_gain_ref,
    part_a_ref,
    part_b_ref,
    part_c_ref,
    part_d_ref,
    mixed,
    context,
    grad_row,
    grad_col,
    query_grad,
    key_grad,
    value_grad,
    joined,
    natural,
    out_ref,
    turned,
    bias,
):
    query_heads, key_heads, head_dim = sizes
    group_size = query_heads // key_heads
    heads = query_heads + key_heads
    columns = natural.shape[1]
    quarter = grad_a_ref.shape[0]
    out_weight = weight_ref[:, columns:]
    for q, rows_ref in enumerate((grad_a_ref, grad_b_ref, grad_c_ref, grad_d_ref)):
        mixed[q * quarter : (q + 1) * quarter, :] = dot(rows_ref[...], out_weight).astype(BFLOAT)
        turned[:, q * quarter : (q + 1) * quarter] = rows_ref[...].T
    weight_grad_ref[:, columns:] = dot(turned[...], context_ref[...]).astype(BFLOAT)
    collect(place_ref, mixed, context)
    for head in range(query_heads):
        part = context[:, head * head_dim : (head + 1) * head_dim]
        grad_row[head] = part
        grad_col[head] = part.astype(SINGLE).T
    key_grad[...] = jnp.zeros(key_grad.shape, SINGLE)
    value_grad[...] = jnp.zeros(value_grad.shape, SINGLE)
    scale = head_dim ** (-0.5)
    factor = LOG2E * scale
    for start in range(0, LEN, TILE):
        low, high = key_span(start)
        span, tile = slice(low, high), slice(start, start + TILE)
        bias[: high - low, :] = mask_bias(begin_ref, start, low, high)

        def one_head(head, carry):
            key_head = head // group_size
            scores = dot(key_row_ref[key_head, span, :], query_ref[head, :, tile])
            probs = jnp.exp2(scores * factor + bias[: high - low, :] - total_ref[head, :, tile])
            grads = grad_col[head, :, tile]
            inner = jnp.sum(grads * attended_ref[head, :, tile], axis=0, keepdims=True)
            probs_grad = dot(value_row_ref[key_head, span, :], grads.astype(BFLOAT))
            scores_grad = (probs * (probs_grad - inner)).astype(BFLOAT)
            value_grad[key_head, span, :] += dot(probs.astype(BFLOAT), grad_row[head, tile, :])
            key_grad[key_head, span, :] += dot(scores_grad, query_row_ref[head, tile, :])
            query_grad[head, :, tile] = dot(key_ref[key_head, :, span], scores_grad)
            return carry

        lax.fori_loop(0, query_heads, one_head, 0)
    cosine, sine = cosine_ref[...], sine_ref[...]
    gains = gain_columns(gain_ref, head_dim)
    for kind in range(2):
        head_gain_ref[kind] = jnp.zeros(head_gain_ref.shape[1:], SINGLE)
    for head in range(heads):
        kind = 0 if head < query_heads else 1
        grads = query_grad[head] if kind == 0 else key_grad[head - query_heads].T
        grads = turn(grads * scale, cosine, -sine)
        values = raw_ref[head * head_dim : (head + 1) * head_dim, :]
        ratio = head_ratio(values)
        normed = values * ratio
        weighted = grads * gains[kind]
        inner = jnp.mean(weighted * normed, axis=0, keepdims=True)
        joined[head * head_dim : (head + 1) * head_dim, :] = ratio * (weighted - normed * inner)
        products = grads * normed
        folded = products[:, :128]
        for first in range(128, LEN, 128):
            folded = folded + products[:, first : first + 128]
        head_gain_ref[kind] += folded
    for start in range(0, LEN, 128):
        natural[start : start + 128, : heads * head_dim] = joined[:, start : start + 128].T.astype(
            BFLOAT
        )
    for head in range(key_heads):
        first = (heads + head) * head_dim
        natural[:, first : first + head_dim] = value_grad[head].astype(BFLOAT)
    spread(place_ref, natural, out_ref)
    weight = weight_ref[:, :columns]
    row_gain = jnp.zeros(row_gain_ref.shape, SINGLE)
    rows_refs = (rows_a_ref, rows_b_ref, rows_c_ref, rows_d_ref)
    for q, part_ref in enumerate((part_a_ref, part_b_ref, part_c_ref, part_d_ref)):
        part = dot_last(out_ref[q * quarter : (q + 1) * quarter, :], weight)
        part_ref[...] = part.astype(BFLOAT)
        row_gain += jnp.sum(part * rows_refs[q][...].astype(SINGLE), axis=0, keepdims=True)
    row_gain_ref[...] = row_gain
    for q, rows_ref in enumerate(rows_refs):
        turned[:, q * quarter : (q + 1) * quarter] = rows_ref[...].T
    weight_grad_ref[:, :columns] = dot(turned[...], out_ref[...]).astype(BFLOAT)


def attend_back(sizes, place, grads, quarters, weight, gains, saved, context, earlier):
    query_heads, key_heads, head_dim = sizes
    heads = query_heads + key_heads
    columns = (heads + key_heads) * head_dim
    quarter, width = quarters[0].shape
    shapes = [
        (weight.shape, BFLOAT),
        ((2, head_dim, 128), SINGLE),
        ((1, width), SINGLE),
    ] + [((quarter, width), BFLOAT)] * 4
    scratch = [
        ((LEN, query_heads * head_dim), BFLOAT),
        ((LEN, query_heads * head_dim), BFLOAT),
        ((query_heads, LEN, head_dim), BFLOAT),
        ((query_heads, head_dim, LEN), SINGLE),
        ((query_heads, head_dim, LEN), SINGLE),
        ((key_heads, LEN, head_dim), SINGLE),
        ((key_heads, LEN, head_dim), SINGLE),
        ((heads * head_dim, LEN), SINGLE),
        ((LEN, columns), BFLOAT),
        ((LEN, columns), BFLOAT),
        ((width, LEN), BFLOAT),
        ((LEN, TILE), SINGLE),
    ]
    arrays = (*grads, *quarters, weight, gains, *saved, context)
    kernel = partial(attend_back_kernel, sizes)
    outs = call_kernel(
        kernel, "attend_back", HEAVY, 56, shapes, (place,), arrays, scratch, (earlier,)
    )
    return outs[0], outs[1], outs[2], outs[3:]


def feedfwd_kernel(
    rows_a_ref,
    rows_b_ref,
    rows_c_ref,
    rows_d_ref,
    cot_a_ref,
    cot_b_ref,
    cot_c_ref,
    cot_d_ref,
    weight_ref,
    hidden_ref,
    out_ref,
    part_a_ref,
    part_b_ref,
    part_c_ref,
    part_d_ref,
    rows_turned,
    cot_turned,
    gate_up_grad,
    total,
):
    step = pl.program_id(0)
    quarter = rows_a_ref.shape[0]
    cols = hidden_ref.shape[1]
    rows_refs = (rows_a_ref, rows_b_ref, rows_c_ref, rows_d_ref)
    cot_refs = (cot_a_ref, cot_b_ref, cot_c_ref, cot_d_ref)
    part_refs = (part_a_ref, part_b_ref, part_c_ref, part_d_ref)

    @pl.when(step == 0)
    def _():
        for q in range(4):
            rows_turned[:, q * quarter : (q + 1) * quarter] = rows_refs[q][...].T
            cot_turned[:, q * quarter : (q + 1) * quarter] = cot_refs[q][...].T
        total[...] = jnp.zeros(total.shape, SINGLE)

    for q in range(4):
        tile = slice(q * quarter, (q + 1) * quarter)
        gate_up = dot(rows_refs[q][...], weight_ref[:, : 2 * cols])
        gate_proj, upward = gate_up[:, :cols], gate_up[:, cols:]
        grad_hidden = dot(cot_refs[q][...], weight_ref[:, 2 * cols :])
        sigmoid = 0.5 * jnp.tanh(0.5 * gate_proj) + 0.5
        active = gate_proj * sigmoid
        hidden_ref[tile, :] = (active * upward).astype(BFLOAT)
        slope = sigmoid + active * (1.0 - sigmoid)
        gate_up_grad[tile, :cols] = (grad_hidden * upward * slope).astype(BFLOAT)
        gate_up_grad[tile, cols:] = (grad_hidden * active).astype(BFLOAT)
        total[tile, :] += dot_last(gate_up_grad[tile, :], weight_ref[:, : 2 * cols])
    out_ref[:, : 2 * cols] = dot(rows_turned[...], gate_up_grad[...]).astype(BFLOAT)
    out_ref[:, 2 * cols :] = dot(cot_turned[...], hidden_ref[...]).astype(BFLOAT)

    @pl.when(step == pl.num_programs(0) - 1)
    def _():
        for q in range(4):
            part_refs[q][...] = total[q * quarter : (q + 1) * quarter, :].astype(BFLOAT)


def tile_of(hidden_cols):
    return 384 if hidden_cols % 384 == 0 else hidden_cols


def interleave(gate, up, down):
    tile = tile_of(gate.shape[1])
    pieces = []
    for first in range(0, gate.shape[1], tile):
        pieces += [value[:, first : first + tile] for value in (gate, up, down)]
    return jnp.concatenate(pieces, axis=1)


def part_of(value, kind):
    tile = tile_of(value.shape[1] // 3)
    starts = range(kind * tile, value.shape[1], 3 * tile)
    return jnp.concatenate([value[:, first : first + tile] for first in starts], axis=1)


def feedfwd(quarters, cots, weight):
    quarter, width = quarters[0].shape
    hidden_cols = weight.shape[1] // 3
    cols = tile_of(hidden_cols)
    whole = pl.BlockSpec((quarter, width), lambda j: (0, 0))
    block = pl.BlockSpec((width, 3 * cols), lambda j: (0, j))
    outs = pl.pallas_call(
        feedfwd_kernel,
        grid=(hidden_cols // cols,),
        out_shape=[
            jax.ShapeDtypeStruct((LEN, hidden_cols), BFLOAT),
            jax.ShapeDtypeStruct((width, 3 * hidden_cols), BFLOAT),
        ]
        + [jax.ShapeDtypeStruct((quarter, width), BFLOAT)] * 4,
        in_specs=[whole] * 8 + [block],
        out_specs=[pl.BlockSpec((LEN, cols), lambda j: (0, j)), block] + [whole] * 4,
        scratch_shapes=[
            pltpu.VMEM((width, LEN), BFLOAT),
            pltpu.VMEM((width, LEN), BFLOAT),
            pltpu.VMEM((LEN, 2 * cols), BFLOAT),
            pltpu.VMEM((LEN, width), SINGLE),
        ],
        compiler_params=pltpu.CompilerParams(vmem_limit_bytes=56 * MIB),
        cost_estimate=pl.CostEstimate(flops=HEAVY, bytes_accessed=2**20, transcendentals=0),
        name="feedfwd",
    )(*quarters, *cots, weight)
    return outs[0], outs[1], outs[2:]


def pair_sum_kernel(stay_a_ref, got_a_ref, stay_b_ref, got_b_ref, *refs):
    outs = refs[-4:]
    rows = stay_a_ref.shape[0] // 2
    pairs = ((stay_a_ref, got_a_ref), (stay_b_ref, got_b_ref))
    for half, (stay_ref, got_ref) in enumerate(pairs):
        total = stay_ref[...].astype(SINGLE) + got_ref[...].astype(SINGLE)
        outs[2 * half][...] = total[:rows].astype(outs[2 * half].dtype)
        outs[2 * half + 1][...] = total[rows:].astype(BFLOAT)


def pair_sum(stays, gots, last, earlier):
    rows, width = stays[0].shape
    shapes = [((rows // 2, width), SINGLE if last else BFLOAT), ((rows // 2, width), BFLOAT)] * 2
    arrays = (stays[0], gots[0], stays[1], gots[1])
    outs = call_kernel(pair_sum_kernel, "pair_sum", LIGHT, 8, shapes, (), arrays, earlier=earlier)
    return outs[0::2], outs[1::2]


def down_kernel(hidden_ref, weight_ref, *refs):
    outs, total = refs[-5:-1], refs[-1]
    step = pl.program_id(0)
    product = dot_last(hidden_ref[...], weight_ref[...])

    @pl.when(step == 0)
    def _():
        total[...] = product

    @pl.when(step > 0)
    def _():
        total[...] += product

    @pl.when(step == pl.num_programs(0) - 1)
    def _():
        quarter = total.shape[0] // 4
        for q, part_ref in enumerate(outs):
            part_ref[...] = total[q * quarter : (q + 1) * quarter, :].astype(BFLOAT)


def down_parts_of(hidden, weight, earlier):
    hidden_cols = hidden.shape[1]
    quarter, width = LEN // 4, weight.shape[0]
    cols = tile_of(hidden_cols)
    if cols % 128:
        down = part_of(weight, 2)
        return [
            dot_last(hidden[q * quarter : (q + 1) * quarter], down).astype(BFLOAT) for q in range(4)
        ]
    part = pl.BlockSpec((quarter, width), lambda i: (0, 0))
    return pl.pallas_call(
        down_kernel,
        grid=(hidden_cols // cols,),
        out_shape=[jax.ShapeDtypeStruct((quarter, width), BFLOAT)] * 4,
        in_specs=[
            pl.BlockSpec((LEN, cols), lambda i: (0, i)),
            pl.BlockSpec((width, cols), lambda i: (0, 3 * i + 2)),
        ]
        + [pl.BlockSpec(memory_space=pl.ANY)] * len(earlier),
        out_specs=[part] * 4,
        scratch_shapes=[pltpu.VMEM((LEN, width), SINGLE)],
        compiler_params=pltpu.CompilerParams(vmem_limit_bytes=56 * MIB),
        cost_estimate=pl.CostEstimate(flops=LIGHT, bytes_accessed=2**20, transcendentals=0),
        name="down_parts",
    )(hidden, weight, *earlier)


def finish_kernel(tokens_ref, gain_ref, *refs):
    block_ref, tokens_out_ref = refs[-2:]
    rows = tokens_ref.shape[0] // 2
    for half in range(2):
        part = slice(half * rows, (half + 1) * rows)
        residual, grad, down, down_got, norm, norm_got = refs[6 * half : 6 * half + 6]
        summed = down[...] + down_got[...].astype(SINGLE)
        block_ref[part, :] = (residual[...] + summed).astype(BFLOAT)
        back = norm[...] + norm_got[...].astype(SINGLE)
        back, _ = rms_back(tokens_ref[part, :].astype(SINGLE), gain_ref[...], back)
        tokens_out_ref[part, :] = (grad[...] + back).astype(BFLOAT)


def finish(tokens, gain, halves):
    arrays = (tokens, gain[None, :], *(array for half in halves for array in half))
    kinds = [(tokens.shape, BFLOAT)] * 2
    return call_kernel(finish_kernel, "finish", HEAVY, 56, kinds, (), arrays)


def split_kernel(value_ref, query_ref, key_ref, value_out_ref, out_ref):
    first = 0
    for ref in (query_ref, key_ref, value_out_ref):
        ref[...] = value_ref[:, first : first + ref.shape[1]].astype(SINGLE)
        first += ref.shape[1]
    out_ref[...] = value_ref[:, first:].astype(SINGLE).T


def split_weights(value, shapes):
    kinds = [(shape, SINGLE) for shape in shapes]
    return call_kernel(split_kernel, "split_weights", LIGHT, 56, kinds, (), (value,))


def pack_kernel(query_ref, key_ref, value_ref, out_ref, packed_ref):
    first = 0
    for ref in (query_ref, key_ref, value_ref):
        packed_ref[:, first : first + ref.shape[1]] = ref[...]
        first += ref.shape[1]
    packed_ref[:, first:] = out_ref[...].astype(SINGLE).T.astype(BFLOAT)


def pack_weights(*values):
    columns = sum(value.shape[1] for value in values[:3]) + values[3].shape[0]
    kinds = [((values[0].shape[0], columns), BFLOAT)]
    return call_kernel(pack_kernel, "pack_weights", LIGHT, 56, kinds, (), values)[0]


def later(value, *earlier):
    anywhere = pl.BlockSpec(memory_space=pl.ANY)
    return pl.pallas_call(
        lambda *refs: None,
        out_shape=jax.ShapeDtypeStruct(value.shape, value.dtype),
        in_specs=[anywhere] * (1 + len(earlier)),
        out_specs=anywhere,
        input_output_aliases={0: 0},
        name="later",
    )(value, *earlier)


def wait_aways(parts, *earlier):
    return [later(part, *earlier) if q % 2 else part for q, part in enumerate(parts)]


def rms_scale(values, gain):
    return values * lax.rsqrt(jnp.mean(values * values, axis=-1, keepdims=True) + EPSILON) * gain


def swap(value, axis, bit):
    size = lax.axis_size(axis)
    return lax.ppermute(value, axis, [(i, i ^ bit) for i in range(size)])


def axis_bits(axis):
    return [1 << k for k in range(lax.axis_size(axis).bit_length() - 1)]


def block_order(bits):
    order = [0]
    for bit in bits:
        order = order + [r ^ bit for r in order]
    return order


def butterfly_sum(value):
    for axis in ("dp", "tensor"):
        for bit in axis_bits(axis):
            value = value + swap(value, axis, bit)
    return value


def rms_back(values, gain, grad):
    ratio = lax.rsqrt(jnp.mean(values * values, axis=-1, keepdims=True) + EPSILON)
    scaled = grad * gain
    inner = jnp.mean(scaled * values, axis=-1, keepdims=True)
    return ratio * scaled - values * (ratio * ratio * ratio * inner), grad * values * ratio


def on_device(
    tokens,
    segments,
    cotangent,
    query_weight,
    key_weight,
    value_weight,
    out_weight,
    gate_weight,
    up_weight,
    down_weight,
    attention_gain,
    feedfwd_gain,
    query_gain,
    key_gain,
):
    head_dim = query_gain.shape[0]
    local_rows, width = tokens.shape
    half_rows = local_rows // 2
    tensor_size, here = lax.axis_size("tensor"), lax.axis_index("tensor")
    tensor_bits = axis_bits("tensor")
    half_bits = (tensor_bits, tensor_bits[::-1])
    half_order = [block_order(bits) for bits in half_bits]
    place = jnp.stack(
        [
            jnp.array([order.index(r) for r in range(tensor_size)], jnp.int32)[here ^ j] * half_rows
            + c * (LEN // 2)
            for j in range(tensor_size)
            for c, order in enumerate(half_order)
        ]
    )

    def rows_gather(halves):
        for bits in zip(*half_bits):
            pairs = [(part, swap(part, "tensor", bit)) for part, bit in zip(halves, bits)]
            halves = [jnp.concatenate(pair, axis=0) for pair in pairs]
        return [*pairs[0], *pairs[1]]

    def rows_scatter(parts, earlier=()):
        stays, aways = parts[0::2], parts[1::2]
        for step, bits in enumerate(zip(*(bits[::-1] for bits in half_bits))):
            gots = [swap(part, "tensor", bit) for part, bit in zip(aways, bits)]
            if step < len(tensor_bits) - 1:
                last = step == len(tensor_bits) - 2
                stays, aways = pair_sum(stays, gots, last, earlier)
                first = stays[0] if step == 0 else first
                earlier = ()
        return stays, gots, first

    def halves_of(value):
        return [value[:half_rows], value[half_rows:]]

    token_values = tokens.astype(SINGLE)
    normed = rms_scale(token_values, attention_gain).astype(BFLOAT)
    gathered = rows_gather(halves_of(normed))
    attention_full = lax.all_gather(
        pack_weights(query_weight, key_weight, value_weight, out_weight),
        "dp",
        axis=0,
        tiled=True,
    )
    feedfwd_full = lax.all_gather(
        interleave(gate_weight, up_weight, down_weight.T), "dp", axis=0, tiled=True
    )
    cots = rows_gather(halves_of(cotangent))

    query_cols, key_cols = query_weight.shape[1], key_weight.shape[1]
    sizes = (query_cols // head_dim, key_cols // head_dim, head_dim)
    gains = jnp.concatenate([query_gain, key_gain])[None, :]
    saved, context, attended_parts = attend(
        sizes, place, gathered, attention_full, gains, segments[None, :]
    )
    attended_parts = wait_aways(attended_parts, cots[1], cots[3])
    residuals, normed_two = [], []
    stays, gots, _ = rows_scatter(attended_parts)
    for token_part, stay, got in zip(halves_of(token_values), stays, gots):
        residuals.append(token_part + (stay + got.astype(SINGLE)))
        normed_two.append(rms_scale(residuals[-1], feedfwd_gain).astype(BFLOAT))
    gathered_two = rows_gather(normed_two)

    hidden, feedfwd_part, two_parts = feedfwd(gathered_two, cots, feedfwd_full)
    grad_feedfwd = lax.psum_scatter(feedfwd_part, "dp", scatter_dimension=0, tiled=True)
    stays, gots, _ = rows_scatter(two_parts)
    two_sums = [stay + got.astype(SINGLE) for stay, got in zip(stays, gots)]
    grad_residual, gain_two_part = [], 0.0
    for residual_part, sum_part, cot_part in zip(residuals, two_sums, halves_of(cotangent)):
        back, gain_part = rms_back(residual_part, feedfwd_gain, sum_part)
        grad_residual.append(cot_part.astype(SINGLE) + back)
        gain_two_part = gain_two_part + jnp.sum(gain_part, axis=0)
    grad_low = [part.astype(BFLOAT) for part in grad_residual]
    down_parts = down_parts_of(hidden, feedfwd_full, grad_low)
    gathered_grad = rows_gather(grad_low)

    attention_part, head_gains, row_gain, normed_parts = attend_back(
        sizes, place, gathered_grad, gathered, attention_full, gains, saved, context, down_parts[0]
    )
    down_stays, down_gots, down_first = rows_scatter(
        wait_aways(down_parts, gathered_grad[1], gathered_grad[3]), (head_gains,)
    )
    attention_part = later(attention_part, grad_feedfwd, down_first)
    grad_attention = lax.psum_scatter(attention_part, "dp", scatter_dimension=0, tiled=True)
    normed_stays, normed_gots, normed_first = rows_scatter(normed_parts, (attention_part,))

    gain_parts = jnp.concatenate(
        [row_gain[0] / attention_gain, gain_two_part, *jnp.sum(head_gains, axis=2)]
    )
    gain_sums = butterfly_sum(gain_parts + 0.0 * normed_first[0, 0].astype(SINGLE))
    grad_feedfwd = grad_feedfwd.astype(SINGLE)
    halves = [*zip(residuals, grad_residual, down_stays, down_gots, normed_stays, normed_gots)]
    shapes = [value.shape for value in (query_weight, key_weight, value_weight, out_weight)]
    return (
        *finish(tokens, attention_gain, halves),
        *split_weights(grad_attention, shapes),
        part_of(grad_feedfwd, 0),
        part_of(grad_feedfwd, 1),
        part_of(grad_feedfwd, 2).T,
        gain_sums[:width],
        gain_sums[width : 2 * width],
        gain_sums[2 * width : 2 * width + head_dim],
        gain_sums[2 * width + head_dim :],
    )


def solution(mesh):
    in_specs = (
        P(("dp", "tensor"), None),
        P("dp"),
        P(("dp", "tensor"), None),
        P("dp", "tensor"),
        P("dp", "tensor"),
        P("dp", "tensor"),
        P("tensor", "dp"),
        P("dp", "tensor"),
        P("dp", "tensor"),
        P("tensor", "dp"),
        P(),
        P(),
        P(),
        P(),
    )
    out_specs = (
        P(("dp", "tensor"), None),
        P(("dp", "tensor"), None),
        P("dp", "tensor"),
        P("dp", "tensor"),
        P("dp", "tensor"),
        P("tensor", "dp"),
        P("dp", "tensor"),
        P("dp", "tensor"),
        P("tensor", "dp"),
        P(),
        P(),
        P(),
        P(),
    )
    return jax.shard_map(
        on_device, mesh=mesh, in_specs=in_specs, out_specs=out_specs, check_vma=False
    )
```

```python
from functools import partial
import math

import jax
import jax.numpy as jnp
from jax import lax
from jax.experimental import pallas as pl
from jax.experimental.pallas import tpu as pltpu
from jax.sharding import PartitionSpec as P

LEN = 1024


EPSILON = 1e-05
THETA = 1000000.0
MASKED = -1e30
DOCUMENTS = 3
SHORTEST = 204
TILE = 256
LOG2E = math.log2(math.e)
MIB = 2**20
HEAVY, LIGHT = 16 * 10**9, 10**9
BFLOAT, SINGLE = jnp.bfloat16, jnp.float32


def call_kernel(kernel, name, weight, limit, shapes, scalars, arrays, scratch=(), earlier=()):
    whole = pl.BlockSpec(memory_space=pltpu.VMEM)
    specs = [pl.BlockSpec(memory_space=pltpu.SMEM)] * len(scalars) + [whole] * len(arrays)
    return pl.pallas_call(
        kernel,
        out_shape=[jax.ShapeDtypeStruct(*shape) for shape in shapes],
        in_specs=specs + [pl.BlockSpec(memory_space=pl.ANY)] * len(earlier),
        out_specs=[whole] * len(shapes),
        scratch_shapes=[pltpu.VMEM(*shape) for shape in scratch],
        compiler_params=pltpu.CompilerParams(vmem_limit_bytes=limit * MIB),
        cost_estimate=pl.CostEstimate(flops=weight, bytes_accessed=2**20, transcendentals=0),
        name=name,
    )(*scalars, *arrays, *earlier)


def dot(left, right):
    return jnp.dot(left, right, preferred_element_type=SINGLE)


def dot_last(left, right):
    return lax.dot_general(left, right, (((1,), (1,)), ((), ())), preferred_element_type=SINGLE)


def dot_first(left_refs, right_ref):
    total, first = 0.0, 0
    for left_ref in left_refs:
        rows = left_ref.shape[0]
        total = total + lax.dot_general(
            left_ref[...],
            right_ref[first : first + rows, :],
            (((0,), (0,)), ((), ())),
            preferred_element_type=SINGLE,
        )
        first += rows
    return total


def key_span(start):
    reach = LEN - (DOCUMENTS - 1) * SHORTEST - 1
    return max(0, (start - reach) // 128 * 128), start + TILE


def mask_bias(begin_ref, start, low, high):
    shape = (high - low, TILE)
    key_pos = low + lax.broadcasted_iota(jnp.int32, shape, 0)
    query_pos = start + lax.broadcasted_iota(jnp.int32, shape, 1)
    counts = (key_pos >= begin_ref[:, start : start + TILE]) & (key_pos <= query_pos)
    return jnp.where(counts, 0.0, MASKED)


def head_ratio(values):
    return lax.rsqrt(jnp.mean(values * values, axis=0, keepdims=True) + EPSILON)


def turn(values, cosine, sine):
    half_dim = values.shape[0] // 2
    first, second = values[:half_dim], values[half_dim:]
    return jnp.concatenate([first * cosine - second * sine, second * cosine + first * sine], axis=0)


def gain_columns(gain_ref, head_dim):
    turned = jnp.broadcast_to(gain_ref[...], (8, gain_ref.shape[1])).T
    return turned[:head_dim, :1], turned[head_dim : 2 * head_dim, :1]


def spread(place_ref, natural, out_ref):
    rows = LEN // place_ref.shape[0]
    for block in range(place_ref.shape[0]):
        start = pl.multiple_of(place_ref[block], rows)
        out_ref[pl.ds(start, rows), :] = natural[block * rows : (block + 1) * rows, :]


def collect(place_ref, value_ref, natural):
    rows = LEN // place_ref.shape[0]
    for block in range(place_ref.shape[0]):
        start = pl.multiple_of(place_ref[block], rows)
        natural[block * rows : (block + 1) * rows, :] = value_ref[pl.ds(start, rows), :]


def attend_kernel(
    sizes,
    place_ref,
    rows_a_ref,
    rows_b_ref,
    rows_c_ref,
    rows_d_ref,
    weight_ref,
    gain_ref,
    segment_ref,
    raw_ref,
    query_ref,
    key_ref,
    query_row_ref,
    key_row_ref,
    value_row_ref,
    total_ref,
    attended_ref,
    cosine_ref,
    sine_ref,
    begin_ref,
    context_ref,
    part_a_ref,
    part_b_ref,
    part_c_ref,
    part_d_ref,
    mixed,
    natural,
    extended,
    bias,
    context,
):
    query_heads, key_heads, head_dim = sizes
    group_size = query_heads // key_heads
    heads = query_heads + key_heads
    columns = natural.shape[1]
    quarter = rows_a_ref.shape[0]
    weight = weight_ref[:, :columns]
    for q, rows_ref in enumerate((rows_a_ref, rows_b_ref, rows_c_ref, rows_d_ref)):
        mixed[q * quarter : (q + 1) * quarter, :] = dot(rows_ref[...], weight)
    collect(place_ref, mixed, natural)
    for start in range(0, LEN, 128):
        raw_ref[:, start : start + 128] = natural[start : start + 128, :].T

    segment = segment_ref[...]
    first_count = jnp.sum((segment == 0).astype(SINGLE), axis=1, keepdims=True)
    second_count = jnp.sum((segment == 1).astype(SINGLE), axis=1, keepdims=True)
    begin = jnp.where(
        segment == 0, 0.0, jnp.where(segment == 1, first_count, first_count + second_count)
    )
    begin_ref[...] = begin.astype(jnp.int32)
    half_dim = head_dim // 2
    shape = (half_dim, LEN)
    steps = lax.broadcasted_iota(jnp.int32, shape, 0).astype(SINGLE)
    order = lax.broadcasted_iota(jnp.int32, shape, 1).astype(SINGLE)
    angles = (order - begin) * jnp.exp(steps * (-math.log(THETA) / half_dim))
    cosine, sine = jnp.cos(angles), jnp.sin(angles)
    cosine_ref[...] = cosine
    sine_ref[...] = sine

    gains = gain_columns(gain_ref, head_dim)
    for head in range(heads):
        values = raw_ref[head * head_dim : (head + 1) * head_dim, :]
        gain = gains[0] if head < query_heads else gains[1]
        turned = turn(values * head_ratio(values) * gain, cosine, sine)
        if head < query_heads:
            query_ref[head] = turned.astype(BFLOAT)
            query_row_ref[head] = turned.T.astype(BFLOAT)
        else:
            key_ref[head - query_heads] = turned.astype(BFLOAT)
            key_row_ref[head - query_heads] = turned.T.astype(BFLOAT)
    for head in range(key_heads):
        first = (heads + head) * head_dim
        extended[head, :head_dim, :] = raw_ref[first : first + head_dim, :].astype(BFLOAT)
        extended[head, head_dim:, :] = jnp.ones((extended.shape[1] - head_dim, LEN), BFLOAT)
        value_row_ref[head] = natural[:, first : first + head_dim].astype(BFLOAT)
    factor = LOG2E * head_dim ** (-0.5)
    for start in range(0, LEN, TILE):
        low, high = key_span(start)
        span, tile = slice(low, high), slice(start, start + TILE)
        bias[: high - low, :] = mask_bias(begin_ref, start, low, high)

        def one_head(head, carry):
            key_head = head // group_size
            scores = dot(key_row_ref[key_head, span, :], query_ref[head, :, tile])
            powers = jnp.exp2(scores * factor + bias[: high - low, :])
            summed = dot(extended[key_head, :, span], powers.astype(BFLOAT))
            total = summed[head_dim : head_dim + 1, :]
            total_ref[head, :, tile] = jnp.log2(total)
            attended_ref[head, :, tile] = summed[:head_dim, :] / total
            return carry

        lax.fori_loop(0, query_heads, one_head, 0)
    for head in range(query_heads):
        context[:, head * head_dim : (head + 1) * head_dim] = attended_ref[head].T.astype(BFLOAT)
    spread(place_ref, context, context_ref)
    out_weight = weight_ref[:, columns:]
    for q, part_ref in enumerate((part_a_ref, part_b_ref, part_c_ref, part_d_ref)):
        rows = context_ref[q * quarter : (q + 1) * quarter, :]
        part_ref[...] = dot_last(rows, out_weight).astype(BFLOAT)


def attend(sizes, place, quarters, weight, gains, segments):
    query_heads, key_heads, head_dim = sizes
    columns = (query_heads + 2 * key_heads) * head_dim
    quarter, width = quarters[0].shape
    shapes = [
        ((columns, LEN), SINGLE),
        ((query_heads, head_dim, LEN), BFLOAT),
        ((key_heads, head_dim, LEN), BFLOAT),
        ((query_heads, LEN, head_dim), BFLOAT),
        ((key_heads, LEN, head_dim), BFLOAT),
        ((key_heads, LEN, head_dim), BFLOAT),
        ((query_heads, 1, LEN), SINGLE),
        ((query_heads, head_dim, LEN), SINGLE),
        ((head_dim // 2, LEN), SINGLE),
        ((head_dim // 2, LEN), SINGLE),
        ((1, LEN), jnp.int32),
        ((LEN, query_heads * head_dim), BFLOAT),
    ] + [((quarter, width), BFLOAT)] * 4
    scratch = [
        ((LEN, columns), SINGLE),
        ((LEN, columns), SINGLE),
        ((key_heads, head_dim + 16, LEN), BFLOAT),
        ((LEN, TILE), SINGLE),
        ((LEN, query_heads * head_dim), BFLOAT),
    ]
    arrays = (*quarters, weight, gains, segments)
    outs = call_kernel(
        partial(attend_kernel, sizes), "attend", HEAVY, 56, shapes, (place,), arrays, scratch
    )
    return outs[:11], outs[11], outs[12:]


def attend_back_kernel(
    sizes,
    place_ref,
    grad_a_ref,
    grad_b_ref,
    grad_c_ref,
    grad_d_ref,
    rows_a_ref,
    rows_b_ref,
    rows_c_ref,
    rows_d_ref,
    weight_ref,
    gain_ref,
    raw_ref,
    query_ref,
    key_ref,
    query_row_ref,
    key_row_ref,
    value_row_ref,
    total_ref,
    attended_ref,
    cosine_ref,
    sine_ref,
    begin_ref,
    context_ref,
    earlier_ref,
    weight_grad_ref,
    head_gain_ref,
    row_gain_ref,
    part_a_ref,
    part_b_ref,
    part_c_ref,
    part_d_ref,
    mixed,
    context,
    grad_row,
    grad_col,
    query_grad,
    key_grad,
    value_grad,
    joined,
    natural,
    out_ref,
    bias,
):
    query_heads, key_heads, head_dim = sizes
    group_size = query_heads // key_heads
    heads = query_heads + key_heads
    columns = natural.shape[1]
    quarter = grad_a_ref.shape[0]
    out_weight = weight_ref[:, columns:]
    grad_refs = (grad_a_ref, grad_b_ref, grad_c_ref, grad_d_ref)
    for q, rows_ref in enumerate(grad_refs):
        mixed[q * quarter : (q + 1) * quarter, :] = dot(rows_ref[...], out_weight).astype(BFLOAT)
    weight_grad_ref[:, columns:] = dot_first(grad_refs, context_ref).astype(BFLOAT)
    collect(place_ref, mixed, context)
    for head in range(query_heads):
        part = context[:, head * head_dim : (head + 1) * head_dim]
        grad_row[head] = part
        grad_col[head] = part.astype(SINGLE).T
    key_grad[...] = jnp.zeros(key_grad.shape, SINGLE)
    value_grad[...] = jnp.zeros(value_grad.shape, SINGLE)
    scale = head_dim ** (-0.5)
    factor = LOG2E * scale
    for start in range(0, LEN, TILE):
        low, high = key_span(start)
        span, tile = slice(low, high), slice(start, start + TILE)
        bias[: high - low, :] = mask_bias(begin_ref, start, low, high)

        def one_head(head, carry):
            key_head = head // group_size
            scores = dot(key_row_ref[key_head, span, :], query_ref[head, :, tile])
            probs = jnp.exp2(scores * factor + bias[: high - low, :] - total_ref[head, :, tile])
            grads = grad_col[head, :, tile]
            inner = jnp.sum(grads * attended_ref[head, :, tile], axis=0, keepdims=True)
            probs_grad = dot(value_row_ref[key_head, span, :], grads.astype(BFLOAT))
            scores_grad = (probs * (probs_grad - inner)).astype(BFLOAT)
            value_grad[key_head, span, :] += dot(probs.astype(BFLOAT), grad_row[head, tile, :])
            key_grad[key_head, span, :] += dot(scores_grad, query_row_ref[head, tile, :])
            query_grad[head, :, tile] = dot(key_ref[key_head, :, span], scores_grad)
            return carry

        lax.fori_loop(0, query_heads, one_head, 0)
    cosine, sine = cosine_ref[...], sine_ref[...]
    gains = gain_columns(gain_ref, head_dim)
    for kind in range(2):
        head_gain_ref[kind] = jnp.zeros(head_gain_ref.shape[1:], SINGLE)
    for head in range(heads):
        kind = 0 if head < query_heads else 1
        grads = query_grad[head] if kind == 0 else key_grad[head - query_heads].T
        grads = turn(grads * scale, cosine, -sine)
        values = raw_ref[head * head_dim : (head + 1) * head_dim, :]
        ratio = head_ratio(values)
        normed = values * ratio
        weighted = grads * gains[kind]
        inner = jnp.mean(weighted * normed, axis=0, keepdims=True)
        joined[head * head_dim : (head + 1) * head_dim, :] = ratio * (weighted - normed * inner)
        products = grads * normed
        folded = products[:, :128]
        for first in range(128, LEN, 128):
            folded = folded + products[:, first : first + 128]
        head_gain_ref[kind] += folded
    for start in range(0, LEN, 128):
        natural[start : start + 128, : heads * head_dim] = joined[:, start : start + 128].T.astype(
            BFLOAT
        )
    for head in range(key_heads):
        first = (heads + head) * head_dim
        natural[:, first : first + head_dim] = value_grad[head].astype(BFLOAT)
    spread(place_ref, natural, out_ref)
    weight = weight_ref[:, :columns]
    row_gain = jnp.zeros(row_gain_ref.shape, SINGLE)
    rows_refs = (rows_a_ref, rows_b_ref, rows_c_ref, rows_d_ref)
    for q, part_ref in enumerate((part_a_ref, part_b_ref, part_c_ref, part_d_ref)):
        part = dot_last(out_ref[q * quarter : (q + 1) * quarter, :], weight)
        part_ref[...] = part.astype(BFLOAT)
        row_gain += jnp.sum(part * rows_refs[q][...].astype(SINGLE), axis=0, keepdims=True)
    row_gain_ref[...] = row_gain
    weight_grad_ref[:, :columns] = dot_first(rows_refs, out_ref).astype(BFLOAT)


def attend_back(sizes, place, grads, quarters, weight, gains, saved, context, earlier):
    query_heads, key_heads, head_dim = sizes
    heads = query_heads + key_heads
    columns = (heads + key_heads) * head_dim
    quarter, width = quarters[0].shape
    shapes = [
        (weight.shape, BFLOAT),
        ((2, head_dim, 128), SINGLE),
        ((1, width), SINGLE),
    ] + [((quarter, width), BFLOAT)] * 4
    scratch = [
        ((LEN, query_heads * head_dim), BFLOAT),
        ((LEN, query_heads * head_dim), BFLOAT),
        ((query_heads, LEN, head_dim), BFLOAT),
        ((query_heads, head_dim, LEN), SINGLE),
        ((query_heads, head_dim, LEN), SINGLE),
        ((key_heads, LEN, head_dim), SINGLE),
        ((key_heads, LEN, head_dim), SINGLE),
        ((heads * head_dim, LEN), SINGLE),
        ((LEN, columns), BFLOAT),
        ((LEN, columns), BFLOAT),
        ((LEN, TILE), SINGLE),
    ]
    arrays = (*grads, *quarters, weight, gains, *saved, context)
    kernel = partial(attend_back_kernel, sizes)
    outs = call_kernel(
        kernel, "attend_back", HEAVY, 56, shapes, (place,), arrays, scratch, (earlier,)
    )
    return outs[0], outs[1], outs[2], outs[3:]


def feedfwd_kernel(
    rows_a_ref,
    rows_b_ref,
    rows_c_ref,
    rows_d_ref,
    cot_a_ref,
    cot_b_ref,
    cot_c_ref,
    cot_d_ref,
    weight_ref,
    hidden_ref,
    out_ref,
    part_a_ref,
    part_b_ref,
    part_c_ref,
    part_d_ref,
    gate_up_grad,
    total,
):
    step = pl.program_id(0)
    quarter = rows_a_ref.shape[0]
    cols = hidden_ref.shape[1]
    rows_refs = (rows_a_ref, rows_b_ref, rows_c_ref, rows_d_ref)
    cot_refs = (cot_a_ref, cot_b_ref, cot_c_ref, cot_d_ref)
    part_refs = (part_a_ref, part_b_ref, part_c_ref, part_d_ref)

    @pl.when(step == 0)
    def _():
        total[...] = jnp.zeros(total.shape, SINGLE)

    for q in range(4):
        tile = slice(q * quarter, (q + 1) * quarter)
        gate_up = dot(rows_refs[q][...], weight_ref[:, : 2 * cols])
        gate_proj, upward = gate_up[:, :cols], gate_up[:, cols:]
        grad_hidden = dot(cot_refs[q][...], weight_ref[:, 2 * cols :])
        sigmoid = 0.5 * jnp.tanh(0.5 * gate_proj) + 0.5
        active = gate_proj * sigmoid
        hidden_ref[tile, :] = (active * upward).astype(BFLOAT)
        slope = sigmoid + active * (1.0 - sigmoid)
        gate_up_grad[tile, :cols] = (grad_hidden * upward * slope).astype(BFLOAT)
        gate_up_grad[tile, cols:] = (grad_hidden * active).astype(BFLOAT)
        total[tile, :] += dot_last(gate_up_grad[tile, :], weight_ref[:, : 2 * cols])
    out_ref[:, : 2 * cols] = dot_first(rows_refs, gate_up_grad).astype(BFLOAT)
    out_ref[:, 2 * cols :] = dot_first(cot_refs, hidden_ref).astype(BFLOAT)

    @pl.when(step == pl.num_programs(0) - 1)
    def _():
        for q in range(4):
            part_refs[q][...] = total[q * quarter : (q + 1) * quarter, :].astype(BFLOAT)


def tile_of(hidden_cols):
    return 384 if hidden_cols % 384 == 0 else hidden_cols


def interleave(gate, up, down):
    tile = tile_of(gate.shape[1])
    pieces = []
    for first in range(0, gate.shape[1], tile):
        pieces += [value[:, first : first + tile] for value in (gate, up, down)]
    return jnp.concatenate(pieces, axis=1)


def part_of(value, kind):
    tile = tile_of(value.shape[1] // 3)
    starts = range(kind * tile, value.shape[1], 3 * tile)
    return jnp.concatenate([value[:, first : first + tile] for first in starts], axis=1)


def feedfwd(quarters, cots, weight):
    quarter, width = quarters[0].shape
    hidden_cols = weight.shape[1] // 3
    cols = tile_of(hidden_cols)
    whole = pl.BlockSpec((quarter, width), lambda j: (0, 0))
    block = pl.BlockSpec((width, 3 * cols), lambda j: (0, j))
    outs = pl.pallas_call(
        feedfwd_kernel,
        grid=(hidden_cols // cols,),
        out_shape=[
            jax.ShapeDtypeStruct((LEN, hidden_cols), BFLOAT),
            jax.ShapeDtypeStruct((width, 3 * hidden_cols), BFLOAT),
        ]
        + [jax.ShapeDtypeStruct((quarter, width), BFLOAT)] * 4,
        in_specs=[whole] * 8 + [block],
        out_specs=[pl.BlockSpec((LEN, cols), lambda j: (0, j)), block] + [whole] * 4,
        scratch_shapes=[
            pltpu.VMEM((LEN, 2 * cols), BFLOAT),
            pltpu.VMEM((LEN, width), SINGLE),
        ],
        compiler_params=pltpu.CompilerParams(vmem_limit_bytes=56 * MIB),
        cost_estimate=pl.CostEstimate(flops=HEAVY, bytes_accessed=2**20, transcendentals=0),
        name="feedfwd",
    )(*quarters, *cots, weight)
    return outs[0], outs[1], outs[2:]


def pair_sum_kernel(stay_a_ref, got_a_ref, stay_b_ref, got_b_ref, *refs):
    outs = refs[-4:]
    rows = stay_a_ref.shape[0] // 2
    pairs = ((stay_a_ref, got_a_ref), (stay_b_ref, got_b_ref))
    for half, (stay_ref, got_ref) in enumerate(pairs):
        total = stay_ref[...].astype(SINGLE) + got_ref[...].astype(SINGLE)
        outs[2 * half][...] = total[:rows].astype(outs[2 * half].dtype)
        outs[2 * half + 1][...] = total[rows:].astype(BFLOAT)


def pair_sum(stays, gots, last, earlier):
    rows, width = stays[0].shape
    shapes = [((rows // 2, width), SINGLE if last else BFLOAT), ((rows // 2, width), BFLOAT)] * 2
    arrays = (stays[0], gots[0], stays[1], gots[1])
    outs = call_kernel(pair_sum_kernel, "pair_sum", LIGHT, 8, shapes, (), arrays, earlier=earlier)
    return outs[0::2], outs[1::2]


def down_kernel(hidden_ref, weight_ref, *refs):
    outs, total = refs[-5:-1], refs[-1]
    step = pl.program_id(0)
    product = dot_last(hidden_ref[...], weight_ref[...])

    @pl.when(step == 0)
    def _():
        total[...] = product

    @pl.when(step > 0)
    def _():
        total[...] += product

    @pl.when(step == pl.num_programs(0) - 1)
    def _():
        quarter = total.shape[0] // 4
        for q, part_ref in enumerate(outs):
            part_ref[...] = total[q * quarter : (q + 1) * quarter, :].astype(BFLOAT)


def down_parts_of(hidden, weight, earlier):
    hidden_cols = hidden.shape[1]
    quarter, width = LEN // 4, weight.shape[0]
    cols = tile_of(hidden_cols)
    if cols % 128:
        down = part_of(weight, 2)
        return [
            dot_last(hidden[q * quarter : (q + 1) * quarter], down).astype(BFLOAT) for q in range(4)
        ]
    part = pl.BlockSpec((quarter, width), lambda i: (0, 0))
    return pl.pallas_call(
        down_kernel,
        grid=(hidden_cols // cols,),
        out_shape=[jax.ShapeDtypeStruct((quarter, width), BFLOAT)] * 4,
        in_specs=[
            pl.BlockSpec((LEN, cols), lambda i: (0, i)),
            pl.BlockSpec((width, cols), lambda i: (0, 3 * i + 2)),
        ]
        + [pl.BlockSpec(memory_space=pl.ANY)] * len(earlier),
        out_specs=[part] * 4,
        scratch_shapes=[pltpu.VMEM((LEN, width), SINGLE)],
        compiler_params=pltpu.CompilerParams(vmem_limit_bytes=56 * MIB),
        cost_estimate=pl.CostEstimate(flops=LIGHT, bytes_accessed=2**20, transcendentals=0),
        name="down_parts",
    )(hidden, weight, *earlier)


def finish_kernel(tokens_ref, gain_ref, *refs):
    block_ref, tokens_out_ref = refs[-2:]
    rows = tokens_ref.shape[0] // 2
    for half in range(2):
        part = slice(half * rows, (half + 1) * rows)
        residual, grad, down, down_got, norm, norm_got = refs[6 * half : 6 * half + 6]
        summed = down[...] + down_got[...].astype(SINGLE)
        block_ref[part, :] = (residual[...] + summed).astype(BFLOAT)
        back = norm[...] + norm_got[...].astype(SINGLE)
        back, _ = rms_back(tokens_ref[part, :].astype(SINGLE), gain_ref[...], back)
        tokens_out_ref[part, :] = (grad[...] + back).astype(BFLOAT)


def finish(tokens, gain, halves):
    arrays = (tokens, gain[None, :], *(array for half in halves for array in half))
    kinds = [(tokens.shape, BFLOAT)] * 2
    return call_kernel(finish_kernel, "finish", HEAVY, 56, kinds, (), arrays)


def split_kernel(value_ref, query_ref, key_ref, value_out_ref, out_ref):
    first = 0
    for ref in (query_ref, key_ref, value_out_ref):
        ref[...] = value_ref[:, first : first + ref.shape[1]].astype(SINGLE)
        first += ref.shape[1]
    out_ref[...] = value_ref[:, first:].astype(SINGLE).T


def split_weights(value, shapes):
    kinds = [(shape, SINGLE) for shape in shapes]
    return call_kernel(split_kernel, "split_weights", LIGHT, 56, kinds, (), (value,))


def pack_kernel(query_ref, key_ref, value_ref, out_ref, packed_ref):
    first = 0
    for ref in (query_ref, key_ref, value_ref):
        packed_ref[:, first : first + ref.shape[1]] = ref[...]
        first += ref.shape[1]
    packed_ref[:, first:] = out_ref[...].astype(SINGLE).T.astype(BFLOAT)


def pack_weights(*values):
    columns = sum(value.shape[1] for value in values[:3]) + values[3].shape[0]
    kinds = [((values[0].shape[0], columns), BFLOAT)]
    return call_kernel(pack_kernel, "pack_weights", LIGHT, 56, kinds, (), values)[0]


def later(value, *earlier):
    anywhere = pl.BlockSpec(memory_space=pl.ANY)
    return pl.pallas_call(
        lambda *refs: None,
        out_shape=jax.ShapeDtypeStruct(value.shape, value.dtype),
        in_specs=[anywhere] * (1 + len(earlier)),
        out_specs=anywhere,
        input_output_aliases={0: 0},
        name="later",
    )(value, *earlier)


def wait_aways(parts, *earlier):
    return [later(part, *earlier) if q % 2 else part for q, part in enumerate(parts)]


def rms_scale(values, gain):
    return values * lax.rsqrt(jnp.mean(values * values, axis=-1, keepdims=True) + EPSILON) * gain


def swap(value, axis, bit):
    size = lax.axis_size(axis)
    return lax.ppermute(value, axis, [(i, i ^ bit) for i in range(size)])


def axis_bits(axis):
    return [1 << k for k in range(lax.axis_size(axis).bit_length() - 1)]


def block_order(bits):
    order = [0]
    for bit in bits:
        order = order + [r ^ bit for r in order]
    return order


def butterfly_sum(value):
    for axis in ("dp", "tensor"):
        for bit in axis_bits(axis):
            value = value + swap(value, axis, bit)
    return value


def rms_back(values, gain, grad):
    ratio = lax.rsqrt(jnp.mean(values * values, axis=-1, keepdims=True) + EPSILON)
    scaled = grad * gain
    inner = jnp.mean(scaled * values, axis=-1, keepdims=True)
    return ratio * scaled - values * (ratio * ratio * ratio * inner), grad * values * ratio


def on_device(
    tokens,
    segments,
    cotangent,
    query_weight,
    key_weight,
    value_weight,
    out_weight,
    gate_weight,
    up_weight,
    down_weight,
    attention_gain,
    feedfwd_gain,
    query_gain,
    key_gain,
):
    head_dim = query_gain.shape[0]
    local_rows, width = tokens.shape
    half_rows = local_rows // 2
    tensor_size, here = lax.axis_size("tensor"), lax.axis_index("tensor")
    tensor_bits = axis_bits("tensor")
    half_bits = (tensor_bits, tensor_bits[::-1])
    half_order = [block_order(bits) for bits in half_bits]
    place = jnp.stack(
        [
            jnp.array([order.index(r) for r in range(tensor_size)], jnp.int32)[here ^ j] * half_rows
            + c * (LEN // 2)
            for j in range(tensor_size)
            for c, order in enumerate(half_order)
        ]
    )

    def rows_gather(halves):
        for bits in zip(*half_bits):
            pairs = [(part, swap(part, "tensor", bit)) for part, bit in zip(halves, bits)]
            halves = [jnp.concatenate(pair, axis=0) for pair in pairs]
        return [*pairs[0], *pairs[1]]

    def rows_scatter(parts, earlier=()):
        stays, aways = parts[0::2], parts[1::2]
        for step, bits in enumerate(zip(*(bits[::-1] for bits in half_bits))):
            gots = [swap(part, "tensor", bit) for part, bit in zip(aways, bits)]
            if step < len(tensor_bits) - 1:
                last = step == len(tensor_bits) - 2
                stays, aways = pair_sum(stays, gots, last, earlier)
                first = stays[0] if step == 0 else first
                earlier = ()
        return stays, gots, first

    def halves_of(value):
        return [value[:half_rows], value[half_rows:]]

    token_values = tokens.astype(SINGLE)
    normed = rms_scale(token_values, attention_gain).astype(BFLOAT)
    gathered = rows_gather(halves_of(normed))
    attention_full = lax.all_gather(
        pack_weights(query_weight, key_weight, value_weight, out_weight),
        "dp",
        axis=0,
        tiled=True,
    )
    feedfwd_full = lax.all_gather(
        interleave(gate_weight, up_weight, down_weight.T), "dp", axis=0, tiled=True
    )
    cots = rows_gather(halves_of(cotangent))

    query_cols, key_cols = query_weight.shape[1], key_weight.shape[1]
    sizes = (query_cols // head_dim, key_cols // head_dim, head_dim)
    gains = jnp.concatenate([query_gain, key_gain])[None, :]
    saved, context, attended_parts = attend(
        sizes, place, gathered, attention_full, gains, segments[None, :]
    )
    attended_parts = wait_aways(attended_parts, cots[1], cots[3])
    residuals, normed_two = [], []
    stays, gots, _ = rows_scatter(attended_parts)
    for token_part, stay, got in zip(halves_of(token_values), stays, gots):
        residuals.append(token_part + (stay + got.astype(SINGLE)))
        normed_two.append(rms_scale(residuals[-1], feedfwd_gain).astype(BFLOAT))
    gathered_two = rows_gather(normed_two)

    hidden, feedfwd_part, two_parts = feedfwd(gathered_two, cots, feedfwd_full)
    grad_feedfwd = lax.psum_scatter(feedfwd_part, "dp", scatter_dimension=0, tiled=True)
    stays, gots, _ = rows_scatter(two_parts)
    two_sums = [stay + got.astype(SINGLE) for stay, got in zip(stays, gots)]
    grad_residual, gain_two_part = [], 0.0
    for residual_part, sum_part, cot_part in zip(residuals, two_sums, halves_of(cotangent)):
        back, gain_part = rms_back(residual_part, feedfwd_gain, sum_part)
        grad_residual.append(cot_part.astype(SINGLE) + back)
        gain_two_part = gain_two_part + jnp.sum(gain_part, axis=0)
    grad_low = [part.astype(BFLOAT) for part in grad_residual]
    down_parts = down_parts_of(hidden, feedfwd_full, grad_low)
    gathered_grad = rows_gather(grad_low)

    attention_part, head_gains, row_gain, normed_parts = attend_back(
        sizes, place, gathered_grad, gathered, attention_full, gains, saved, context, down_parts[0]
    )
    down_stays, down_gots, down_first = rows_scatter(
        wait_aways(down_parts, gathered_grad[1], gathered_grad[3]), (head_gains,)
    )
    attention_part = later(attention_part, grad_feedfwd, down_first)
    grad_attention = lax.psum_scatter(attention_part, "dp", scatter_dimension=0, tiled=True)
    normed_stays, normed_gots, normed_first = rows_scatter(normed_parts, (attention_part,))

    gain_parts = jnp.concatenate(
        [row_gain[0] / attention_gain, gain_two_part, *jnp.sum(head_gains, axis=2)]
    )
    gain_sums = butterfly_sum(gain_parts + 0.0 * normed_first[0, 0].astype(SINGLE))
    grad_feedfwd = grad_feedfwd.astype(SINGLE)
    halves = [*zip(residuals, grad_residual, down_stays, down_gots, normed_stays, normed_gots)]
    shapes = [value.shape for value in (query_weight, key_weight, value_weight, out_weight)]
    return (
        *finish(tokens, attention_gain, halves),
        *split_weights(grad_attention, shapes),
        part_of(grad_feedfwd, 0),
        part_of(grad_feedfwd, 1),
        part_of(grad_feedfwd, 2).T,
        gain_sums[:width],
        gain_sums[width : 2 * width],
        gain_sums[2 * width : 2 * width + head_dim],
        gain_sums[2 * width + head_dim :],
    )


def solution(mesh):
    in_specs = (
        P(("dp", "tensor"), None),
        P("dp"),
        P(("dp", "tensor"), None),
        P("dp", "tensor"),
        P("dp", "tensor"),
        P("dp", "tensor"),
        P("tensor", "dp"),
        P("dp", "tensor"),
        P("dp", "tensor"),
        P("tensor", "dp"),
        P(),
        P(),
        P(),
        P(),
    )
    out_specs = (
        P(("dp", "tensor"), None),
        P(("dp", "tensor"), None),
        P("dp", "tensor"),
        P("dp", "tensor"),
        P("dp", "tensor"),
        P("tensor", "dp"),
        P("dp", "tensor"),
        P("dp", "tensor"),
        P("tensor", "dp"),
        P(),
        P(),
        P(),
        P(),
    )
    return jax.shard_map(
        on_device, mesh=mesh, in_specs=in_specs, out_specs=out_specs, check_vma=False
    )
```

```python
from functools import partial
import math

import jax
import jax.numpy as jnp
from jax import lax
from jax.experimental import pallas as pl
from jax.experimental.pallas import tpu as pltpu
from jax.sharding import PartitionSpec as P

LEN = 1024


EPSILON = 1e-05
THETA = 1000000.0
MASKED = -1e30
DOCUMENTS = 3
SHORTEST = 204
TILE = 256
LOG2E = math.log2(math.e)
MIB = 2**20
HEAVY, LIGHT = 16 * 10**9, 10**9
BFLOAT, SINGLE = jnp.bfloat16, jnp.float32


def call_kernel(kernel, name, weight, limit, shapes, scalars, arrays, scratch=(), earlier=()):
    whole = pl.BlockSpec(memory_space=pltpu.VMEM)
    specs = [pl.BlockSpec(memory_space=pltpu.SMEM)] * len(scalars) + [whole] * len(arrays)
    return pl.pallas_call(
        kernel,
        out_shape=[jax.ShapeDtypeStruct(*shape) for shape in shapes],
        in_specs=specs + [pl.BlockSpec(memory_space=pl.ANY)] * len(earlier),
        out_specs=[whole] * len(shapes),
        scratch_shapes=[pltpu.VMEM(*shape) for shape in scratch],
        compiler_params=pltpu.CompilerParams(vmem_limit_bytes=limit * MIB),
        cost_estimate=pl.CostEstimate(flops=weight, bytes_accessed=2**20, transcendentals=0),
        name=name,
    )(*scalars, *arrays, *earlier)


def dot(left, right):
    return jnp.dot(left, right, preferred_element_type=SINGLE)


def dot_last(left, right):
    return lax.dot_general(left, right, (((1,), (1,)), ((), ())), preferred_element_type=SINGLE)


def dot_first(left_refs, right_ref):
    total, first = 0.0, 0
    for left_ref in left_refs:
        rows = left_ref.shape[0]
        total = total + lax.dot_general(
            left_ref[...],
            right_ref[first : first + rows, :],
            (((0,), (0,)), ((), ())),
            preferred_element_type=SINGLE,
        )
        first += rows
    return total


def key_span(start):
    reach = LEN - (DOCUMENTS - 1) * SHORTEST - 1
    return max(0, (start - reach) // 128 * 128), start + TILE


def mask_bias(begin_ref, start, low, high):
    shape = (high - low, TILE)
    key_pos = low + lax.broadcasted_iota(jnp.int32, shape, 0)
    query_pos = start + lax.broadcasted_iota(jnp.int32, shape, 1)
    counts = (key_pos >= begin_ref[:, start : start + TILE]) & (key_pos <= query_pos)
    return jnp.where(counts, 0.0, MASKED)


def head_ratio(values):
    return lax.rsqrt(jnp.mean(values * values, axis=0, keepdims=True) + EPSILON)


def turn(values, cosine, sine):
    half_dim = values.shape[0] // 2
    first, second = values[:half_dim], values[half_dim:]
    return jnp.concatenate([first * cosine - second * sine, second * cosine + first * sine], axis=0)


def gain_columns(gain_ref, head_dim):
    turned = jnp.broadcast_to(gain_ref[...], (8, gain_ref.shape[1])).T
    return turned[:head_dim, :1], turned[head_dim : 2 * head_dim, :1]


def spread(place_ref, natural, out_ref):
    rows = LEN // place_ref.shape[0]
    for block in range(place_ref.shape[0]):
        start = pl.multiple_of(place_ref[block], rows)
        out_ref[pl.ds(start, rows), :] = natural[block * rows : (block + 1) * rows, :]


def collect(place_ref, value_ref, natural):
    rows = LEN // place_ref.shape[0]
    for block in range(place_ref.shape[0]):
        start = pl.multiple_of(place_ref[block], rows)
        natural[block * rows : (block + 1) * rows, :] = value_ref[pl.ds(start, rows), :]


def attend_kernel(
    sizes,
    place_ref,
    rows_a_ref,
    rows_b_ref,
    rows_c_ref,
    rows_d_ref,
    weight_ref,
    gain_ref,
    segment_ref,
    raw_ref,
    query_ref,
    key_ref,
    query_row_ref,
    key_row_ref,
    value_row_ref,
    total_ref,
    attended_ref,
    cosine_ref,
    sine_ref,
    begin_ref,
    context_ref,
    part_a_ref,
    part_b_ref,
    part_c_ref,
    part_d_ref,
    mixed,
    natural,
    extended,
    bias,
    context,
):
    query_heads, key_heads, head_dim = sizes
    group_size = query_heads // key_heads
    heads = query_heads + key_heads
    columns = natural.shape[1]
    quarter = rows_a_ref.shape[0]
    weight = weight_ref[:, :columns]
    for q, rows_ref in enumerate((rows_a_ref, rows_b_ref, rows_c_ref, rows_d_ref)):
        mixed[q * quarter : (q + 1) * quarter, :] = dot(rows_ref[...], weight)
    collect(place_ref, mixed, natural)
    for start in range(0, LEN, 128):
        turned = natural[start : start + 128, :].T
        raw_ref[:, start : start + 128] = turned[: heads * head_dim]
        for head in range(key_heads):
            first = (heads + head) * head_dim
            extended[head, :head_dim, start : start + 128] = turned[
                first : first + head_dim
            ].astype(BFLOAT)

    segment = segment_ref[...]
    first_count = jnp.sum((segment == 0).astype(SINGLE), axis=1, keepdims=True)
    second_count = jnp.sum((segment == 1).astype(SINGLE), axis=1, keepdims=True)
    begin = jnp.where(
        segment == 0, 0.0, jnp.where(segment == 1, first_count, first_count + second_count)
    )
    begin_ref[...] = begin.astype(jnp.int32)
    half_dim = head_dim // 2
    shape = (half_dim, LEN)
    steps = lax.broadcasted_iota(jnp.int32, shape, 0).astype(SINGLE)
    order = lax.broadcasted_iota(jnp.int32, shape, 1).astype(SINGLE)
    angles = (order - begin) * jnp.exp(steps * (-math.log(THETA) / half_dim))
    cosine, sine = jnp.cos(angles), jnp.sin(angles)
    cosine_ref[...] = cosine
    sine_ref[...] = sine

    gains = gain_columns(gain_ref, head_dim)
    for head in range(heads):
        values = raw_ref[head * head_dim : (head + 1) * head_dim, :]
        gain = gains[0] if head < query_heads else gains[1]
        turned = turn(values * head_ratio(values) * gain, cosine, sine)
        if head < query_heads:
            query_ref[head] = turned.astype(BFLOAT)
            query_row_ref[head] = turned.T.astype(BFLOAT)
        else:
            key_ref[head - query_heads] = turned.astype(BFLOAT)
            key_row_ref[head - query_heads] = turned.T.astype(BFLOAT)
    for head in range(key_heads):
        first = (heads + head) * head_dim
        extended[head, head_dim:, :] = jnp.ones((extended.shape[1] - head_dim, LEN), BFLOAT)
        value_row_ref[head] = natural[:, first : first + head_dim].astype(BFLOAT)
    factor = LOG2E * head_dim ** (-0.5)
    for start in range(0, LEN, TILE):
        low, high = key_span(start)
        span, tile = slice(low, high), slice(start, start + TILE)
        bias[: high - low, :] = mask_bias(begin_ref, start, low, high)

        def one_head(head, carry):
            key_head = head // group_size
            scores = dot(key_row_ref[key_head, span, :], query_ref[head, :, tile])
            powers = jnp.exp2(scores * factor + bias[: high - low, :])
            summed = dot(extended[key_head, :, span], powers.astype(BFLOAT))
            total = summed[head_dim : head_dim + 1, :]
            total_ref[head, :, tile] = jnp.log2(total)
            attended_ref[head, :, tile] = summed[:head_dim, :] / total
            return carry

        lax.fori_loop(0, query_heads, one_head, 0)
    for head in range(query_heads):
        context[:, head * head_dim : (head + 1) * head_dim] = attended_ref[head].T.astype(BFLOAT)
    spread(place_ref, context, context_ref)
    out_weight = weight_ref[:, columns:]
    for q, part_ref in enumerate((part_a_ref, part_b_ref, part_c_ref, part_d_ref)):
        rows = context_ref[q * quarter : (q + 1) * quarter, :]
        part_ref[...] = dot_last(rows, out_weight).astype(BFLOAT)


def attend(sizes, place, quarters, weight, gains, segments):
    query_heads, key_heads, head_dim = sizes
    columns = (query_heads + 2 * key_heads) * head_dim
    quarter, width = quarters[0].shape
    shapes = [
        (((query_heads + key_heads) * head_dim, LEN), SINGLE),
        ((query_heads, head_dim, LEN), BFLOAT),
        ((key_heads, head_dim, LEN), BFLOAT),
        ((query_heads, LEN, head_dim), BFLOAT),
        ((key_heads, LEN, head_dim), BFLOAT),
        ((key_heads, LEN, head_dim), BFLOAT),
        ((query_heads, 1, LEN), SINGLE),
        ((query_heads, head_dim, LEN), SINGLE),
        ((head_dim // 2, LEN), SINGLE),
        ((head_dim // 2, LEN), SINGLE),
        ((1, LEN), jnp.int32),
        ((LEN, query_heads * head_dim), BFLOAT),
    ] + [((quarter, width), BFLOAT)] * 4
    scratch = [
        ((LEN, columns), SINGLE),
        ((LEN, columns), SINGLE),
        ((key_heads, head_dim + 16, LEN), BFLOAT),
        ((LEN, TILE), SINGLE),
        ((LEN, query_heads * head_dim), BFLOAT),
    ]
    arrays = (*quarters, weight, gains, segments)
    outs = call_kernel(
        partial(attend_kernel, sizes), "attend", HEAVY, 56, shapes, (place,), arrays, scratch
    )
    return outs[:11], outs[11], outs[12:]


def attend_back_kernel(
    sizes,
    place_ref,
    grad_a_ref,
    grad_b_ref,
    grad_c_ref,
    grad_d_ref,
    rows_a_ref,
    rows_b_ref,
    rows_c_ref,
    rows_d_ref,
    weight_ref,
    gain_ref,
    raw_ref,
    query_ref,
    key_ref,
    query_row_ref,
    key_row_ref,
    value_row_ref,
    total_ref,
    attended_ref,
    cosine_ref,
    sine_ref,
    begin_ref,
    context_ref,
    earlier_ref,
    weight_grad_ref,
    head_gain_ref,
    row_gain_ref,
    part_a_ref,
    part_b_ref,
    part_c_ref,
    part_d_ref,
    mixed,
    context,
    grad_row,
    grad_col,
    query_grad,
    key_grad,
    value_grad,
    joined,
    natural,
    out_ref,
    bias,
):
    query_heads, key_heads, head_dim = sizes
    group_size = query_heads // key_heads
    heads = query_heads + key_heads
    columns = natural.shape[1]
    quarter = grad_a_ref.shape[0]
    out_weight = weight_ref[:, columns:]
    grad_refs = (grad_a_ref, grad_b_ref, grad_c_ref, grad_d_ref)
    for q, rows_ref in enumerate(grad_refs):
        mixed[q * quarter : (q + 1) * quarter, :] = dot(rows_ref[...], out_weight).astype(BFLOAT)
    weight_grad_ref[:, columns:] = dot_first(grad_refs, context_ref).astype(BFLOAT)
    collect(place_ref, mixed, context)
    for head in range(query_heads):
        part = context[:, head * head_dim : (head + 1) * head_dim]
        grad_row[head] = part
        grad_col[head] = part.astype(SINGLE).T
    key_grad[...] = jnp.zeros(key_grad.shape, SINGLE)
    value_grad[...] = jnp.zeros(value_grad.shape, SINGLE)
    scale = head_dim ** (-0.5)
    factor = LOG2E * scale
    for start in range(0, LEN, TILE):
        low, high = key_span(start)
        span, tile = slice(low, high), slice(start, start + TILE)
        bias[: high - low, :] = mask_bias(begin_ref, start, low, high)

        def one_head(head, carry):
            key_head = head // group_size
            scores = dot(key_row_ref[key_head, span, :], query_ref[head, :, tile])
            probs = jnp.exp2(scores * factor + bias[: high - low, :] - total_ref[head, :, tile])
            grads = grad_col[head, :, tile]
            inner = jnp.sum(grads * attended_ref[head, :, tile], axis=0, keepdims=True)
            probs_grad = dot(value_row_ref[key_head, span, :], grads.astype(BFLOAT))
            scores_grad = (probs * (probs_grad - inner)).astype(BFLOAT)
            value_grad[key_head, span, :] += dot(probs.astype(BFLOAT), grad_row[head, tile, :])
            key_grad[key_head, span, :] += dot(scores_grad, query_row_ref[head, tile, :])
            query_grad[head, :, tile] = dot(key_ref[key_head, :, span], scores_grad)
            return carry

        lax.fori_loop(0, query_heads, one_head, 0)
    cosine, sine = cosine_ref[...], sine_ref[...]
    gains = gain_columns(gain_ref, head_dim)
    for kind in range(2):
        head_gain_ref[kind] = jnp.zeros(head_gain_ref.shape[1:], SINGLE)
    for head in range(heads):
        kind = 0 if head < query_heads else 1
        grads = query_grad[head] if kind == 0 else key_grad[head - query_heads].T
        grads = turn(grads * scale, cosine, -sine)
        values = raw_ref[head * head_dim : (head + 1) * head_dim, :]
        ratio = head_ratio(values)
        normed = values * ratio
        weighted = grads * gains[kind]
        inner = jnp.mean(weighted * normed, axis=0, keepdims=True)
        joined[head * head_dim : (head + 1) * head_dim, :] = ratio * (weighted - normed * inner)
        products = grads * normed
        folded = products[:, :128]
        for first in range(128, LEN, 128):
            folded = folded + products[:, first : first + 128]
        head_gain_ref[kind] += folded
    for start in range(0, LEN, 128):
        natural[start : start + 128, : heads * head_dim] = joined[:, start : start + 128].T.astype(
            BFLOAT
        )
    for head in range(key_heads):
        first = (heads + head) * head_dim
        natural[:, first : first + head_dim] = value_grad[head].astype(BFLOAT)
    spread(place_ref, natural, out_ref)
    weight = weight_ref[:, :columns]
    row_gain = jnp.zeros(row_gain_ref.shape, SINGLE)
    rows_refs = (rows_a_ref, rows_b_ref, rows_c_ref, rows_d_ref)
    for q, part_ref in enumerate((part_a_ref, part_b_ref, part_c_ref, part_d_ref)):
        part = dot_last(out_ref[q * quarter : (q + 1) * quarter, :], weight)
        part_ref[...] = part.astype(BFLOAT)
        row_gain += jnp.sum(part * rows_refs[q][...].astype(SINGLE), axis=0, keepdims=True)
    row_gain_ref[...] = row_gain
    weight_grad_ref[:, :columns] = dot_first(rows_refs, out_ref).astype(BFLOAT)


def attend_back(sizes, place, grads, quarters, weight, gains, saved, context, earlier):
    query_heads, key_heads, head_dim = sizes
    heads = query_heads + key_heads
    columns = (heads + key_heads) * head_dim
    quarter, width = quarters[0].shape
    shapes = [
        (weight.shape, BFLOAT),
        ((2, head_dim, 128), SINGLE),
        ((1, width), SINGLE),
    ] + [((quarter, width), BFLOAT)] * 4
    scratch = [
        ((LEN, query_heads * head_dim), BFLOAT),
        ((LEN, query_heads * head_dim), BFLOAT),
        ((query_heads, LEN, head_dim), BFLOAT),
        ((query_heads, head_dim, LEN), SINGLE),
        ((query_heads, head_dim, LEN), SINGLE),
        ((key_heads, LEN, head_dim), SINGLE),
        ((key_heads, LEN, head_dim), SINGLE),
        ((heads * head_dim, LEN), SINGLE),
        ((LEN, columns), BFLOAT),
        ((LEN, columns), BFLOAT),
        ((LEN, TILE), SINGLE),
    ]
    arrays = (*grads, *quarters, weight, gains, *saved, context)
    kernel = partial(attend_back_kernel, sizes)
    outs = call_kernel(
        kernel, "attend_back", HEAVY, 56, shapes, (place,), arrays, scratch, (earlier,)
    )
    return outs[0], outs[1], outs[2], outs[3:]


def feedfwd_kernel(
    rows_a_ref,
    rows_b_ref,
    rows_c_ref,
    rows_d_ref,
    cot_a_ref,
    cot_b_ref,
    cot_c_ref,
    cot_d_ref,
    weight_ref,
    hidden_ref,
    out_ref,
    part_a_ref,
    part_b_ref,
    part_c_ref,
    part_d_ref,
    gate_up_grad,
    total,
):
    step = pl.program_id(0)
    quarter = rows_a_ref.shape[0]
    cols = hidden_ref.shape[1]
    rows_refs = (rows_a_ref, rows_b_ref, rows_c_ref, rows_d_ref)
    cot_refs = (cot_a_ref, cot_b_ref, cot_c_ref, cot_d_ref)
    part_refs = (part_a_ref, part_b_ref, part_c_ref, part_d_ref)

    @pl.when(step == 0)
    def _():
        total[...] = jnp.zeros(total.shape, SINGLE)

    for q in range(4):
        tile = slice(q * quarter, (q + 1) * quarter)
        gate_up = dot(rows_refs[q][...], weight_ref[:, : 2 * cols])
        gate_proj, upward = gate_up[:, :cols], gate_up[:, cols:]
        grad_hidden = dot(cot_refs[q][...], weight_ref[:, 2 * cols :])
        sigmoid = 0.5 * jnp.tanh(0.5 * gate_proj) + 0.5
        active = gate_proj * sigmoid
        hidden_ref[tile, :] = (active * upward).astype(BFLOAT)
        slope = sigmoid + active * (1.0 - sigmoid)
        gate_up_grad[tile, :cols] = (grad_hidden * upward * slope).astype(BFLOAT)
        gate_up_grad[tile, cols:] = (grad_hidden * active).astype(BFLOAT)
        total[tile, :] += dot_last(gate_up_grad[tile, :], weight_ref[:, : 2 * cols])
    out_ref[:, : 2 * cols] = dot_first(rows_refs, gate_up_grad).astype(BFLOAT)
    out_ref[:, 2 * cols :] = dot_first(cot_refs, hidden_ref).astype(BFLOAT)

    @pl.when(step == pl.num_programs(0) - 1)
    def _():
        for q in range(4):
            part_refs[q][...] = total[q * quarter : (q + 1) * quarter, :].astype(BFLOAT)


def tile_of(hidden_cols):
    return 384 if hidden_cols % 384 == 0 else hidden_cols


def interleave(gate, up, down):
    tile = tile_of(gate.shape[1])
    pieces = []
    for first in range(0, gate.shape[1], tile):
        pieces += [value[:, first : first + tile] for value in (gate, up, down)]
    return jnp.concatenate(pieces, axis=1)


def part_of(value, kind):
    tile = tile_of(value.shape[1] // 3)
    starts = range(kind * tile, value.shape[1], 3 * tile)
    return jnp.concatenate([value[:, first : first + tile] for first in starts], axis=1)


def feedfwd(quarters, cots, weight):
    quarter, width = quarters[0].shape
    hidden_cols = weight.shape[1] // 3
    cols = tile_of(hidden_cols)
    whole = pl.BlockSpec((quarter, width), lambda j: (0, 0))
    block = pl.BlockSpec((width, 3 * cols), lambda j: (0, j))
    outs = pl.pallas_call(
        feedfwd_kernel,
        grid=(hidden_cols // cols,),
        out_shape=[
            jax.ShapeDtypeStruct((LEN, hidden_cols), BFLOAT),
            jax.ShapeDtypeStruct((width, 3 * hidden_cols), BFLOAT),
        ]
        + [jax.ShapeDtypeStruct((quarter, width), BFLOAT)] * 4,
        in_specs=[whole] * 8 + [block],
        out_specs=[pl.BlockSpec((LEN, cols), lambda j: (0, j)), block] + [whole] * 4,
        scratch_shapes=[
            pltpu.VMEM((LEN, 2 * cols), BFLOAT),
            pltpu.VMEM((LEN, width), SINGLE),
        ],
        compiler_params=pltpu.CompilerParams(vmem_limit_bytes=56 * MIB),
        cost_estimate=pl.CostEstimate(flops=HEAVY, bytes_accessed=2**20, transcendentals=0),
        name="feedfwd",
    )(*quarters, *cots, weight)
    return outs[0], outs[1], outs[2:]


def pair_sum_kernel(stay_a_ref, got_a_ref, stay_b_ref, got_b_ref, *refs):
    outs = refs[-4:]
    rows = stay_a_ref.shape[0] // 2
    pairs = ((stay_a_ref, got_a_ref), (stay_b_ref, got_b_ref))
    for half, (stay_ref, got_ref) in enumerate(pairs):
        total = stay_ref[...].astype(SINGLE) + got_ref[...].astype(SINGLE)
        outs[2 * half][...] = total[:rows].astype(outs[2 * half].dtype)
        outs[2 * half + 1][...] = total[rows:].astype(BFLOAT)


def pair_sum(stays, gots, last, earlier):
    rows, width = stays[0].shape
    shapes = [((rows // 2, width), SINGLE if last else BFLOAT), ((rows // 2, width), BFLOAT)] * 2
    arrays = (stays[0], gots[0], stays[1], gots[1])
    outs = call_kernel(pair_sum_kernel, "pair_sum", LIGHT, 8, shapes, (), arrays, earlier=earlier)
    return outs[0::2], outs[1::2]


def down_kernel(hidden_ref, weight_ref, *refs):
    outs, total = refs[-5:-1], refs[-1]
    step = pl.program_id(0)
    product = dot_last(hidden_ref[...], weight_ref[...])

    @pl.when(step == 0)
    def _():
        total[...] = product

    @pl.when(step > 0)
    def _():
        total[...] += product

    @pl.when(step == pl.num_programs(0) - 1)
    def _():
        quarter = total.shape[0] // 4
        for q, part_ref in enumerate(outs):
            part_ref[...] = total[q * quarter : (q + 1) * quarter, :].astype(BFLOAT)


def down_parts_of(hidden, weight, earlier):
    hidden_cols = hidden.shape[1]
    quarter, width = LEN // 4, weight.shape[0]
    cols = tile_of(hidden_cols)
    if cols % 128:
        down = part_of(weight, 2)
        return [
            dot_last(hidden[q * quarter : (q + 1) * quarter], down).astype(BFLOAT) for q in range(4)
        ]
    part = pl.BlockSpec((quarter, width), lambda i: (0, 0))
    return pl.pallas_call(
        down_kernel,
        grid=(hidden_cols // cols,),
        out_shape=[jax.ShapeDtypeStruct((quarter, width), BFLOAT)] * 4,
        in_specs=[
            pl.BlockSpec((LEN, cols), lambda i: (0, i)),
            pl.BlockSpec((width, cols), lambda i: (0, 3 * i + 2)),
        ]
        + [pl.BlockSpec(memory_space=pl.ANY)] * len(earlier),
        out_specs=[part] * 4,
        scratch_shapes=[pltpu.VMEM((LEN, width), SINGLE)],
        compiler_params=pltpu.CompilerParams(vmem_limit_bytes=56 * MIB),
        cost_estimate=pl.CostEstimate(flops=LIGHT, bytes_accessed=2**20, transcendentals=0),
        name="down_parts",
    )(hidden, weight, *earlier)


def finish_kernel(tokens_ref, gain_ref, *refs):
    block_ref, tokens_out_ref = refs[-2:]
    rows = tokens_ref.shape[0] // 2
    for half in range(2):
        part = slice(half * rows, (half + 1) * rows)
        residual, grad, down, down_got, norm, norm_got = refs[6 * half : 6 * half + 6]
        summed = down[...] + down_got[...].astype(SINGLE)
        block_ref[part, :] = (residual[...] + summed).astype(BFLOAT)
        back = norm[...] + norm_got[...].astype(SINGLE)
        back, _ = rms_back(tokens_ref[part, :].astype(SINGLE), gain_ref[...], back)
        tokens_out_ref[part, :] = (grad[...] + back).astype(BFLOAT)


def finish(tokens, gain, halves):
    arrays = (tokens, gain[None, :], *(array for half in halves for array in half))
    kinds = [(tokens.shape, BFLOAT)] * 2
    return call_kernel(finish_kernel, "finish", HEAVY, 56, kinds, (), arrays)


def split_kernel(value_ref, query_ref, key_ref, value_out_ref, out_ref):
    first = 0
    for ref in (query_ref, key_ref, value_out_ref):
        ref[...] = value_ref[:, first : first + ref.shape[1]].astype(SINGLE)
        first += ref.shape[1]
    out_ref[...] = value_ref[:, first:].astype(SINGLE).T


def split_weights(value, shapes):
    kinds = [(shape, SINGLE) for shape in shapes]
    return call_kernel(split_kernel, "split_weights", LIGHT, 56, kinds, (), (value,))


def pack_kernel(query_ref, key_ref, value_ref, out_ref, packed_ref):
    first = 0
    for ref in (query_ref, key_ref, value_ref):
        packed_ref[:, first : first + ref.shape[1]] = ref[...]
        first += ref.shape[1]
    packed_ref[:, first:] = out_ref[...].astype(SINGLE).T.astype(BFLOAT)


def pack_weights(*values):
    columns = sum(value.shape[1] for value in values[:3]) + values[3].shape[0]
    kinds = [((values[0].shape[0], columns), BFLOAT)]
    return call_kernel(pack_kernel, "pack_weights", LIGHT, 56, kinds, (), values)[0]


def later(value, *earlier):
    anywhere = pl.BlockSpec(memory_space=pl.ANY)
    return pl.pallas_call(
        lambda *refs: None,
        out_shape=jax.ShapeDtypeStruct(value.shape, value.dtype),
        in_specs=[anywhere] * (1 + len(earlier)),
        out_specs=anywhere,
        input_output_aliases={0: 0},
        name="later",
    )(value, *earlier)


def wait_aways(parts, *earlier):
    return [later(part, *earlier) if q % 2 else part for q, part in enumerate(parts)]


def rms_scale(values, gain):
    return values * lax.rsqrt(jnp.mean(values * values, axis=-1, keepdims=True) + EPSILON) * gain


def swap(value, axis, bit):
    size = lax.axis_size(axis)
    return lax.ppermute(value, axis, [(i, i ^ bit) for i in range(size)])


def axis_bits(axis):
    return [1 << k for k in range(lax.axis_size(axis).bit_length() - 1)]


def block_order(bits):
    order = [0]
    for bit in bits:
        order = order + [r ^ bit for r in order]
    return order


def butterfly_sum(value):
    for axis in ("dp", "tensor"):
        for bit in axis_bits(axis):
            value = value + swap(value, axis, bit)
    return value


def rms_back(values, gain, grad):
    ratio = lax.rsqrt(jnp.mean(values * values, axis=-1, keepdims=True) + EPSILON)
    scaled = grad * gain
    inner = jnp.mean(scaled * values, axis=-1, keepdims=True)
    return ratio * scaled - values * (ratio * ratio * ratio * inner), grad * values * ratio


def on_device(
    tokens,
    segments,
    cotangent,
    query_weight,
    key_weight,
    value_weight,
    out_weight,
    gate_weight,
    up_weight,
    down_weight,
    attention_gain,
    feedfwd_gain,
    query_gain,
    key_gain,
):
    head_dim = query_gain.shape[0]
    local_rows, width = tokens.shape
    half_rows = local_rows // 2
    tensor_size, here = lax.axis_size("tensor"), lax.axis_index("tensor")
    tensor_bits = axis_bits("tensor")
    half_bits = (tensor_bits, tensor_bits[::-1])
    half_order = [block_order(bits) for bits in half_bits]
    place = jnp.stack(
        [
            jnp.array([order.index(r) for r in range(tensor_size)], jnp.int32)[here ^ j] * half_rows
            + c * (LEN // 2)
            for j in range(tensor_size)
            for c, order in enumerate(half_order)
        ]
    )

    def rows_gather(halves):
        for bits in zip(*half_bits):
            pairs = [(part, swap(part, "tensor", bit)) for part, bit in zip(halves, bits)]
            halves = [jnp.concatenate(pair, axis=0) for pair in pairs]
        return [*pairs[0], *pairs[1]]

    def rows_scatter(parts, earlier=()):
        stays, aways = parts[0::2], parts[1::2]
        for step, bits in enumerate(zip(*(bits[::-1] for bits in half_bits))):
            gots = [swap(part, "tensor", bit) for part, bit in zip(aways, bits)]
            if step < len(tensor_bits) - 1:
                last = step == len(tensor_bits) - 2
                stays, aways = pair_sum(stays, gots, last, earlier)
                first = stays[0] if step == 0 else first
                earlier = ()
        return stays, gots, first

    def halves_of(value):
        return [value[:half_rows], value[half_rows:]]

    token_values = tokens.astype(SINGLE)
    normed = rms_scale(token_values, attention_gain).astype(BFLOAT)
    gathered = rows_gather(halves_of(normed))
    attention_full = lax.all_gather(
        pack_weights(query_weight, key_weight, value_weight, out_weight),
        "dp",
        axis=0,
        tiled=True,
    )
    feedfwd_full = lax.all_gather(
        interleave(gate_weight, up_weight, down_weight.T), "dp", axis=0, tiled=True
    )
    cots = rows_gather(halves_of(cotangent))

    query_cols, key_cols = query_weight.shape[1], key_weight.shape[1]
    sizes = (query_cols // head_dim, key_cols // head_dim, head_dim)
    gains = jnp.concatenate([query_gain, key_gain])[None, :]
    saved, context, attended_parts = attend(
        sizes, place, gathered, attention_full, gains, segments[None, :]
    )
    attended_parts = wait_aways(attended_parts, cots[1], cots[3])
    residuals, normed_two = [], []
    stays, gots, _ = rows_scatter(attended_parts)
    for token_part, stay, got in zip(halves_of(token_values), stays, gots):
        residuals.append(token_part + (stay + got.astype(SINGLE)))
        normed_two.append(rms_scale(residuals[-1], feedfwd_gain).astype(BFLOAT))
    gathered_two = rows_gather(normed_two)

    hidden, feedfwd_part, two_parts = feedfwd(gathered_two, cots, feedfwd_full)
    grad_feedfwd = lax.psum_scatter(feedfwd_part, "dp", scatter_dimension=0, tiled=True)
    stays, gots, _ = rows_scatter(two_parts)
    two_sums = [stay + got.astype(SINGLE) for stay, got in zip(stays, gots)]
    grad_residual, gain_two_part = [], 0.0
    for residual_part, sum_part, cot_part in zip(residuals, two_sums, halves_of(cotangent)):
        back, gain_part = rms_back(residual_part, feedfwd_gain, sum_part)
        grad_residual.append(cot_part.astype(SINGLE) + back)
        gain_two_part = gain_two_part + jnp.sum(gain_part, axis=0)
    grad_low = [part.astype(BFLOAT) for part in grad_residual]
    down_parts = down_parts_of(hidden, feedfwd_full, grad_low)
    gathered_grad = rows_gather(grad_low)

    attention_part, head_gains, row_gain, normed_parts = attend_back(
        sizes, place, gathered_grad, gathered, attention_full, gains, saved, context, down_parts[0]
    )
    down_stays, down_gots, down_first = rows_scatter(
        wait_aways(down_parts, gathered_grad[1], gathered_grad[3]), (head_gains,)
    )
    attention_part = later(attention_part, grad_feedfwd, down_first)
    grad_attention = lax.psum_scatter(attention_part, "dp", scatter_dimension=0, tiled=True)
    normed_stays, normed_gots, normed_first = rows_scatter(normed_parts, (attention_part,))

    gain_parts = jnp.concatenate(
        [row_gain[0] / attention_gain, gain_two_part, *jnp.sum(head_gains, axis=2)]
    )
    gain_sums = butterfly_sum(gain_parts + 0.0 * normed_first[0, 0].astype(SINGLE))
    grad_feedfwd = grad_feedfwd.astype(SINGLE)
    halves = [*zip(residuals, grad_residual, down_stays, down_gots, normed_stays, normed_gots)]
    shapes = [value.shape for value in (query_weight, key_weight, value_weight, out_weight)]
    return (
        *finish(tokens, attention_gain, halves),
        *split_weights(grad_attention, shapes),
        part_of(grad_feedfwd, 0),
        part_of(grad_feedfwd, 1),
        part_of(grad_feedfwd, 2).T,
        gain_sums[:width],
        gain_sums[width : 2 * width],
        gain_sums[2 * width : 2 * width + head_dim],
        gain_sums[2 * width + head_dim :],
    )


def solution(mesh):
    in_specs = (
        P(("dp", "tensor"), None),
        P("dp"),
        P(("dp", "tensor"), None),
        P("dp", "tensor"),
        P("dp", "tensor"),
        P("dp", "tensor"),
        P("tensor", "dp"),
        P("dp", "tensor"),
        P("dp", "tensor"),
        P("tensor", "dp"),
        P(),
        P(),
        P(),
        P(),
    )
    out_specs = (
        P(("dp", "tensor"), None),
        P(("dp", "tensor"), None),
        P("dp", "tensor"),
        P("dp", "tensor"),
        P("dp", "tensor"),
        P("tensor", "dp"),
        P("dp", "tensor"),
        P("dp", "tensor"),
        P("tensor", "dp"),
        P(),
        P(),
        P(),
        P(),
    )
    return jax.shard_map(
        on_device, mesh=mesh, in_specs=in_specs, out_specs=out_specs, check_vma=False
    )
```
